512 devices in a mesh: section: 16 (over z), tm: 32 (over y, x, core).
Axes of the slice: x: 4, y: 4, z: 16, core: 2. Of those that a mesh axis runs over, the one named last changes fastest.
Arguments:
- resid: bfloat16 [16, 4096, 768], P('section', 'tm'), may hold values from -40 to 40
- queries: bfloat16 [16, 4096, 768], P('section', 'tm'), may hold values from -100 to 100
- keys: bfloat16 [16, 4096, 768], P('section', 'tm'), may hold values from -4 to 4
- values: bfloat16 [16, 4096, 768], P('section', 'tm'), may hold values from -5 to 5
- gain: float32 [16, 768], P('section'), may hold values from 0.5 to 1.5
- taps: float32 [16, 31, 768], P('section'), may hold values from -1 to 1
- cotangent: bfloat16 [16, 4096, 768], P('section', 'tm'), may hold values from -8 to 8
Outputs:
- next_input: bfloat16 [16, 4096, 768], P('section', 'tm')
- grad_resid: bfloat16 [16, 4096, 768], P('section', 'tm')
- grad_queries: bfloat16 [16, 4096, 768], P('section', 'tm')
- grad_keys: bfloat16 [16, 4096, 768], P('section', 'tm')
- grad_values: bfloat16 [16, 4096, 768], P('section', 'tm')
- grad_gain: float32 [16, 768], P('section')
- grad_taps: float32 [16, 31, 768], P('section')
The draws below stay inside these ranges and needn't reach their ends.
All inputs are finite; a program needn't handle non-finite values.
Results may differ from the reference program's by a relative error of at most 0.024.
Values may be sent and summed in bfloat16 or wider, within the bound.
No kernel may reach another device: no remote copies, remote signals or barrier semaphores. Data moves between devices by JAX's collectives and lax.ppermute only.
A program may use at most 64 MiB of HBM per device.

```python
import jax
import jax.numpy as jnp
from jax import lax

HEADS = 8
HEAD_DIM = 96
TAPS = 31
CH = 768
FRAMES = 4096
SECTIONS = 16


def shared_keys(key):
    base = jnp.clip(jax.random.normal(jax.random.fold_in(key, 21), (SECTIONS, FRAMES, HEADS, HEAD_DIM), jnp.float32), -4.0, 4.0)
    first = jax.random.randint(jax.random.fold_in(key, 22), (SECTIONS, 3), 0, FRAMES)
    offset = jax.random.randint(jax.random.fold_in(key, 23), (SECTIONS, 3), 1, FRAMES)
    second = (first + offset) % FRAMES
    head_ids = jax.random.randint(jax.random.fold_in(key, 24), (SECTIONS, 3), 0, HEADS)
    strength = jnp.array([12.0, 18.0, 25.0], jnp.float32)
    section_ids = jnp.broadcast_to(jnp.arange(SECTIONS)[:, None], (SECTIONS, 3))
    factor = 1.0 - 2.0 / (strength * jnp.sqrt(jnp.float32(HEAD_DIM)))
    near = base[section_ids, first, head_ids] * factor[None, :, None]
    shaped = base.at[section_ids, second, head_ids].set(near)
    return shaped


def draw_keys(key, part):
    shaped = shared_keys(key)
    return shaped.reshape(SECTIONS, FRAMES, HEADS * HEAD_DIM).astype(jnp.bfloat16)


def draw_queries(key, part):
    key = jax.random.fold_in(key, 3)
    base = 2.0 * jnp.clip(jax.random.normal(key, (SECTIONS, FRAMES, HEADS, HEAD_DIM), jnp.float32), -4.0, 4.0)
    return base.reshape(SECTIONS, FRAMES, HEADS * HEAD_DIM).astype(jnp.bfloat16)


def draw_resid(key, part):
    key = jax.random.fold_in(key, 1)
    shape = (SECTIONS, FRAMES, HEADS * HEAD_DIM)
    core = jnp.clip(jax.random.normal(jax.random.fold_in(key, 11), shape, jnp.float32), -4.0, 4.0)
    rows = jnp.exp(jax.random.uniform(jax.random.fold_in(key, 12), (SECTIONS, FRAMES, 1), jnp.float32, jnp.log(0.3), jnp.log(3.0)))
    cols = jnp.exp(jax.random.uniform(jax.random.fold_in(key, 13), (SECTIONS, 1, shape[2]), jnp.float32, jnp.log(0.3), jnp.log(3.0)))
    return (core * rows * cols).astype(jnp.bfloat16)


def draw_cotangent(key, part):
    key = jax.random.fold_in(key, 4)
    shape = (SECTIONS, FRAMES, HEADS * HEAD_DIM)
    core = jnp.clip(jax.random.normal(jax.random.fold_in(key, 41), shape, jnp.float32), -4.0, 4.0)
    place = jnp.arange(FRAMES, dtype=jnp.float32)[None, :, None] / FRAMES
    result = core * (0.5 + place)
    return result.astype(jnp.bfloat16)


def block_scale(key, dims, split, low, largest):
    factor_of = 1.0
    for dim, blocks in split:
        steps = jax.random.uniform(jax.random.fold_in(jax.random.fold_in(key, 6), dim), (blocks,), jnp.float32, low / len(split), largest / len(split))
        factor_of = factor_of * jnp.repeat(jnp.exp(steps), dims[dim] // blocks).reshape((-1,) + (1,) * (len(dims) - 1 - dim))
    return factor_of


def gaussian(own_key, dims, deviation, bound, cuts=(), held_as=jnp.bfloat16):
    drawn = deviation * jax.random.normal(own_key, dims, jnp.float32)
    if cuts:
        drawn = drawn * block_scale(own_key, dims, cuts, -0.22, 0.18)
    return jnp.clip(drawn, -bound, bound).astype(held_as)


def setup_inputs(seed: int = 0) -> dict:
    seeds = jax.random.split(jax.random.key(seed), 8)
    return {
        "resid": draw_resid(jax.random.fold_in(seeds[7], 71), 0),
        "queries": draw_queries(jax.random.fold_in(seeds[7], 71), 0),
        "keys": draw_keys(jax.random.fold_in(seeds[7], 71), 0),
        "values": gaussian(seeds[3], (SECTIONS, FRAMES, CH), 1.0, 5.0, ((0, 16), (1, 32))),
        "gain": jnp.clip(0.5 + 1.0 * jax.random.uniform(seeds[4], (SECTIONS, CH), jnp.float32) ** block_scale(seeds[4], (SECTIONS, CH), ((0, 16),), -0.2, 0.2), 0.5, 1.5),
        "taps": gaussian(seeds[5], (SECTIONS, TAPS, CH), TAPS ** -0.5, 1.0, ((0, 16),), jnp.float32),
        "cotangent": draw_cotangent(jax.random.fold_in(seeds[7], 71), 0),
    }


EPS = 1e-06

def head_forward(query_head, key_head, value_head, scale):
    logits = jnp.dot(query_head, key_head.T, preferred_element_type=jnp.float32) * scale
    peak = lax.optimization_barrier(jnp.max(logits, axis=1, keepdims=True))
    log_total = peak + jnp.log(lax.optimization_barrier(jnp.sum(jnp.exp(logits - peak), axis=1, keepdims=True)))
    weights = jnp.exp(logits - log_total).astype(jnp.bfloat16)
    result = jnp.dot(weights, value_head, preferred_element_type=jnp.float32).astype(jnp.bfloat16)
    return (result, log_total[:, 0])

def head_backward(query_head, key_head, value_head, result, log_total, grad_head, scale):
    logits = jnp.dot(query_head, key_head.T, preferred_element_type=jnp.float32) * scale
    probs = jnp.exp(logits - log_total[:, None])
    weights = probs.astype(jnp.bfloat16)
    delta = lax.optimization_barrier(jnp.sum(grad_head.astype(jnp.float32) * result.astype(jnp.float32), axis=1, keepdims=True))
    grad_vals = jnp.dot(weights.T, grad_head, preferred_element_type=jnp.float32)
    grad_probs = jnp.dot(grad_head, value_head.T, preferred_element_type=jnp.float32)
    grad_scores = (probs * (grad_probs - delta)).astype(jnp.bfloat16)
    grad_q = jnp.dot(grad_scores, key_head, preferred_element_type=jnp.float32) * scale
    grad_k = jnp.dot(grad_scores.T, query_head, preferred_element_type=jnp.float32) * scale
    return (grad_q, grad_k, grad_vals)

def head_major(rows):
    return rows.reshape(FRAMES, HEADS, HEAD_DIM).transpose(1, 0, 2)

def frame_major(heads):
    return heads.transpose(1, 0, 2).reshape(FRAMES, HEADS * HEAD_DIM)

def section_step(inputs):
    resid, queries, keys, values, gain, taps, cotangent = inputs
    scale = HEAD_DIM ** (-0.5)
    half = (TAPS - 1) // 2
    query_heads = head_major(queries)
    key_heads = head_major(keys)
    value_heads = head_major(values)
    results, log_totals = lax.map(lambda t: head_forward(t[0], t[1], t[2], scale), (query_heads, key_heads, value_heads))
    attended = frame_major(results)
    mixed = resid.astype(jnp.float32) + attended.astype(jnp.float32)
    inverse = lax.rsqrt(lax.optimization_barrier(jnp.mean(mixed * mixed, axis=1, keepdims=True)) + EPS)
    unit = mixed * inverse
    normed = (unit * gain[None, :]).astype(jnp.bfloat16)
    padded = jnp.pad(normed, ((half, half), (0, 0)))
    conv = jnp.zeros(mixed.shape, jnp.float32)
    for tap in range(TAPS):
        conv = conv + taps[tap][None, :] * padded[tap:tap + FRAMES].astype(jnp.float32)
    block_out = (mixed + jax.nn.silu(conv)).astype(jnp.bfloat16)
    cot_rows = cotangent.astype(jnp.float32)
    sig = jax.nn.sigmoid(conv)
    grad_conv = (cot_rows * sig * (1.0 + conv * (1.0 - sig))).astype(jnp.bfloat16)
    padded_grad = jnp.pad(grad_conv, ((half, half), (0, 0)))
    grad_normed = jnp.zeros(mixed.shape, jnp.float32)
    tap_terms = []
    for tap in range(TAPS):
        grad_normed = grad_normed + taps[tap][None, :] * padded_grad[2 * half - tap:2 * half - tap + FRAMES].astype(jnp.float32)
        tap_terms.append(lax.optimization_barrier(jnp.sum(grad_conv.astype(jnp.float32) * padded[tap:tap + FRAMES].astype(jnp.float32), axis=0)))
    grad_taps = jnp.stack(tap_terms)
    grad_gain = lax.optimization_barrier(jnp.sum(grad_normed * unit, axis=0))
    scaled = grad_normed * gain[None, :]
    grad_mixed = cot_rows + inverse * (scaled - unit * lax.optimization_barrier(jnp.mean(scaled * unit, axis=1, keepdims=True)))
    grad_resid = grad_mixed.astype(jnp.bfloat16)
    grad_heads = head_major(grad_resid)
    grad_q, grad_k, grad_v = lax.map(lambda t: head_backward(t[0], t[1], t[2], t[3], t[4], t[5], scale), (query_heads, key_heads, value_heads, results, log_totals, grad_heads))
    return (block_out, grad_resid, frame_major(grad_q).astype(jnp.bfloat16), frame_major(grad_k).astype(jnp.bfloat16), frame_major(grad_v).astype(jnp.bfloat16), grad_gain, grad_taps)

def reference(resid, queries, keys, values, gain, taps, cotangent):
    block_out, grad_resid, grad_queries, grad_keys, grad_values, grad_gain, grad_taps = lax.map(section_step, (resid, queries, keys, values, gain, taps, cotangent))
    next_input = jnp.roll(block_out, 1, axis=0)
    return (next_input, grad_resid, grad_queries, grad_keys, grad_values, grad_gain, grad_taps)
```

```python
import math

import jax
import jax.numpy as jnp
from jax import lax
from jax.experimental import pallas as pl
from jax.experimental.pallas import tpu as pltpu
from jax.sharding import PartitionSpec as P

HEADS = 8
HEAD_DIM = 96
TAPS = 31
CH = 768
LANES = 128
EPS = 1e-06

SCALE = HEAD_DIM ** (-0.5)
SCALE2 = SCALE * math.log2(math.e)

F32 = jnp.float32
BF16 = jnp.bfloat16

K_ROWS = slice(0, 96)
V_ROWS = slice(96, 192)
Q_ROWS = slice(192, 224)
PIECE_ROWS = 224

VMEM = pl.BlockSpec(memory_space=pltpu.VMEM)
SMEM = pl.BlockSpec(memory_space=pltpu.SMEM)
VMEM_LIMIT = 56 * 1024 * 1024


def lanes_of(rows):
    return lax.broadcasted_iota(jnp.int32, (rows, LANES), 1)


def roll_lanes(block, by):
    by = by % LANES
    return block if by == 0 else pltpu.roll(block, by, 1)


def heads_to_tiles(heads):
    lane = lanes_of(heads[0].shape[0])
    second = roll_lanes(heads[1], 96)
    third = roll_lanes(heads[2], 64)
    fourth = roll_lanes(heads[3], 32)
    return (
        jnp.where(lane < 96, heads[0], second),
        jnp.where(lane < 64, second, third),
        jnp.where(lane < 32, third, fourth),
    )


def tiles_to_heads(tiles):
    lane = lanes_of(tiles[0].shape[0])
    return (
        tiles[0],
        roll_lanes(jnp.where(lane >= 96, tiles[0], tiles[1]), 32),
        roll_lanes(jnp.where(lane >= 64, tiles[1], tiles[2]), 64),
        roll_lanes(tiles[2], 96),
    )


def call(kernel, out_shape, in_specs, scratch, flops, name, transcendentals=0):
    return pl.pallas_call(
        kernel,
        out_shape=out_shape,
        in_specs=in_specs,
        out_specs=jax.tree.map(lambda unused: VMEM, out_shape),
        scratch_shapes=scratch,
        compiler_params=pltpu.CompilerParams(vmem_limit_bytes=VMEM_LIMIT),
        cost_estimate=pl.CostEstimate(
            flops=flops, bytes_accessed=4 * 1024 * 1024, transcendentals=transcendentals
        ),
        name=name,
    )


def pack_kernel(groups, q_ref, k_ref, v_ref, send_ref, turned):
    frames = q_ref.shape[0]
    sub = frames // groups
    for source, rows in ((k_ref, K_ROWS), (v_ref, V_ROWS)):
        for tile in range(CH // LANES):
            at = slice(tile * LANES, (tile + 1) * LANES)
            turned[at, :] = source[:, at].astype(F32).T.astype(BF16)
        for head in range(HEADS):
            block = turned[head * HEAD_DIM : (head + 1) * HEAD_DIM, :]
            for group in range(groups):
                send_ref[head * groups + group, rows, :] = block
    lane = lanes_of(frames)
    for half in range(2):
        tiles = [
            q_ref[:, (3 * half + i) * LANES : (3 * half + i + 1) * LANES].astype(F32)
            for i in range(3)
        ]
        for i, block in enumerate(tiles_to_heads(tiles)):
            block = jnp.where(lane < HEAD_DIM, block, 0.0).astype(BF16)
            for group in range(groups):
                send_ref[(4 * half + i) * groups + group, Q_ROWS, :] = block[
                    group * sub : (group + 1) * sub
                ]


def fill_keys(got_ref, rows, turned, count):
    for source in range(count):
        at = slice(source * LANES, (source + 1) * LANES)
        turned[0:HEAD_DIM, at] = got_ref[source, rows, :]
        turned[HEAD_DIM:LANES, at] = jnp.zeros((LANES - HEAD_DIM, LANES), BF16)


def fill_natural(turned, natural, count):
    for source in range(count):
        at = slice(source * LANES, (source + 1) * LANES)
        natural[at, :] = turned[:, at].astype(F32).T.astype(BF16)


def forward_kernel(
    block, chunk, groups, place_ref, got_ref, send_ref, out_ref, log_ref, keys, values_t, values, scores
):
    count = got_ref.shape[0]
    key_count = keys.shape[1]
    sub = LANES // groups
    per = block // sub
    fill_keys(got_ref, K_ROWS, keys, count)
    fill_keys(got_ref, V_ROWS, values_t, count)
    fill_natural(values_t, values, count)

    def one_block(step, unused):
        rows = got_ref[pl.ds(step * per, per), Q_ROWS, :].reshape(block, LANES)
        peak = jnp.full((block, LANES), -jnp.inf, F32)
        for start in range(0, key_count, chunk):
            part = jnp.dot(rows, keys[:, start : start + chunk], preferred_element_type=F32)
            scores[:, start : start + chunk] = part
            for tile in range(0, chunk, LANES):
                peak = jnp.maximum(peak, part[:, tile : tile + LANES])
        peak = jnp.max(peak, axis=1, keepdims=True) * SCALE2
        total = jnp.zeros((block, LANES), F32)
        result = jnp.zeros((block, LANES), F32)
        for start in range(0, key_count, chunk):
            weights = jnp.exp2(scores[:, start : start + chunk] * SCALE2 - peak)
            for tile in range(0, chunk, LANES):
                total = total + weights[:, tile : tile + LANES]
            result = result + jnp.dot(
                weights.astype(BF16), values[start : start + chunk, :], preferred_element_type=F32
            )
        total = jnp.sum(total, axis=1, keepdims=True)
        here = (result / total).astype(BF16)
        at = pl.ds(pl.multiple_of(step * block, block), block)
        out_ref[at, :] = here
        log_ref[at, :] = jnp.broadcast_to(peak + jnp.log2(total), (block, LANES))
        send_ref[pl.ds(step * per, per), 0:sub, :] = here.reshape(per, sub, LANES)
        return 0

    lax.fori_loop(0, key_count // groups // block, one_block, 0)

    side = jnp.where(place_ref[0] % groups == groups - 1, -1, 1)
    for device in range(count):
        near = jnp.clip(device + side, 0, count - 1)
        send_ref[device, sub : 2 * sub, :] = send_ref[near, 0:sub, :]


def conv_kernel(
    groups,
    count,
    place_ref,
    got_ref,
    resid_ref,
    cot_ref,
    before_ref,
    after_ref,
    gain_ref,
    taps_ref,
    send_ref,
    out_ref,
    grad_ref,
    mixed,
    normed,
    grad_conv,
    scaled,
    sums,
):
    frames = resid_ref.shape[0]
    sub = frames // groups
    wide = frames + 2 * sub
    half_taps = (TAPS - 1) // 2
    edge = 16
    inner = frames + 2 * edge
    tiles = CH // LANES
    place = place_ref[0]

    square = jnp.zeros((wide, LANES), F32)
    for half in range(2):
        heads = []
        for i in range(4):
            first = (4 * half + i) * groups
            parts = [got_ref[first + groups - 1, sub : 2 * sub, :]]
            parts += [got_ref[first + group, 0:sub, :] for group in range(groups)]
            parts += [got_ref[first, sub : 2 * sub, :]]
            heads.append(jnp.concatenate(parts, axis=0).astype(F32))
        for i, attended in enumerate(heads_to_tiles(heads)):
            at = slice((3 * half + i) * LANES, (3 * half + i + 1) * LANES)
            block = jnp.concatenate(
                [before_ref[0:sub, at], resid_ref[:, at], after_ref[0:sub, at]], axis=0
            ).astype(F32)
            block = block + attended
            mixed[:, at] = block
            square = square + block * block
    inverse = lax.rsqrt(jnp.sum(square, axis=1, keepdims=True) * (1.0 / CH) + EPS)

    row = lax.broadcasted_iota(jnp.int32, (wide, LANES), 0)
    inside = ((row >= sub) | (place > 0)) & ((row < sub + frames) | (place < count - 1))
    lo, hi = sub - edge, sub - edge + inner
    row_inner = lax.broadcasted_iota(jnp.int32, (inner, LANES), 0) + lo
    inside_inner = ((row_inner >= sub) | (place > 0)) & (
        (row_inner < sub + frames) | (place < count - 1)
    )
    own = slice(sub, sub + frames)
    inverse_own = inverse[sub : sub + frames]

    dots = jnp.zeros((frames, LANES), F32)
    for tile in range(tiles):
        at = slice(tile * LANES, (tile + 1) * LANES)
        gain_row = gain_ref[0:1, at]
        value = (mixed[:, at] * inverse * gain_row).astype(BF16).astype(F32)
        normed[...] = jnp.where(inside, value, 0.0)
        conv = jnp.zeros((inner, LANES), F32)
        for tap in range(TAPS):
            first = lo + tap - half_taps
            conv = conv + taps_ref[tap : tap + 1, at] * normed[first : first + inner, :]
        sig = jax.nn.sigmoid(conv)
        out_ref[:, at] = (
            mixed[own, at] + (conv * sig)[edge : edge + frames]
        ).astype(BF16)
        cot = jnp.concatenate(
            [before_ref[sub : sub + edge, at], cot_ref[:, at], after_ref[sub : sub + edge, at]],
            axis=0,
        ).astype(F32)
        value = (cot * sig * (1.0 + conv * (1.0 - sig))).astype(BF16).astype(F32)
        grad_conv[...] = jnp.where(inside_inner, value, 0.0)
        grad_normed = jnp.zeros((frames, LANES), F32)
        grad_own = grad_conv[edge : edge + frames, :]
        for tap in range(TAPS):
            first = edge + half_taps - tap
            grad_normed = (
                grad_normed
                + taps_ref[tap : tap + 1, at] * grad_conv[first : first + frames, :]
            )
            first = sub + tap - half_taps
            sums[tap : tap + 1, at] = jnp.sum(
                grad_own * normed[first : first + frames, :], axis=0, keepdims=True
            )
        unit = mixed[own, at] * inverse_own
        sums[TAPS : TAPS + 1, at] = jnp.sum(grad_normed * unit, axis=0, keepdims=True)
        here = grad_normed * gain_row
        scaled[:, at] = here
        dots = dots + here * unit
    mean = jnp.sum(dots, axis=1, keepdims=True) * (1.0 / CH)

    lane = lanes_of(sub)
    sublane = lax.broadcasted_iota(jnp.int32, (8, LANES), 0)
    for half in range(2):
        grads = []
        for i in range(3):
            at = slice((3 * half + i) * LANES, (3 * half + i + 1) * LANES)
            unit = mixed[own, at] * inverse_own
            grad = cot_ref[:, at].astype(F32) + inverse_own * (scaled[:, at] - unit * mean)
            grad_ref[:, at] = grad.astype(BF16)
            grads.append(grad)
        for i, block in enumerate(tiles_to_heads(grads)):
            for group in range(groups):
                device = (4 * half + i) * groups + group
                eight = jnp.zeros((8, LANES), F32)
                for tile in range(tiles):
                    line = sums[device : device + 1, tile * LANES : (tile + 1) * LANES]
                    eight = jnp.where(sublane == tile, line, eight)
                spare = jnp.concatenate(
                    [roll_lanes(eight, 96 - 32 * a) for a in range(4)], axis=0
                )
                piece = jnp.where(lane < HEAD_DIM, block[group * sub : (group + 1) * sub], spare)
                send_ref[device] = piece.astype(BF16)


def backward_kernel(
    block,
    chunk,
    groups,
    got_ref,
    grads_ref,
    out_ref,
    log_ref,
    send_ref,
    keys_t,
    values_t,
    keys,
    grad_keys,
    grad_values,
):
    count = got_ref.shape[0]
    key_count = keys.shape[0]
    sub = LANES // groups
    per = block // sub
    fill_keys(got_ref, K_ROWS, keys_t, count)
    fill_keys(got_ref, V_ROWS, values_t, count)
    fill_natural(keys_t, keys, count)
    grad_keys[...] = jnp.zeros_like(grad_keys)
    grad_values[...] = jnp.zeros_like(grad_values)

    sums = jnp.zeros((sub, LANES), F32)
    for source in range(count):
        sums = sums + grads_ref[source].astype(F32)
    lane = lanes_of(block)
    lane_sub = lax.broadcasted_iota(jnp.int32, (per, sub, LANES), 2)

    def one_block(step, unused):
        rows = got_ref[pl.ds(step * per, per), Q_ROWS, :].reshape(block, LANES)
        grads = grads_ref[pl.ds(step * per, per), :, :].reshape(block, LANES).astype(F32)
        grads = jnp.where(lane < HEAD_DIM, grads, 0.0)
        at = pl.ds(pl.multiple_of(step * block, block), block)
        delta = jnp.sum(grads * out_ref[at, :].astype(F32), axis=1, keepdims=True)
        logs = jnp.concatenate([log_ref[at, :]] * (chunk // LANES), axis=1)
        rows_t = rows.astype(F32).T.astype(BF16)[0:HEAD_DIM]
        grads_t = grads.T.astype(BF16)[0:HEAD_DIM]
        grads = grads.astype(BF16)
        result = jnp.zeros((block, LANES), F32)
        for start in range(0, key_count, chunk):
            part = slice(start, start + chunk)
            logits = jnp.dot(rows, keys_t[:, part], preferred_element_type=F32)
            probs = jnp.exp2(logits * SCALE2 - logs)
            grad_probs = jnp.dot(grads, values_t[:, part], preferred_element_type=F32)
            grad_scores = (probs * (grad_probs - delta)).astype(BF16)
            result = result + jnp.dot(grad_scores, keys[part, :], preferred_element_type=F32)
            grad_keys[:, part] += jnp.dot(rows_t, grad_scores, preferred_element_type=F32)
            grad_values[:, part] += jnp.dot(
                grads_t, probs.astype(BF16), preferred_element_type=F32
            )
        piece = (result * SCALE).reshape(per, sub, LANES)
        piece = jnp.where(lane_sub < HEAD_DIM, piece, sums[None])
        send_ref[pl.ds(step * per, per), Q_ROWS, :] = piece.astype(BF16)
        return 0

    lax.fori_loop(0, key_count // groups // block, one_block, 0)
    for device in range(count):
        at = slice(device * LANES, (device + 1) * LANES)
        send_ref[device, K_ROWS, :] = (grad_keys[:, at] * SCALE).astype(BF16)
        send_ref[device, V_ROWS, :] = grad_values[:, at].astype(BF16)


def unpack_kernel(groups, got_ref, q_ref, k_ref, v_ref, gain_ref, taps_ref, turned):
    count = got_ref.shape[0]
    sub = LANES // groups
    for target, rows in ((k_ref, K_ROWS), (v_ref, V_ROWS)):
        for head in range(HEADS):
            total = got_ref[head * groups, rows, :].astype(F32)
            for group in range(1, groups):
                total = total + got_ref[head * groups + group, rows, :].astype(F32)
            turned[head * HEAD_DIM : (head + 1) * HEAD_DIM, :] = total
        for tile in range(CH // LANES):
            at = slice(tile * LANES, (tile + 1) * LANES)
            target[:, at] = turned[at, :].T.astype(BF16)
    for half in range(2):
        heads = [
            jnp.concatenate(
                [got_ref[(4 * half + i) * groups + group, Q_ROWS, :] for group in range(groups)],
                axis=0,
            ).astype(F32)
            for i in range(4)
        ]
        for i, block in enumerate(heads_to_tiles(heads)):
            at = slice((3 * half + i) * LANES, (3 * half + i + 1) * LANES)
            q_ref[:, at] = block.astype(BF16)
    lane = lanes_of(8)
    for device in range(count):
        piece = got_ref[device, Q_ROWS, :].astype(F32)
        eight = roll_lanes(piece[0:8], 32)
        for a in range(1, 4):
            eight = jnp.where(
                lane >= 32 * a, roll_lanes(piece[8 * a : 8 * a + 8], 32 * a - 96), eight
            )
        for tile in range(CH // LANES):
            at = slice(tile * LANES, (tile + 1) * LANES)
            if device < TAPS:
                taps_ref[device : device + 1, at] = eight[tile : tile + 1]
            else:
                gain_ref[:, at] = eight[tile : tile + 1]


def exchange(pieces):
    return lax.all_to_all(pieces, "tm", split_axis=0, concat_axis=0, tiled=True)


def local(resid, queries, keys, values, gain, taps, cotangent):
    count = lax.axis_size("tm")
    sections = lax.axis_size("section")
    groups = count // HEADS
    frames = resid.shape[1]
    sub = frames // groups
    total = frames * count
    per_device = total // groups
    place = lax.axis_index("tm").astype(jnp.int32).reshape(1)
    edge = 16
    block, chunk = 256, 512
    matmul = 2 * per_device * total * LANES

    resid, queries, keys, values, cotangent = (
        array[0] for array in (resid, queries, keys, values, cotangent)
    )
    up = [(i, i + 1) for i in range(count - 1)]
    down = [(i + 1, i) for i in range(count - 1)]
    before = lax.ppermute(
        jnp.concatenate([resid[frames - sub :], cotangent[frames - edge :]], axis=0), "tm", up
    )
    after = lax.ppermute(jnp.concatenate([resid[:sub], cotangent[:edge]], axis=0), "tm", down)

    pieces = jax.ShapeDtypeStruct((count, PIECE_ROWS, LANES), BF16)
    rows_shape = jax.ShapeDtypeStruct((frames, CH), BF16)
    sent = call(
        lambda *refs: pack_kernel(groups, *refs),
        pieces,
        [VMEM] * 3,
        [pltpu.VMEM((CH, LANES), BF16)],
        1000000,
        "pack_qkv",
    )(queries, keys, values)
    got = exchange(sent)

    results, head_out, logs = call(
        lambda *refs: forward_kernel(block, chunk, groups, *refs),
        (
            jax.ShapeDtypeStruct((count, 2 * sub, LANES), BF16),
            jax.ShapeDtypeStruct((per_device, LANES), BF16),
            jax.ShapeDtypeStruct((per_device, LANES), F32),
        ),
        [SMEM, VMEM],
        [
            pltpu.VMEM((LANES, total), BF16),
            pltpu.VMEM((LANES, total), BF16),
            pltpu.VMEM((total, LANES), BF16),
            pltpu.VMEM((block, total), F32),
        ],
        2 * matmul,
        "attend_forward",
        per_device * total,
    )(place, got)
    returned = exchange(results)

    grads_sent, block_out, grad_resid = call(
        lambda *refs: conv_kernel(groups, count, *refs),
        (
            jax.ShapeDtypeStruct((count, sub, LANES), BF16),
            rows_shape,
            rows_shape,
        ),
        [SMEM] + [VMEM] * 7,
        [
            pltpu.VMEM((frames + 2 * sub, CH), F32),
            pltpu.VMEM((frames + 2 * sub, LANES), F32),
            pltpu.VMEM((frames + 2 * edge, LANES), F32),
            pltpu.VMEM((frames, CH), F32),
            pltpu.VMEM((TAPS + 1, CH), F32),
        ],
        10000000,
        "conv_block",
    )(place, returned, resid, cotangent, before, after, gain, taps[0])
    grads_got = exchange(grads_sent)
    next_input = lax.ppermute(
        block_out, "section", [(i, (i + 1) % sections) for i in range(sections)]
    )

    grads_out = call(
        lambda *refs: backward_kernel(block, chunk, groups, *refs),
        pieces,
        [VMEM] * 4,
        [
            pltpu.VMEM((LANES, total), BF16),
            pltpu.VMEM((LANES, total), BF16),
            pltpu.VMEM((total, LANES), BF16),
            pltpu.VMEM((HEAD_DIM, total), F32),
            pltpu.VMEM((HEAD_DIM, total), F32),
        ],
        5 * matmul,
        "attend_backward",
        per_device * total,
    )(got, grads_got, head_out, logs)
    back = exchange(grads_out)

    grad_q, grad_k, grad_v, grad_gain, grad_taps = call(
        lambda *refs: unpack_kernel(groups, *refs),
        (
            rows_shape,
            rows_shape,
            rows_shape,
            jax.ShapeDtypeStruct((1, CH), F32),
            jax.ShapeDtypeStruct((TAPS, CH), F32),
        ),
        [VMEM],
        [pltpu.VMEM((CH, LANES), F32)],
        1000000,
        "unpack_grads",
    )(back)
    return (
        next_input[None],
        grad_resid[None],
        grad_q[None],
        grad_k[None],
        grad_v[None],
        grad_gain,
        grad_taps[None],
    )


def solution(mesh):
    rows = P("section", "tm", None)
    in_specs = (rows, rows, rows, rows, P("section", None), P("section", None, None), rows)
    out_specs = (rows, rows, rows, rows, rows, P("section", None), P("section", None, None))
    return jax.shard_map(local, mesh=mesh, in_specs=in_specs, out_specs=out_specs, check_vma=False)
```

```python
import math

import jax
import jax.numpy as jnp
from jax import lax
from jax.experimental import pallas as pl
from jax.experimental.pallas import tpu as pltpu
from jax.sharding import PartitionSpec as P

HEADS = 8
HEAD_DIM = 96
TAPS = 31
CH = 768
LANES = 128
EPS = 1e-06

SCALE = HEAD_DIM ** (-0.5)
SCALE2 = SCALE * math.log2(math.e)

F32 = jnp.float32
BF16 = jnp.bfloat16

KV_ROWS = slice(0, 96)
Q_ROWS = slice(96, 128)
PIECE_ROWS = 128
HALF = 64
SUB = 32

VMEM = pl.BlockSpec(memory_space=pltpu.VMEM)
SMEM = pl.BlockSpec(memory_space=pltpu.SMEM)
HBM = pl.BlockSpec(memory_space=pltpu.HBM)
MIB = 1024 * 1024


def lanes_of(rows):
    return lax.broadcasted_iota(jnp.int32, (rows, LANES), 1)


def roll_lanes(block, by):
    by = by % LANES
    return block if by == 0 else pltpu.roll(block, by, 1)


def heads_to_tiles(heads):
    lane = lanes_of(heads[0].shape[0])
    second = roll_lanes(heads[1], 96)
    third = roll_lanes(heads[2], 64)
    fourth = roll_lanes(heads[3], 32)
    return (
        jnp.where(lane < 96, heads[0], second),
        jnp.where(lane < 64, second, third),
        jnp.where(lane < 32, third, fourth),
    )


def tiles_to_heads(tiles):
    lane = lanes_of(tiles[0].shape[0])
    return (
        tiles[0],
        roll_lanes(jnp.where(lane >= 96, tiles[0], tiles[1]), 32),
        roll_lanes(jnp.where(lane >= 64, tiles[1], tiles[2]), 64),
        roll_lanes(tiles[2], 96),
    )


def call(kernel, out_shape, in_specs, out_specs, scratch, limit, flops, name, transcendentals=0):
    return pl.pallas_call(
        kernel,
        out_shape=out_shape,
        in_specs=in_specs,
        out_specs=out_specs,
        scratch_shapes=scratch,
        compiler_params=pltpu.CompilerParams(vmem_limit_bytes=limit * MIB),
        cost_estimate=pl.CostEstimate(
            flops=flops, bytes_accessed=2 * MIB, transcendentals=transcendentals
        ),
        name=name,
    )


def pack_kernel(groups, q_ref, k_ref, v_ref, send_ref, keys_t, values_t):
    frames = q_ref.shape[0]
    for source, turned in ((k_ref, keys_t), (v_ref, values_t)):
        for tile in range(CH // LANES):
            at = slice(tile * LANES, (tile + 1) * LANES)
            turned[at, :] = source[:, at].astype(F32).T
    lane = lanes_of(HEAD_DIM)
    for head in range(HEADS):
        at = slice(head * HEAD_DIM, (head + 1) * HEAD_DIM)
        keys_here, values_here = keys_t[at, :], values_t[at, :]
        halves = (
            jnp.where(lane < HALF, keys_here, roll_lanes(values_here, HALF)).astype(BF16),
            jnp.where(lane < HALF, roll_lanes(keys_here, HALF), values_here).astype(BF16),
        )
        for group in range(groups):
            send_ref[head * groups + group, KV_ROWS, :] = halves[group % 2]
    lane = lanes_of(frames)
    for half in range(2):
        tiles = [
            q_ref[:, (3 * half + i) * LANES : (3 * half + i + 1) * LANES].astype(F32)
            for i in range(3)
        ]
        for i, block in enumerate(tiles_to_heads(tiles)):
            block = jnp.where(lane < HEAD_DIM, block, 0.0).astype(BF16)
            for group in range(groups):
                send_ref[(4 * half + i) * groups + group, Q_ROWS, :] = block[
                    group * SUB : (group + 1) * SUB
                ]


def fill_half(half_ref, keys_t, values_t, keys, values):
    lane = lanes_of(HEAD_DIM)
    zeros = jnp.zeros((LANES - HEAD_DIM, LANES), F32)
    for pair in range(half_ref.shape[0] // 2):
        at = slice(pair * LANES, (pair + 1) * LANES)
        even = half_ref[2 * pair, KV_ROWS, :].astype(F32)
        odd = half_ref[2 * pair + 1, KV_ROWS, :].astype(F32)
        for turned, natural, block in (
            (keys_t, keys, jnp.where(lane < HALF, even, roll_lanes(odd, HALF))),
            (values_t, values, jnp.where(lane < HALF, roll_lanes(even, HALF), odd)),
        ):
            block = jnp.concatenate([block, zeros], axis=0)
            if turned is not None:
                turned[:, at] = block.astype(BF16)
            if natural is not None:
                natural[at, :] = block.T.astype(BF16)


def attend(got_ref, state, finish, block, chunk, keys, values, scores):
    key_count = keys.shape[1]
    per = block // SUB
    blocks = got_ref.shape[0] // per

    def rows_of(step):
        return got_ref[step * per : (step + 1) * per, Q_ROWS, :].reshape(block, LANES)

    def score(step, rows, start, peak):
        part = jnp.dot(rows, keys[:, start : start + chunk], preferred_element_type=F32)
        scores[step % 2, :, start : start + chunk] = part
        for tile in range(0, chunk, LANES):
            peak = jnp.maximum(peak, part[:, tile : tile + LANES])
        return peak

    lowest = jnp.full((block, LANES), -jnp.inf, F32)
    peak = lowest
    rows = rows_of(0)
    for start in range(0, key_count, chunk):
        peak = score(0, rows, start, peak)
    for step in range(blocks):
        at = slice(step * block, (step + 1) * block)
        top = jnp.broadcast_to(jnp.max(peak, axis=1, keepdims=True) * SCALE2, (block, LANES))
        if state is None:
            total = jnp.zeros((block, LANES), F32)
            result = jnp.zeros((block, LANES), F32)
        else:
            old = state[0][at, :]
            top = jnp.maximum(top, old)
            shrink = jnp.exp2(old - top)
            total = state[1][at, :] * shrink
            result = state[2][at, :] * shrink
        tops = jnp.concatenate([top] * (chunk // LANES), axis=1)
        peak = lowest
        if step + 1 < blocks:
            rows = rows_of(step + 1)
        for start in range(0, key_count, chunk):
            if step + 1 < blocks:
                peak = score(step + 1, rows, start, peak)
            weights = jnp.exp2(scores[step % 2, :, start : start + chunk] * SCALE2 - tops)
            for tile in range(0, chunk, LANES):
                total = total + weights[:, tile : tile + LANES]
            result = result + jnp.dot(
                weights.astype(BF16), values[start : start + chunk, :], preferred_element_type=F32
            )
        finish(at, top, total, result)


def forward_first_kernel(block, chunk, got_ref, top_ref, total_ref, result_ref, keys, values, scores):
    fill_half(got_ref, keys, None, None, values)

    def finish(at, top, total, result):
        top_ref[at, :] = top
        total_ref[at, :] = total
        result_ref[at, :] = result

    attend(got_ref, None, finish, block, chunk, keys, values, scores)


def forward_second_kernel(
    block,
    chunk,
    groups,
    place_ref,
    got_ref,
    swapped_ref,
    top_ref,
    total_ref,
    result_ref,
    send_ref,
    out_hbm,
    log_hbm,
    keys,
    values,
    scores,
    out_ref,
    log_ref,
    sems,
):
    fill_half(swapped_ref, keys, None, None, values)

    def finish(at, top, total, result):
        total = jnp.sum(total, axis=1, keepdims=True)
        out_ref[at, :] = (result / total).astype(BF16)
        log_ref[at, :] = top + jnp.log2(total)

    attend(got_ref, (top_ref, total_ref, result_ref), finish, block, chunk, keys, values, scores)
    copies = (
        pltpu.make_async_copy(out_ref, out_hbm, sems.at[0]),
        pltpu.make_async_copy(log_ref, log_hbm, sems.at[1]),
    )
    for copy in copies:
        copy.start()
    count = got_ref.shape[0]
    side = jnp.where(place_ref[0] % groups == groups - 1, -1, 1)
    lane = lanes_of(48)
    for device in range(count):
        near = jnp.clip(device + side, 0, count - 1)
        beside = out_ref[pl.ds(pl.multiple_of(near * SUB, SUB), SUB), :].astype(F32)
        own = out_ref[device * SUB : (device + 1) * SUB, :].astype(F32)
        tail = beside[16:32]
        spare = jnp.concatenate([roll_lanes(tail, by) for by in (96, 64, 32)], axis=0)
        piece = jnp.concatenate([own, beside[0:16]], axis=0)
        send_ref[device] = jnp.where(lane < HEAD_DIM, piece, spare).astype(BF16)
    for copy in copies:
        copy.wait()


def halo_of(piece):
    lane = lanes_of(16)
    tail = jnp.where(
        lane < 32,
        roll_lanes(piece[0:16], 32),
        jnp.where(lane < 64, roll_lanes(piece[16:32], 64), roll_lanes(piece[32:48], 96)),
    )
    return [piece[32:48], tail]


def conv_kernel(
    groups,
    count,
    place_ref,
    got_ref,
    resid_ref,
    cot_ref,
    before_ref,
    after_ref,
    gain_ref,
    taps_ref,
    send_ref,
    out_ref,
    grad_ref,
    mixed,
    normed,
    grad_conv,
    scaled,
    sums,
):
    frames = resid_ref.shape[0]
    sub = frames // groups
    wide = frames + 2 * sub
    half_taps = (TAPS - 1) // 2
    edge = 16
    inner = frames + 2 * edge
    tiles = CH // LANES
    place = place_ref[0]

    square = jnp.zeros((wide, LANES), F32)
    for half in range(2):
        heads = []
        for i in range(4):
            first = (4 * half + i) * groups
            before_piece = got_ref[first + groups - 1].astype(F32)
            after_piece = got_ref[first].astype(F32)
            parts = halo_of(before_piece)
            parts += [got_ref[first + group, 0:sub, :].astype(F32) for group in range(groups)]
            parts += halo_of(after_piece)
            heads.append(jnp.concatenate(parts, axis=0))
        for i, attended in enumerate(heads_to_tiles(heads)):
            at = slice((3 * half + i) * LANES, (3 * half + i + 1) * LANES)
            block = jnp.concatenate(
                [before_ref[0:sub, at], resid_ref[:, at], after_ref[0:sub, at]], axis=0
            ).astype(F32)
            block = block + attended
            mixed[:, at] = block
            square = square + block * block
    inverse = lax.rsqrt(jnp.sum(square, axis=1, keepdims=True) * (1.0 / CH) + EPS)

    row = lax.broadcasted_iota(jnp.int32, (wide, LANES), 0)
    inside = ((row >= sub) | (place > 0)) & ((row < sub + frames) | (place < count - 1))
    lo, hi = sub - edge, sub - edge + inner
    row_inner = lax.broadcasted_iota(jnp.int32, (inner, LANES), 0) + lo
    inside_inner = ((row_inner >= sub) | (place > 0)) & (
        (row_inner < sub + frames) | (place < count - 1)
    )
    own = slice(sub, sub + frames)
    inverse_own = inverse[sub : sub + frames]

    dots = jnp.zeros((frames, LANES), F32)
    for tile in range(tiles):
        at = slice(tile * LANES, (tile + 1) * LANES)
        gain_row = gain_ref[0:1, at]
        value = (mixed[:, at] * inverse * gain_row).astype(BF16).astype(F32)
        normed[...] = jnp.where(inside, value, 0.0)
        conv = jnp.zeros((inner, LANES), F32)
        for tap in range(TAPS):
            first = lo + tap - half_taps
            conv = conv + taps_ref[tap, :, at] * normed[first : first + inner, :]
        sig = jax.nn.sigmoid(conv)
        out_ref[:, at] = (
            mixed[own, at] + (conv * sig)[edge : edge + frames]
        ).astype(BF16)
        cot = jnp.concatenate(
            [before_ref[sub : sub + edge, at], cot_ref[:, at], after_ref[sub : sub + edge, at]],
            axis=0,
        ).astype(F32)
        value = (cot * sig * (1.0 + conv * (1.0 - sig))).astype(BF16).astype(F32)
        grad_conv[...] = jnp.where(inside_inner, value, 0.0)
        grad_normed = jnp.zeros((frames, LANES), F32)
        grad_own = grad_conv[edge : edge + frames, :]
        for tap in range(TAPS):
            first = edge + half_taps - tap
            grad_normed = (
                grad_normed
                + taps_ref[tap, :, at] * grad_conv[first : first + frames, :]
            )
            first = sub + tap - half_taps
            sums[tap : tap + 1, at] = jnp.sum(
                grad_own * normed[first : first + frames, :], axis=0, keepdims=True
            )
        unit = mixed[own, at] * inverse_own
        sums[TAPS : TAPS + 1, at] = jnp.sum(grad_normed * unit, axis=0, keepdims=True)
        here = grad_normed * gain_row
        scaled[:, at] = here
        dots = dots + here * unit
    mean = jnp.sum(dots, axis=1, keepdims=True) * (1.0 / CH)

    lane = lanes_of(sub)
    sublane = lax.broadcasted_iota(jnp.int32, (8, LANES), 0)
    for half in range(2):
        grads = []
        for i in range(3):
            at = slice((3 * half + i) * LANES, (3 * half + i + 1) * LANES)
            unit = mixed[own, at] * inverse_own
            grad = cot_ref[:, at].astype(F32) + inverse_own * (scaled[:, at] - unit * mean)
            grad_ref[:, at] = grad.astype(BF16)
            grads.append(grad)
        for i, block in enumerate(tiles_to_heads(grads)):
            for group in range(groups):
                device = (4 * half + i) * groups + group
                eight = jnp.zeros((8, LANES), F32)
                for tile in range(tiles):
                    line = sums[device : device + 1, tile * LANES : (tile + 1) * LANES]
                    eight = jnp.where(sublane == tile, line, eight)
                spare = jnp.concatenate(
                    [roll_lanes(eight, 96 - 32 * a) for a in range(4)], axis=0
                )
                piece = jnp.where(lane < HEAD_DIM, block[group * sub : (group + 1) * sub], spare)
                send_ref[device] = piece.astype(BF16)


def backward(
    half_ref,
    got_ref,
    grads_ref,
    out_hbm,
    log_hbm,
    part_ref,
    finish,
    block,
    chunk,
    keys_t,
    values_t,
    keys,
    grad_keys,
    grad_values,
    out_ref,
    log_ref,
    sems,
):
    copies = (
        pltpu.make_async_copy(out_hbm, out_ref, sems.at[0]),
        pltpu.make_async_copy(log_hbm, log_ref, sems.at[1]),
    )
    for copy in copies:
        copy.start()
    fill_half(half_ref, keys_t, values_t, keys, None)
    for copy in copies:
        copy.wait()
    key_count = keys.shape[0]
    per = block // SUB
    lane = lanes_of(block)
    for step in range(got_ref.shape[0] // per):
        sources = slice(step * per, (step + 1) * per)
        at = slice(step * block, (step + 1) * block)
        rows = got_ref[sources, Q_ROWS, :].reshape(block, LANES)
        grads = grads_ref[sources].reshape(block, LANES).astype(F32)
        grads = jnp.where(lane < HEAD_DIM, grads, 0.0)
        delta = jnp.sum(grads * out_ref[at, :].astype(F32), axis=1, keepdims=True)
        logs = jnp.concatenate([log_ref[at, :]] * (chunk // LANES), axis=1)
        rows_t = rows.astype(F32).T.astype(BF16)[0:HEAD_DIM]
        grads_t = grads.T.astype(BF16)[0:HEAD_DIM]
        grads = grads.astype(BF16)
        result = jnp.zeros((block, LANES), F32)
        for start in range(0, key_count, chunk):
            part = slice(start, start + chunk)
            logits = jnp.dot(rows, keys_t[:, part], preferred_element_type=F32)
            probs = jnp.exp2(logits * SCALE2 - logs)
            grad_probs = jnp.dot(grads, values_t[:, part], preferred_element_type=F32)
            grad_scores = (probs * (grad_probs - delta)).astype(BF16)
            result = result + jnp.dot(grad_scores, keys[part, :], preferred_element_type=F32)
            grad_k = jnp.dot(rows_t, grad_scores, preferred_element_type=F32)
            grad_v = jnp.dot(grads_t, probs.astype(BF16), preferred_element_type=F32)
            if step == 0:
                grad_keys[:, part] = grad_k
                grad_values[:, part] = grad_v
            else:
                grad_keys[:, part] += grad_k
                grad_values[:, part] += grad_v
        finish(step, sources, at, result * SCALE)
    lane = lanes_of(HEAD_DIM)
    for pair in range(got_ref.shape[0] // 2):
        at = slice(pair * LANES, (pair + 1) * LANES)
        grad_k = grad_keys[:, at] * SCALE
        grad_v = grad_values[:, at]
        part_ref[2 * pair] = jnp.where(lane < HALF, grad_k, roll_lanes(grad_v, HALF)).astype(BF16)
        part_ref[2 * pair + 1] = jnp.where(
            lane < HALF, roll_lanes(grad_k, HALF), grad_v
        ).astype(BF16)


def backward_first_kernel(
    block, chunk, swapped_ref, got_ref, grads_ref, out_hbm, log_hbm, part_ref, grad_q_ref, *scratch
):
    def finish(step, sources, at, result):
        grad_q_ref[at, :] = result

    backward(
        swapped_ref, got_ref, grads_ref, out_hbm, log_hbm, part_ref, finish, block, chunk, *scratch
    )


def backward_second_kernel(
    block,
    chunk,
    got_ref,
    grads_ref,
    out_hbm,
    log_hbm,
    grad_q_ref,
    part_ref,
    piece_ref,
    *scratch,
):
    sums = jnp.zeros((SUB, LANES), F32)
    for source in range(grads_ref.shape[0]):
        sums = sums + grads_ref[source].astype(F32)

    def finish(step, sources, at, result):
        result = (result + grad_q_ref[at, :]).reshape(-1, SUB, LANES)
        lane = lax.broadcasted_iota(jnp.int32, result.shape, 2)
        piece_ref[sources] = jnp.where(lane < HEAD_DIM, result, sums[None]).astype(BF16)

    backward(
        got_ref, got_ref, grads_ref, out_hbm, log_hbm, part_ref, finish, block, chunk, *scratch
    )


def join_kernel(part_ref, other_ref, piece_ref, send_ref):
    for device in range(part_ref.shape[0]):
        send_ref[device, KV_ROWS, :] = (
            part_ref[device].astype(F32) + other_ref[device].astype(F32)
        ).astype(BF16)
        send_ref[device, Q_ROWS, :] = piece_ref[device]


def unpack_kernel(
    groups, got_ref, arrived_ref, q_ref, k_ref, v_ref, gain_ref, taps_ref, next_ref, keys_t, values_t
):
    next_ref[...] = arrived_ref[...]
    count = got_ref.shape[0]
    lane = lanes_of(HEAD_DIM)
    for head in range(HEADS):
        at = slice(head * HEAD_DIM, (head + 1) * HEAD_DIM)
        low, high = (
            sum(
                got_ref[head * groups + group, KV_ROWS, :].astype(F32)
                for group in range(parity, groups, 2)
            )
            for parity in range(2)
        )
        keys_t[at, :] = jnp.where(lane < HALF, low, roll_lanes(high, HALF))
        values_t[at, :] = jnp.where(lane < HALF, roll_lanes(low, HALF), high)
    for target, turned in ((k_ref, keys_t), (v_ref, values_t)):
        for tile in range(CH // LANES):
            at = slice(tile * LANES, (tile + 1) * LANES)
            target[:, at] = turned[at, :].T.astype(BF16)
    for half in range(2):
        heads = [
            jnp.concatenate(
                [got_ref[(4 * half + i) * groups + group, Q_ROWS, :] for group in range(groups)],
                axis=0,
            ).astype(F32)
            for i in range(4)
        ]
        for i, block in enumerate(heads_to_tiles(heads)):
            at = slice((3 * half + i) * LANES, (3 * half + i + 1) * LANES)
            q_ref[:, at] = block.astype(BF16)
    lane = lanes_of(8)
    for device in range(count):
        piece = got_ref[device, Q_ROWS, :].astype(F32)
        eight = roll_lanes(piece[0:8], 32)
        for a in range(1, 4):
            eight = jnp.where(
                lane >= 32 * a, roll_lanes(piece[8 * a : 8 * a + 8], 32 * a - 96), eight
            )
        for tile in range(CH // LANES):
            at = slice(tile * LANES, (tile + 1) * LANES)
            if device < TAPS:
                taps_ref[device, :, at] = eight[tile : tile + 1]
            else:
                gain_ref[:, at] = eight[tile : tile + 1]


def exchange(pieces):
    return lax.all_to_all(pieces, "tm", split_axis=0, concat_axis=0, tiled=True)


def local(resid, queries, keys, values, gain, taps, cotangent):
    count = lax.axis_size("tm")
    sections = lax.axis_size("section")
    groups = count // HEADS
    frames = resid.shape[1]
    total = frames * count
    own = total // groups
    half = total // 2
    place = lax.axis_index("tm").astype(jnp.int32).reshape(1)
    edge = 16
    matmul = 2 * own * half * LANES

    resid, queries, keys, values, cotangent = (
        array[0] for array in (resid, queries, keys, values, cotangent)
    )
    up = [(i, i + 1) for i in range(count - 1)]
    down = [(i + 1, i) for i in range(count - 1)]
    partner = [(i, i ^ 1) for i in range(count)]
    before = lax.ppermute(
        jnp.concatenate([resid[frames - SUB :], cotangent[frames - edge :]], axis=0), "tm", up
    )
    after = lax.ppermute(jnp.concatenate([resid[:SUB], cotangent[:edge]], axis=0), "tm", down)

    shape = jax.ShapeDtypeStruct
    pieces = shape((count, PIECE_ROWS, LANES), BF16)
    rows_shape = shape((frames, CH), BF16)
    own_shape = shape((own, LANES), F32)
    sent = call(
        lambda *refs: pack_kernel(groups, *refs),
        pieces,
        [VMEM] * 3,
        VMEM,
        [pltpu.VMEM((CH, LANES), F32)] * 2,
        8,
        1000000,
        "pack_qkv",
    )(queries, keys, values)
    got = exchange(sent)
    swapped = lax.ppermute(got, "tm", partner)

    block, chunk = 256, 512
    attend_scratch = [
        pltpu.VMEM((LANES, half), BF16),
        pltpu.VMEM((half, LANES), BF16),
        pltpu.VMEM((2, block, half), F32),
    ]
    state = call(
        lambda *refs: forward_first_kernel(block, chunk, *refs),
        (own_shape,) * 3,
        [VMEM],
        (VMEM,) * 3,
        attend_scratch,
        24,
        2 * matmul,
        "attend_forward_own",
        own * half,
    )(got)
    results, head_out, logs = call(
        lambda *refs: forward_second_kernel(block, chunk, groups, *refs),
        (shape((count, 48, LANES), BF16), shape((own, LANES), BF16), own_shape),
        [SMEM] + [VMEM] * 5,
        (VMEM, HBM, HBM),
        attend_scratch
        + [
            pltpu.VMEM((own, LANES), BF16),
            pltpu.VMEM((own, LANES), F32),
            pltpu.SemaphoreType.DMA((2,)),
        ],
        24,
        2 * matmul,
        "attend_forward_other",
        own * half,
    )(place, got, swapped, *state)
    returned = exchange(results)

    grads_sent, block_out, grad_resid = call(
        lambda *refs: conv_kernel(groups, count, *refs),
        (shape((count, SUB, LANES), BF16), rows_shape, rows_shape),
        [SMEM] + [VMEM] * 7,
        (VMEM,) * 3,
        [
            pltpu.VMEM((frames + 2 * SUB, CH), F32),
            pltpu.VMEM((frames + 2 * SUB, LANES), F32),
            pltpu.VMEM((frames + 2 * edge, LANES), F32),
            pltpu.VMEM((frames, CH), F32),
            pltpu.VMEM((TAPS + 1, CH), F32),
        ],
        16,
        10000000,
        "conv_block",
    )(place, returned, resid, cotangent, before, after, gain, taps.reshape(TAPS, 1, CH))
    grads_got = exchange(grads_sent)
    arrived = lax.ppermute(
        block_out, "section", [(i, (i + 1) % sections) for i in range(sections)]
    )

    block, chunk = 512, 512
    backward_scratch = [
        pltpu.VMEM((LANES, half), BF16),
        pltpu.VMEM((LANES, half), BF16),
        pltpu.VMEM((half, LANES), BF16),
        pltpu.VMEM((HEAD_DIM, half), F32),
        pltpu.VMEM((HEAD_DIM, half), F32),
        pltpu.VMEM((own, LANES), BF16),
        pltpu.VMEM((own, LANES), F32),
        pltpu.SemaphoreType.DMA((2,)),
    ]
    part_shape = shape((count, HEAD_DIM, LANES), BF16)
    other_part, grad_q = call(
        lambda *refs: backward_first_kernel(block, chunk, *refs),
        (part_shape, own_shape),
        [VMEM] * 3 + [HBM] * 2,
        (VMEM,) * 2,
        backward_scratch,
        24,
        5 * matmul,
        "attend_backward_other",
        own * half,
    )(swapped, got, grads_got, head_out, logs)
    arrived_part = lax.ppermute(other_part, "tm", partner)
    own_part, grad_q_pieces = call(
        lambda *refs: backward_second_kernel(block, chunk, *refs),
        (part_shape, shape((count, SUB, LANES), BF16)),
        [VMEM] * 2 + [HBM] * 2 + [VMEM],
        (VMEM,) * 2,
        backward_scratch,
        24,
        5 * matmul,
        "attend_backward_own",
        own * half,
    )(got, grads_got, head_out, logs, grad_q)
    grads_out = call(
        join_kernel,
        pieces,
        [VMEM] * 3,
        VMEM,
        [],
        8,
        1000000,
        "join_grads",
    )(own_part, arrived_part, grad_q_pieces)
    back = exchange(grads_out)

    grad_q, grad_k, grad_v, grad_gain, grad_taps, next_input = call(
        lambda *refs: unpack_kernel(groups, *refs),
        (
            rows_shape,
            rows_shape,
            rows_shape,
            shape((1, CH), F32),
            shape((TAPS, 1, CH), F32),
            rows_shape,
        ),
        [VMEM] * 2,
        (VMEM,) * 6,
        [pltpu.VMEM((CH, LANES), F32)] * 2,
        8,
        1000000,
        "unpack_grads",
    )(back, arrived)
    return (
        next_input[None],
        grad_resid[None],
        grad_q[None],
        grad_k[None],
        grad_v[None],
        grad_gain,
        grad_taps.reshape(1, TAPS, CH),
    )


def solution(mesh):
    rows = P("section", "tm", None)
    in_specs = (rows, rows, rows, rows, P("section", None), P("section", None, None), rows)
    out_specs = (rows, rows, rows, rows, rows, P("section", None), P("section", None, None))
    return jax.shard_map(local, mesh=mesh, in_specs=in_specs, out_specs=out_specs, check_vma=False)
```

```python
import math

import jax
import jax.numpy as jnp
from jax import lax
from jax.experimental import pallas as pl
from jax.experimental.pallas import tpu as pltpu
from jax.sharding import PartitionSpec as P

HEADS = 8
HEAD_DIM = 96
TAPS = 31
CH = 768
LANES = 128
EPS = 1e-06

SCALE = HEAD_DIM ** (-0.5)
SCALE2 = SCALE * math.log2(math.e)

F32 = jnp.float32
BF16 = jnp.bfloat16

KV_ROWS = slice(0, 96)
Q_ROWS = slice(96, 128)
PIECE_ROWS = 128
HALF = 64
SUB = 32

VMEM = pl.BlockSpec(memory_space=pltpu.VMEM)
SMEM = pl.BlockSpec(memory_space=pltpu.SMEM)
ANY = pl.BlockSpec(memory_space=pl.ANY)
MIB = 1024 * 1024


def lanes_of(rows):
    return lax.broadcasted_iota(jnp.int32, (rows, LANES), 1)


def roll_lanes(block, by):
    by = by % LANES
    return block if by == 0 else pltpu.roll(block, by, 1)


def heads_to_tiles(heads):
    lane = lanes_of(heads[0].shape[0])
    second = roll_lanes(heads[1], 96)
    third = roll_lanes(heads[2], 64)
    fourth = roll_lanes(heads[3], 32)
    return (
        jnp.where(lane < 96, heads[0], second),
        jnp.where(lane < 64, second, third),
        jnp.where(lane < 32, third, fourth),
    )


def tiles_to_heads(tiles):
    lane = lanes_of(tiles[0].shape[0])
    return (
        tiles[0],
        roll_lanes(jnp.where(lane >= 96, tiles[0], tiles[1]), 32),
        roll_lanes(jnp.where(lane >= 64, tiles[1], tiles[2]), 64),
        roll_lanes(tiles[2], 96),
    )


def call(kernel, out_shape, in_specs, out_specs, scratch, limit, flops, name, transcendentals=0):
    return pl.pallas_call(
        kernel,
        out_shape=out_shape,
        in_specs=in_specs,
        out_specs=out_specs,
        scratch_shapes=scratch,
        compiler_params=pltpu.CompilerParams(vmem_limit_bytes=limit * MIB),
        cost_estimate=pl.CostEstimate(
            flops=flops, bytes_accessed=2 * MIB, transcendentals=transcendentals
        ),
        name=name,
    )


def pack_kernel(groups, q_ref, k_ref, v_ref, send_ref, keys_t, values_t):
    frames = q_ref.shape[0]
    for source, turned in ((k_ref, keys_t), (v_ref, values_t)):
        for tile in range(CH // LANES):
            at = slice(tile * LANES, (tile + 1) * LANES)
            turned[at, :] = source[:, at].astype(F32).T
    lane = lanes_of(HEAD_DIM)
    for head in range(HEADS):
        at = slice(head * HEAD_DIM, (head + 1) * HEAD_DIM)
        keys_here, values_here = keys_t[at, :], values_t[at, :]
        halves = (
            jnp.where(lane < HALF, keys_here, roll_lanes(values_here, HALF)).astype(BF16),
            jnp.where(lane < HALF, roll_lanes(keys_here, HALF), values_here).astype(BF16),
        )
        for group in range(groups):
            send_ref[head * groups + group, KV_ROWS, :] = halves[group % 2]
    lane = lanes_of(frames)
    for half in range(2):
        tiles = [
            q_ref[:, (3 * half + i) * LANES : (3 * half + i + 1) * LANES].astype(F32)
            for i in range(3)
        ]
        for i, block in enumerate(tiles_to_heads(tiles)):
            block = jnp.where(lane < HEAD_DIM, block, 0.0).astype(BF16)
            for group in range(groups):
                send_ref[(4 * half + i) * groups + group, Q_ROWS, :] = block[
                    group * SUB : (group + 1) * SUB
                ]


def fill_half(half_ref, keys_t, values_t, keys, values):
    lane = lanes_of(HEAD_DIM)
    zeros = jnp.zeros((LANES - HEAD_DIM, LANES), F32)
    for pair in range(half_ref.shape[0] // 2):
        at = slice(pair * LANES, (pair + 1) * LANES)
        even = half_ref[2 * pair, KV_ROWS, :].astype(F32)
        odd = half_ref[2 * pair + 1, KV_ROWS, :].astype(F32)
        for turned, natural, block in (
            (keys_t, keys, jnp.where(lane < HALF, even, roll_lanes(odd, HALF))),
            (values_t, values, jnp.where(lane < HALF, roll_lanes(even, HALF), odd)),
        ):
            block = jnp.concatenate([block, zeros], axis=0)
            if turned is not None:
                turned[:, at] = block.astype(BF16)
            if natural is not None:
                natural[at, :] = block.T.astype(BF16)


def attend(got_ref, state, finish, block, chunk, keys, values, scores):
    key_count = keys.shape[1]
    per = block // SUB
    blocks = got_ref.shape[0] // per

    def rows_of(step):
        return got_ref[step * per : (step + 1) * per, Q_ROWS, :].reshape(block, LANES)

    def score(step, rows, start, peak):
        part = jnp.dot(rows, keys[:, start : start + chunk], preferred_element_type=F32)
        scores[step % 2, :, start : start + chunk] = part
        for tile in range(0, chunk, LANES):
            peak = jnp.maximum(peak, part[:, tile : tile + LANES])
        return peak

    lowest = jnp.full((block, LANES), -jnp.inf, F32)
    peak = lowest
    rows = rows_of(0)
    for start in range(0, key_count, chunk):
        peak = score(0, rows, start, peak)
    for step in range(blocks):
        at = slice(step * block, (step + 1) * block)
        top = jnp.broadcast_to(jnp.max(peak, axis=1, keepdims=True) * SCALE2, (block, LANES))
        if state is None:
            total = jnp.zeros((block, LANES), F32)
            result = jnp.zeros((block, LANES), F32)
        else:
            old = state[0][at, :]
            top = jnp.maximum(top, old)
            shrink = jnp.exp2(old - top)
            total = state[1][at, :] * shrink
            result = state[2][at, :] * shrink
        tops = jnp.concatenate([top] * (chunk // LANES), axis=1)
        peak = lowest
        if step + 1 < blocks:
            rows = rows_of(step + 1)
        for start in range(0, key_count, chunk):
            if step + 1 < blocks:
                peak = score(step + 1, rows, start, peak)
            weights = jnp.exp2(scores[step % 2, :, start : start + chunk] * SCALE2 - tops)
            for tile in range(0, chunk, LANES):
                total = total + weights[:, tile : tile + LANES]
            result = result + jnp.dot(
                weights.astype(BF16), values[start : start + chunk, :], preferred_element_type=F32
            )
        finish(at, top, total, result)


def forward_first_kernel(
    block,
    chunk,
    got_ref,
    top_ref,
    total_ref,
    result_ref,
    keys,
    values,
    scores,
):
    fill_half(got_ref, keys, None, None, values)

    def finish(at, top, total, result):
        top_ref[at, :] = top
        total_ref[at, :] = total
        result_ref[at, :] = result

    attend(got_ref, None, finish, block, chunk, keys, values, scores)


def forward_second_kernel(
    block,
    chunk,
    groups,
    place_ref,
    got_ref,
    swapped_ref,
    top_ref,
    total_ref,
    result_ref,
    send_ref,
    out_ref,
    keys,
    values,
    scores,
):
    fill_half(swapped_ref, keys, None, None, values)

    def finish(at, top, total, result):
        total = jnp.sum(total, axis=1, keepdims=True)
        rest = top + jnp.log2(total)
        merged = result / total
        lane = lanes_of(block)
        for spot in range(HEAD_DIM, HEAD_DIM + 3):
            part = rest.astype(BF16).astype(F32)
            merged = jnp.where(lane == spot, part, merged)
            rest = rest - part
        out_ref[at, :] = merged.astype(BF16)

    attend(got_ref, (top_ref, total_ref, result_ref), finish, block, chunk, keys, values, scores)
    count = got_ref.shape[0]
    side = jnp.where(place_ref[0] % groups == groups - 1, -1, 1)
    lane = lanes_of(48)
    for device in range(count):
        near = jnp.clip(device + side, 0, count - 1)
        beside = out_ref[pl.ds(pl.multiple_of(near * SUB, SUB), SUB), :].astype(F32)
        own = out_ref[device * SUB : (device + 1) * SUB, :].astype(F32)
        tail = beside[16:32]
        spare = jnp.concatenate([roll_lanes(tail, by) for by in (96, 64, 32)], axis=0)
        piece = jnp.concatenate([own, beside[0:16]], axis=0)
        send_ref[device] = jnp.where(lane < HEAD_DIM, piece, spare).astype(BF16)


def halo_of(piece):
    lane = lanes_of(16)
    tail = jnp.where(
        lane < 32,
        roll_lanes(piece[0:16], 32),
        jnp.where(lane < 64, roll_lanes(piece[16:32], 64), roll_lanes(piece[32:48], 96)),
    )
    return [piece[32:48], tail]


def conv_kernel(
    groups,
    count,
    place_ref,
    got_ref,
    resid_ref,
    cot_ref,
    before_ref,
    after_ref,
    gain_ref,
    taps_ref,
    send_ref,
    out_ref,
    grad_ref,
    mixed,
    normed,
    grad_conv,
    scaled,
    sums,
):
    frames = resid_ref.shape[0]
    sub = frames // groups
    wide = frames + 2 * sub
    half_taps = (TAPS - 1) // 2
    edge = 16
    inner = frames + 2 * edge
    tiles = CH // LANES
    place = place_ref[0]

    square = jnp.zeros((wide, LANES), F32)
    for half in range(2):
        heads = []
        for i in range(4):
            first = (4 * half + i) * groups
            before_piece = got_ref[first + groups - 1].astype(F32)
            after_piece = got_ref[first].astype(F32)
            parts = halo_of(before_piece)
            parts += [got_ref[first + group, 0:sub, :].astype(F32) for group in range(groups)]
            parts += halo_of(after_piece)
            heads.append(jnp.concatenate(parts, axis=0))
        for i, attended in enumerate(heads_to_tiles(heads)):
            at = slice((3 * half + i) * LANES, (3 * half + i + 1) * LANES)
            block = jnp.concatenate(
                [before_ref[0:sub, at], resid_ref[:, at], after_ref[0:sub, at]], axis=0
            ).astype(F32)
            block = block + attended
            mixed[:, at] = block
            square = square + block * block
    inverse = lax.rsqrt(jnp.sum(square, axis=1, keepdims=True) * (1.0 / CH) + EPS)

    row = lax.broadcasted_iota(jnp.int32, (wide, LANES), 0)
    inside = ((row >= sub) | (place > 0)) & ((row < sub + frames) | (place < count - 1))
    lo, hi = sub - edge, sub - edge + inner
    row_inner = lax.broadcasted_iota(jnp.int32, (inner, LANES), 0) + lo
    inside_inner = ((row_inner >= sub) | (place > 0)) & (
        (row_inner < sub + frames) | (place < count - 1)
    )
    own = slice(sub, sub + frames)
    inverse_own = inverse[sub : sub + frames]

    dots = jnp.zeros((frames, LANES), F32)
    for tile in range(tiles):
        at = slice(tile * LANES, (tile + 1) * LANES)
        gain_row = gain_ref[0:1, at]
        value = (mixed[:, at] * inverse * gain_row).astype(BF16).astype(F32)
        normed[...] = jnp.where(inside, value, 0.0)
        conv = jnp.zeros((inner, LANES), F32)
        for tap in range(TAPS):
            first = lo + tap - half_taps
            conv = conv + taps_ref[tap, :, at] * normed[first : first + inner, :]
        sig = jax.nn.sigmoid(conv)
        out_ref[:, at] = (
            mixed[own, at] + (conv * sig)[edge : edge + frames]
        ).astype(BF16)
        cot = jnp.concatenate(
            [before_ref[sub : sub + edge, at], cot_ref[:, at], after_ref[sub : sub + edge, at]],
            axis=0,
        ).astype(F32)
        value = (cot * sig * (1.0 + conv * (1.0 - sig))).astype(BF16).astype(F32)
        grad_conv[...] = jnp.where(inside_inner, value, 0.0)
        grad_normed = jnp.zeros((frames, LANES), F32)
        grad_own = grad_conv[edge : edge + frames, :]
        for tap in range(TAPS):
            first = edge + half_taps - tap
            grad_normed = (
                grad_normed
                + taps_ref[tap, :, at] * grad_conv[first : first + frames, :]
            )
            first = sub + tap - half_taps
            sums[tap : tap + 1, at] = jnp.sum(
                grad_own * normed[first : first + frames, :], axis=0, keepdims=True
            )
        unit = mixed[own, at] * inverse_own
        sums[TAPS : TAPS + 1, at] = jnp.sum(grad_normed * unit, axis=0, keepdims=True)
        here = grad_normed * gain_row
        scaled[:, at] = here
        dots = dots + here * unit
    mean = jnp.sum(dots, axis=1, keepdims=True) * (1.0 / CH)

    lane = lanes_of(sub)
    sublane = lax.broadcasted_iota(jnp.int32, (8, LANES), 0)
    for half in range(2):
        grads = []
        for i in range(3):
            at = slice((3 * half + i) * LANES, (3 * half + i + 1) * LANES)
            unit = mixed[own, at] * inverse_own
            grad = cot_ref[:, at].astype(F32) + inverse_own * (scaled[:, at] - unit * mean)
            grad_ref[:, at] = grad.astype(BF16)
            grads.append(grad)
        for i, block in enumerate(tiles_to_heads(grads)):
            for group in range(groups):
                device = (4 * half + i) * groups + group
                eight = jnp.zeros((8, LANES), F32)
                for tile in range(tiles):
                    line = sums[device : device + 1, tile * LANES : (tile + 1) * LANES]
                    eight = jnp.where(sublane == tile, line, eight)
                spare = jnp.concatenate(
                    [roll_lanes(eight, 96 - 32 * a) for a in range(4)], axis=0
                )
                piece = jnp.where(lane < HEAD_DIM, block[group * sub : (group + 1) * sub], spare)
                send_ref[device] = piece.astype(BF16)


def prepare_kernel(
    block,
    chunk,
    half_ref,
    got_ref,
    out_ref,
    unused_ref,
    weights_ref,
    values_t,
    keys,
    keys_t,
):
    fill_half(half_ref, keys_t, values_t, keys, None)
    per = block // SUB
    lane = lanes_of(block)
    in_log = (lane >= HEAD_DIM) & (lane < HEAD_DIM + 3)
    for step in range(got_ref.shape[0] // per):
        at = slice(step * block, (step + 1) * block)
        rows = got_ref[step * per : (step + 1) * per, Q_ROWS, :].reshape(block, LANES)
        logs = jnp.where(in_log, out_ref[at, :].astype(F32), 0.0)
        logs = jnp.sum(logs, axis=1, keepdims=True)
        for start in range(0, keys.shape[0], chunk):
            part = slice(start, start + chunk)
            logits = jnp.dot(rows, keys_t[:, part], preferred_element_type=F32)
            weights_ref[at, part] = jnp.exp2(logits * SCALE2 - logs).astype(BF16)


def backward(
    weights_ref,
    values_t,
    keys,
    got_ref,
    grads_ref,
    out_ref,
    part_ref,
    finish,
    block,
    chunk,
    grad_keys,
    grad_values,
):
    key_count = keys.shape[0]
    per = block // SUB
    lane = lanes_of(block)
    for step in range(got_ref.shape[0] // per):
        sources = slice(step * per, (step + 1) * per)
        at = slice(step * block, (step + 1) * block)
        rows = got_ref[sources, Q_ROWS, :].reshape(block, LANES)
        grads = grads_ref[sources].reshape(block, LANES).astype(F32)
        grads = jnp.where(lane < HEAD_DIM, grads, 0.0)
        out = out_ref[at, :].astype(F32)
        delta = jnp.sum(grads * out, axis=1, keepdims=True)
        rows_t = rows.astype(F32).T.astype(BF16)[0:HEAD_DIM]
        grads_t = grads.T.astype(BF16)[0:HEAD_DIM]
        grads = grads.astype(BF16)
        result = jnp.zeros((block, LANES), F32)
        for start in range(0, key_count, chunk):
            part = slice(start, start + chunk)
            weights = weights_ref[at, part]
            grad_probs = jnp.dot(grads, values_t[:, part], preferred_element_type=F32)
            grad_scores = (weights.astype(F32) * (grad_probs - delta)).astype(BF16)
            result = result + jnp.dot(grad_scores, keys[part, :], preferred_element_type=F32)
            grad_k = jnp.dot(rows_t, grad_scores, preferred_element_type=F32)
            grad_v = jnp.dot(grads_t, weights, preferred_element_type=F32)
            if step == 0:
                grad_keys[:, part] = grad_k
                grad_values[:, part] = grad_v
            else:
                grad_keys[:, part] += grad_k
                grad_values[:, part] += grad_v
        finish(step, sources, at, result * SCALE)
    lane = lanes_of(HEAD_DIM)
    for pair in range(got_ref.shape[0] // 2):
        at = slice(pair * LANES, (pair + 1) * LANES)
        grad_k = grad_keys[:, at] * SCALE
        grad_v = grad_values[:, at]
        part_ref[2 * pair] = jnp.where(lane < HALF, grad_k, roll_lanes(grad_v, HALF)).astype(BF16)
        part_ref[2 * pair + 1] = jnp.where(
            lane < HALF, roll_lanes(grad_k, HALF), grad_v
        ).astype(BF16)


def backward_first_kernel(
    block,
    chunk,
    weights_ref,
    values_t,
    keys,
    got_ref,
    grads_ref,
    out_ref,
    part_ref,
    grad_q_ref,
    *scratch,
):
    def finish(step, sources, at, result):
        grad_q_ref[at, :] = result

    ready = (weights_ref, values_t, keys)
    backward(*ready, got_ref, grads_ref, out_ref, part_ref, finish, block, chunk, *scratch)


def backward_second_kernel(
    block,
    chunk,
    weights_ref,
    values_t,
    keys,
    got_ref,
    grads_ref,
    out_ref,
    grad_q_ref,
    part_ref,
    piece_ref,
    *scratch,
):
    sums = jnp.zeros((SUB, LANES), F32)
    for source in range(grads_ref.shape[0]):
        sums = sums + grads_ref[source].astype(F32)

    def finish(step, sources, at, result):
        result = (result + grad_q_ref[at, :]).reshape(-1, SUB, LANES)
        lane = lax.broadcasted_iota(jnp.int32, result.shape, 2)
        piece_ref[sources] = jnp.where(lane < HEAD_DIM, result, sums[None]).astype(BF16)

    ready = (weights_ref, values_t, keys)
    backward(*ready, got_ref, grads_ref, out_ref, part_ref, finish, block, chunk, *scratch)


def join_kernel(part_ref, other_ref, piece_ref, send_ref):
    for device in range(part_ref.shape[0]):
        send_ref[device, KV_ROWS, :] = (
            part_ref[device].astype(F32) + other_ref[device].astype(F32)
        ).astype(BF16)
        send_ref[device, Q_ROWS, :] = piece_ref[device]


def unpack_kernel(
    groups, got_ref, arrived_ref, q_ref, k_ref, v_ref, gain_ref, taps_ref, next_ref, keys_t, values_t
):
    next_ref[...] = arrived_ref[...]
    count = got_ref.shape[0]
    lane = lanes_of(HEAD_DIM)
    for head in range(HEADS):
        at = slice(head * HEAD_DIM, (head + 1) * HEAD_DIM)
        low, high = (
            sum(
                got_ref[head * groups + group, KV_ROWS, :].astype(F32)
                for group in range(parity, groups, 2)
            )
            for parity in range(2)
        )
        keys_t[at, :] = jnp.where(lane < HALF, low, roll_lanes(high, HALF))
        values_t[at, :] = jnp.where(lane < HALF, roll_lanes(low, HALF), high)
    for target, turned in ((k_ref, keys_t), (v_ref, values_t)):
        for tile in range(CH // LANES):
            at = slice(tile * LANES, (tile + 1) * LANES)
            target[:, at] = turned[at, :].T.astype(BF16)
    for half in range(2):
        heads = [
            jnp.concatenate(
                [got_ref[(4 * half + i) * groups + group, Q_ROWS, :] for group in range(groups)],
                axis=0,
            ).astype(F32)
            for i in range(4)
        ]
        for i, block in enumerate(heads_to_tiles(heads)):
            at = slice((3 * half + i) * LANES, (3 * half + i + 1) * LANES)
            q_ref[:, at] = block.astype(BF16)
    lane = lanes_of(8)
    for device in range(count):
        piece = got_ref[device, Q_ROWS, :].astype(F32)
        eight = roll_lanes(piece[0:8], 32)
        for a in range(1, 4):
            eight = jnp.where(
                lane >= 32 * a, roll_lanes(piece[8 * a : 8 * a + 8], 32 * a - 96), eight
            )
        for tile in range(CH // LANES):
            at = slice(tile * LANES, (tile + 1) * LANES)
            if device < TAPS:
                taps_ref[device, :, at] = eight[tile : tile + 1]
            else:
                gain_ref[:, at] = eight[tile : tile + 1]


def exchange(pieces):
    return lax.all_to_all(pieces, "tm", split_axis=0, concat_axis=0, tiled=True)


def local(resid, queries, keys, values, gain, taps, cotangent):
    count = lax.axis_size("tm")
    sections = lax.axis_size("section")
    groups = count // HEADS
    frames = resid.shape[1]
    total = frames * count
    own = total // groups
    half = total // 2
    place = lax.axis_index("tm").astype(jnp.int32).reshape(1)
    edge = 16
    matmul = 2 * own * half * LANES

    resid, queries, keys, values, cotangent = (
        array[0] for array in (resid, queries, keys, values, cotangent)
    )
    up = [(i, i + 1) for i in range(count - 1)]
    down = [(i + 1, i) for i in range(count - 1)]
    partner = [(i, i ^ 1) for i in range(count)]
    before = lax.ppermute(
        jnp.concatenate([resid[frames - SUB :], cotangent[frames - edge :]], axis=0), "tm", up
    )
    after = lax.ppermute(jnp.concatenate([resid[:SUB], cotangent[:edge]], axis=0), "tm", down)

    shape = jax.ShapeDtypeStruct
    pieces = shape((count, PIECE_ROWS, LANES), BF16)
    rows_shape = shape((frames, CH), BF16)
    own_shape = shape((own, LANES), F32)
    sent = call(
        lambda *refs: pack_kernel(groups, *refs),
        pieces,
        [VMEM] * 3,
        VMEM,
        [pltpu.VMEM((CH, LANES), F32)] * 2,
        8,
        1000000,
        "pack_qkv",
    )(queries, keys, values)
    got = exchange(sent)
    swapped = lax.ppermute(got, "tm", partner)

    block, chunk = 256, 512
    attend_scratch = [
        pltpu.VMEM((LANES, half), BF16),
        pltpu.VMEM((half, LANES), BF16),
        pltpu.VMEM((2, block, half), F32),
    ]
    state = call(
        lambda *refs: forward_first_kernel(block, chunk, *refs),
        (own_shape,) * 3,
        [VMEM],
        (VMEM,) * 3,
        attend_scratch,
        24,
        2 * matmul,
        "attend_forward_own",
        own * half,
    )(got)
    results, head_out = call(
        lambda *refs: forward_second_kernel(block, chunk, groups, *refs),
        (shape((count, 48, LANES), BF16), shape((own, LANES), BF16)),
        [SMEM] + [VMEM] * 5,
        (VMEM,) * 2,
        attend_scratch,
        24,
        2 * matmul,
        "attend_forward_other",
        own * half,
    )(place, got, swapped, *state)
    returned = exchange(results)

    grads_sent, block_out, grad_resid = call(
        lambda *refs: conv_kernel(groups, count, *refs),
        (shape((count, SUB, LANES), BF16), rows_shape, rows_shape),
        [SMEM] + [VMEM] * 7,
        (VMEM,) * 3,
        [
            pltpu.VMEM((frames + 2 * SUB, CH), F32),
            pltpu.VMEM((frames + 2 * SUB, LANES), F32),
            pltpu.VMEM((frames + 2 * edge, LANES), F32),
            pltpu.VMEM((frames, CH), F32),
            pltpu.VMEM((TAPS + 1, CH), F32),
        ],
        16,
        10000000,
        "conv_block",
    )(place, returned, resid, cotangent, before, after, gain, taps.reshape(TAPS, 1, CH))
    grads_got = exchange(grads_sent)
    arrived = lax.ppermute(
        block_out, "section", [(i, (i + 1) % sections) for i in range(sections)]
    )

    block, chunk = 512, 512
    other_ready, own_ready = (
        call(
            lambda *refs: prepare_kernel(block, chunk, *refs),
            (
                shape((own, half), BF16),
                shape((LANES, half), BF16),
                shape((half, LANES), BF16),
            ),
            [VMEM] * 3 + [ANY],
            (VMEM,) * 3,
            [pltpu.VMEM((LANES, half), BF16)],
            24,
            matmul,
            name,
            own * half,
        )(here, got, head_out, block_out)
        for here, name in ((swapped, "prepare_other"), (got, "prepare_own"))
    )
    backward_scratch = [
        pltpu.VMEM((HEAD_DIM, half), F32),
        pltpu.VMEM((HEAD_DIM, half), F32),
    ]
    part_shape = shape((count, HEAD_DIM, LANES), BF16)
    other_part, grad_q = call(
        lambda *refs: backward_first_kernel(block, chunk, *refs),
        (part_shape, own_shape),
        [VMEM] * 6,
        (VMEM,) * 2,
        backward_scratch,
        24,
        4 * matmul,
        "attend_backward_other",
    )(*other_ready, got, grads_got, head_out)
    arrived_part = lax.ppermute(other_part, "tm", partner)
    own_part, grad_q_pieces = call(
        lambda *refs: backward_second_kernel(block, chunk, *refs),
        (part_shape, shape((count, SUB, LANES), BF16)),
        [VMEM] * 7,
        (VMEM,) * 2,
        backward_scratch,
        24,
        4 * matmul,
        "attend_backward_own",
    )(*own_ready, got, grads_got, head_out, grad_q)
    grads_out = call(
        join_kernel,
        pieces,
        [VMEM] * 3,
        VMEM,
        [],
        8,
        1000000,
        "join_grads",
    )(own_part, arrived_part, grad_q_pieces)
    back = exchange(grads_out)

    grad_q, grad_k, grad_v, grad_gain, grad_taps, next_input = call(
        lambda *refs: unpack_kernel(groups, *refs),
        (
            rows_shape,
            rows_shape,
            rows_shape,
            shape((1, CH), F32),
            shape((TAPS, 1, CH), F32),
            rows_shape,
        ),
        [VMEM] * 2,
        (VMEM,) * 6,
        [pltpu.VMEM((CH, LANES), F32)] * 2,
        8,
        1000000,
        "unpack_grads",
    )(back, arrived)
    return (
        next_input[None],
        grad_resid[None],
        grad_q[None],
        grad_k[None],
        grad_v[None],
        grad_gain,
        grad_taps.reshape(1, TAPS, CH),
    )


def solution(mesh):
    rows = P("section", "tm", None)
    in_specs = (rows, rows, rows, rows, P("section", None), P("section", None, None), rows)
    out_specs = (rows, rows, rows, rows, rows, P("section", None), P("section", None, None))
    return jax.shard_map(local, mesh=mesh, in_specs=in_specs, out_specs=out_specs, check_vma=False)
```

```python
import math

import jax
import jax.numpy as jnp
from jax import lax
from jax.experimental import pallas as pl
from jax.experimental.pallas import tpu as pltpu
from jax.sharding import PartitionSpec as P

HEADS = 8
HEAD_DIM = 96
TAPS = 31
CH = 768
LANES = 128
EPS = 1e-06

SCALE = HEAD_DIM ** (-0.5)
SCALE2 = SCALE * math.log2(math.e)

F32 = jnp.float32
BF16 = jnp.bfloat16

KV_ROWS = slice(0, 96)
Q_ROWS = slice(96, 128)
PIECE_ROWS = 128
HALF = 64
SUB = 32

VMEM = pl.BlockSpec(memory_space=pltpu.VMEM)
SMEM = pl.BlockSpec(memory_space=pltpu.SMEM)
ANY = pl.BlockSpec(memory_space=pl.ANY)
MIB = 1024 * 1024


def lanes_of(rows):
    return lax.broadcasted_iota(jnp.int32, (rows, LANES), 1)


def roll_lanes(block, by):
    by = by % LANES
    return block if by == 0 else pltpu.roll(block, by, 1)


def heads_to_tiles(heads):
    lane = lanes_of(heads[0].shape[0])
    second = roll_lanes(heads[1], 96)
    third = roll_lanes(heads[2], 64)
    fourth = roll_lanes(heads[3], 32)
    return (
        jnp.where(lane < 96, heads[0], second),
        jnp.where(lane < 64, second, third),
        jnp.where(lane < 32, third, fourth),
    )


def tiles_to_heads(tiles):
    lane = lanes_of(tiles[0].shape[0])
    return (
        tiles[0],
        roll_lanes(jnp.where(lane >= 96, tiles[0], tiles[1]), 32),
        roll_lanes(jnp.where(lane >= 64, tiles[1], tiles[2]), 64),
        roll_lanes(tiles[2], 96),
    )


def call(kernel, out_shape, in_specs, out_specs, scratch, limit, flops, name, transcendentals=0, aliases={}):
    return pl.pallas_call(
        kernel,
        out_shape=out_shape,
        in_specs=in_specs,
        out_specs=out_specs,
        scratch_shapes=scratch,
        input_output_aliases=aliases,
        compiler_params=pltpu.CompilerParams(vmem_limit_bytes=limit * MIB),
        cost_estimate=pl.CostEstimate(
            flops=flops, bytes_accessed=2 * MIB, transcendentals=transcendentals
        ),
        name=name,
    )


def pack_kernel(
    groups, q_hbm, k_hbm, v_hbm, send_hbm, q_ref, k_ref, v_ref, send_ref, keys_t, values_t, sems, sent
):
    copies = [
        pltpu.make_async_copy(source, target, sems.at[i])
        for i, (source, target) in enumerate(((q_hbm, q_ref), (k_hbm, k_ref), (v_hbm, v_ref)))
    ]
    for copy in copies:
        copy.start()
    copies[0].wait()
    frames = q_ref.shape[0]
    lane = lanes_of(frames)
    for half in range(2):
        tiles = [
            q_ref[:, (3 * half + i) * LANES : (3 * half + i + 1) * LANES].astype(F32)
            for i in range(3)
        ]
        for i, block in enumerate(tiles_to_heads(tiles)):
            block = jnp.where(lane < HEAD_DIM, block, 0.0).astype(BF16)
            for group in range(groups):
                send_ref[(4 * half + i) * groups + group, Q_ROWS, :] = block[
                    group * SUB : (group + 1) * SUB
                ]
    for copy, source, turned in ((copies[1], k_ref, keys_t), (copies[2], v_ref, values_t)):
        copy.wait()
        for tile in range(CH // LANES):
            at = slice(tile * LANES, (tile + 1) * LANES)
            turned[at, :] = source[:, at].astype(F32).T
    lane = lanes_of(HEAD_DIM)
    out = []
    for head in range(HEADS):
        at = slice(head * HEAD_DIM, (head + 1) * HEAD_DIM)
        keys_here, values_here = keys_t[at, :], values_t[at, :]
        halves = (
            jnp.where(lane < HALF, keys_here, roll_lanes(values_here, HALF)).astype(BF16),
            jnp.where(lane < HALF, roll_lanes(keys_here, HALF), values_here).astype(BF16),
        )
        for group in range(groups):
            send_ref[head * groups + group, KV_ROWS, :] = halves[group % 2]
        devices = pl.ds(head * groups, groups)
        out.append(
            pltpu.make_async_copy(send_ref.at[devices], send_hbm.at[devices], sent.at[head])
        )
        out[-1].start()
    for copy in out:
        copy.wait()


def fill_half(half_ref, keys_t, values_t, keys, values):
    lane = lanes_of(HEAD_DIM)
    zeros = jnp.zeros((LANES - HEAD_DIM, LANES), F32)
    for pair in range(half_ref.shape[0] // 2):
        at = slice(pair * LANES, (pair + 1) * LANES)
        even = half_ref[2 * pair, KV_ROWS, :].astype(F32)
        odd = half_ref[2 * pair + 1, KV_ROWS, :].astype(F32)
        for turned, natural, block in (
            (keys_t, keys, jnp.where(lane < HALF, even, roll_lanes(odd, HALF))),
            (values_t, values, jnp.where(lane < HALF, roll_lanes(even, HALF), odd)),
        ):
            block = jnp.concatenate([block, zeros], axis=0)
            if turned is not None:
                turned[:, at] = block.astype(BF16)
            if natural is not None:
                natural[at, :] = block.T.astype(BF16)


def attend(got_ref, state, finish, block, chunk, keys, values, scores):
    key_count = keys.shape[1]
    per = block // SUB
    blocks = got_ref.shape[0] // per

    def rows_of(step):
        return got_ref[step * per : (step + 1) * per, Q_ROWS, :].reshape(block, LANES)

    def score(step, rows, start, peak):
        part = jnp.dot(rows, keys[:, start : start + chunk], preferred_element_type=F32)
        scores[step % 2, :, start : start + chunk] = part
        for tile in range(0, chunk, LANES):
            peak = jnp.maximum(peak, part[:, tile : tile + LANES])
        return peak

    lowest = jnp.full((block, LANES), -jnp.inf, F32)
    peak = lowest
    rows = rows_of(0)
    for start in range(0, key_count, chunk):
        peak = score(0, rows, start, peak)
    for step in range(blocks):
        at = slice(step * block, (step + 1) * block)
        top = jnp.broadcast_to(jnp.max(peak, axis=1, keepdims=True) * SCALE2, (block, LANES))
        if state is None:
            total = jnp.zeros((block, LANES), F32)
            result = jnp.zeros((block, LANES), F32)
        else:
            old = state[0][at, :]
            top = jnp.maximum(top, old)
            shrink = jnp.exp2(old - top)
            total = state[1][at, :] * shrink
            result = state[2][at, :] * shrink
        tops = jnp.concatenate([top] * (chunk // LANES), axis=1)
        peak = lowest
        if step + 1 < blocks:
            rows = rows_of(step + 1)
        for start in range(0, key_count, chunk):
            if step + 1 < blocks:
                peak = score(step + 1, rows, start, peak)
            weights = jnp.exp2(scores[step % 2, :, start : start + chunk] * SCALE2 - tops)
            for tile in range(0, chunk, LANES):
                total = total + weights[:, tile : tile + LANES]
            result = result + jnp.dot(
                weights.astype(BF16), values[start : start + chunk, :], preferred_element_type=F32
            )
        finish(at, top, total, result)


def forward_first_kernel(
    block,
    chunk,
    got_ref,
    top_ref,
    total_ref,
    result_ref,
    keys,
    values,
    scores,
):
    fill_half(got_ref, keys, None, None, values)

    def finish(at, top, total, result):
        top_ref[at, :] = top
        total_ref[at, :] = total
        result_ref[at, :] = result

    attend(got_ref, None, finish, block, chunk, keys, values, scores)


def forward_second_kernel(
    block,
    chunk,
    groups,
    place_ref,
    got_ref,
    swapped_ref,
    top_ref,
    total_ref,
    result_ref,
    send_ref,
    out_ref,
    keys,
    values,
    scores,
):
    fill_half(swapped_ref, keys, None, None, values)

    def finish(at, top, total, result):
        total = jnp.sum(total, axis=1, keepdims=True)
        rest = top + jnp.log2(total)
        merged = result / total
        lane = lanes_of(block)
        for spot in range(HEAD_DIM, HEAD_DIM + 3):
            part = rest.astype(BF16).astype(F32)
            merged = jnp.where(lane == spot, part, merged)
            rest = rest - part
        out_ref[at, :] = merged.astype(BF16)

    attend(got_ref, (top_ref, total_ref, result_ref), finish, block, chunk, keys, values, scores)
    count = got_ref.shape[0]
    side = jnp.where(place_ref[0] % groups == groups - 1, -1, 1)
    lane = lanes_of(48)
    for device in range(count):
        near = jnp.clip(device + side, 0, count - 1)
        beside = out_ref[pl.ds(pl.multiple_of(near * SUB, SUB), SUB), :].astype(F32)
        own = out_ref[device * SUB : (device + 1) * SUB, :].astype(F32)
        tail = beside[16:32]
        spare = jnp.concatenate([roll_lanes(tail, by) for by in (96, 64, 32)], axis=0)
        piece = jnp.concatenate([own, beside[0:16]], axis=0)
        send_ref[device] = jnp.where(lane < HEAD_DIM, piece, spare).astype(BF16)


def halo_of(piece):
    lane = lanes_of(16)
    tail = jnp.where(
        lane < 32,
        roll_lanes(piece[0:16], 32),
        jnp.where(lane < 64, roll_lanes(piece[16:32], 64), roll_lanes(piece[32:48], 96)),
    )
    return [piece[32:48], tail]


def conv_kernel(
    groups,
    count,
    place_ref,
    got_ref,
    resid_ref,
    cot_ref,
    before_ref,
    after_ref,
    gain_ref,
    taps_ref,
    send_ref,
    out_ref,
    grad_ref,
    mixed,
    normed,
    grad_conv,
    scaled,
    sums,
):
    frames = resid_ref.shape[0]
    sub = frames // groups
    wide = frames + 2 * sub
    half_taps = (TAPS - 1) // 2
    edge = 16
    inner = frames + 2 * edge
    tiles = CH // LANES
    place = place_ref[0]

    square = jnp.zeros((wide, LANES), F32)
    for half in range(2):
        heads = []
        for i in range(4):
            first = (4 * half + i) * groups
            before_piece = got_ref[first + groups - 1].astype(F32)
            after_piece = got_ref[first].astype(F32)
            parts = halo_of(before_piece)
            parts += [got_ref[first + group, 0:sub, :].astype(F32) for group in range(groups)]
            parts += halo_of(after_piece)
            heads.append(jnp.concatenate(parts, axis=0))
        for i, attended in enumerate(heads_to_tiles(heads)):
            at = slice((3 * half + i) * LANES, (3 * half + i + 1) * LANES)
            block = jnp.concatenate(
                [before_ref[0:sub, at], resid_ref[:, at], after_ref[0:sub, at]], axis=0
            ).astype(F32)
            block = block + attended
            mixed[:, at] = block
            square = square + block * block
    inverse = lax.rsqrt(jnp.sum(square, axis=1, keepdims=True) * (1.0 / CH) + EPS)

    row = lax.broadcasted_iota(jnp.int32, (wide, LANES), 0)
    inside = ((row >= sub) | (place > 0)) & ((row < sub + frames) | (place < count - 1))
    lo, hi = sub - edge, sub - edge + inner
    row_inner = lax.broadcasted_iota(jnp.int32, (inner, LANES), 0) + lo
    inside_inner = ((row_inner >= sub) | (place > 0)) & (
        (row_inner < sub + frames) | (place < count - 1)
    )
    own = slice(sub, sub + frames)
    inverse_own = inverse[sub : sub + frames]

    dots = jnp.zeros((frames, LANES), F32)
    for tile in range(tiles):
        at = slice(tile * LANES, (tile + 1) * LANES)
        gain_row = gain_ref[0:1, at]
        value = (mixed[:, at] * inverse * gain_row).astype(BF16).astype(F32)
        normed[...] = jnp.where(inside, value, 0.0)
        conv = jnp.zeros((inner, LANES), F32)
        for tap in range(TAPS):
            first = lo + tap - half_taps
            conv = conv + taps_ref[tap, :, at] * normed[first : first + inner, :]
        sig = jax.nn.sigmoid(conv)
        out_ref[:, at] = (
            mixed[own, at] + (conv * sig)[edge : edge + frames]
        ).astype(BF16)
        cot = jnp.concatenate(
            [before_ref[sub : sub + edge, at], cot_ref[:, at], after_ref[sub : sub + edge, at]],
            axis=0,
        ).astype(F32)
        value = (cot * sig * (1.0 + conv * (1.0 - sig))).astype(BF16).astype(F32)
        grad_conv[...] = jnp.where(inside_inner, value, 0.0)
        grad_normed = jnp.zeros((frames, LANES), F32)
        grad_own = grad_conv[edge : edge + frames, :]
        for tap in range(TAPS):
            first = edge + half_taps - tap
            grad_normed = (
                grad_normed
                + taps_ref[tap, :, at] * grad_conv[first : first + frames, :]
            )
            first = sub + tap - half_taps
            sums[tap : tap + 1, at] = jnp.sum(
                grad_own * normed[first : first + frames, :], axis=0, keepdims=True
            )
        unit = mixed[own, at] * inverse_own
        sums[TAPS : TAPS + 1, at] = jnp.sum(grad_normed * unit, axis=0, keepdims=True)
        here = grad_normed * gain_row
        scaled[:, at] = here
        dots = dots + here * unit
    mean = jnp.sum(dots, axis=1, keepdims=True) * (1.0 / CH)

    lane = lanes_of(sub)
    sublane = lax.broadcasted_iota(jnp.int32, (8, LANES), 0)
    for half in range(2):
        grads = []
        for i in range(3):
            at = slice((3 * half + i) * LANES, (3 * half + i + 1) * LANES)
            unit = mixed[own, at] * inverse_own
            grad = cot_ref[:, at].astype(F32) + inverse_own * (scaled[:, at] - unit * mean)
            grad_ref[:, at] = grad.astype(BF16)
            grads.append(grad)
        for i, block in enumerate(tiles_to_heads(grads)):
            for group in range(groups):
                device = (4 * half + i) * groups + group
                eight = jnp.zeros((8, LANES), F32)
                for tile in range(tiles):
                    line = sums[device : device + 1, tile * LANES : (tile + 1) * LANES]
                    eight = jnp.where(sublane == tile, line, eight)
                spare = jnp.concatenate(
                    [roll_lanes(eight, 96 - 32 * a) for a in range(4)], axis=0
                )
                piece = jnp.where(lane < HEAD_DIM, block[group * sub : (group + 1) * sub], spare)
                send_ref[device] = piece.astype(BF16)


def backward(
    half_ref,
    got_ref,
    grads_ref,
    out_ref,
    part_ref,
    finish,
    block,
    chunk,
    keys_t,
    values_t,
    keys,
    grad_keys,
    grad_values,
):
    fill_half(half_ref, keys_t, values_t, keys, None)
    key_count = keys.shape[0]
    per = block // SUB
    lane = lanes_of(block)
    for step in range(got_ref.shape[0] // per):
        sources = slice(step * per, (step + 1) * per)
        at = slice(step * block, (step + 1) * block)
        rows = got_ref[sources, Q_ROWS, :].reshape(block, LANES)
        grads = grads_ref[sources].reshape(block, LANES).astype(F32)
        grads = jnp.where(lane < HEAD_DIM, grads, 0.0)
        out = out_ref[at, :].astype(F32)
        delta = jnp.sum(grads * out, axis=1, keepdims=True)
        in_log = (lane >= HEAD_DIM) & (lane < HEAD_DIM + 3)
        logs = jnp.sum(jnp.where(in_log, out, 0.0), axis=1, keepdims=True)
        rows_t = rows.astype(F32).T.astype(BF16)[0:HEAD_DIM]
        grads_t = grads.T.astype(BF16)[0:HEAD_DIM]
        grads = grads.astype(BF16)
        result = jnp.zeros((block, LANES), F32)
        for start in range(0, key_count, chunk):
            part = slice(start, start + chunk)
            logits = jnp.dot(rows, keys_t[:, part], preferred_element_type=F32)
            probs = jnp.exp2(logits * SCALE2 - logs)
            grad_probs = jnp.dot(grads, values_t[:, part], preferred_element_type=F32)
            grad_scores = (probs * (grad_probs - delta)).astype(BF16)
            result = result + jnp.dot(grad_scores, keys[part, :], preferred_element_type=F32)
            grad_k = jnp.dot(rows_t, grad_scores, preferred_element_type=F32)
            grad_v = jnp.dot(grads_t, probs.astype(BF16), preferred_element_type=F32)
            if step == 0:
                grad_keys[:, part] = grad_k
                grad_values[:, part] = grad_v
            else:
                grad_keys[:, part] += grad_k
                grad_values[:, part] += grad_v
        finish(step, sources, at, result * SCALE)
    lane = lanes_of(HEAD_DIM)
    for pair in range(got_ref.shape[0] // 2):
        at = slice(pair * LANES, (pair + 1) * LANES)
        grad_k = grad_keys[:, at] * SCALE
        grad_v = grad_values[:, at]
        part_ref[2 * pair] = jnp.where(lane < HALF, grad_k, roll_lanes(grad_v, HALF)).astype(BF16)
        part_ref[2 * pair + 1] = jnp.where(
            lane < HALF, roll_lanes(grad_k, HALF), grad_v
        ).astype(BF16)


def backward_first_kernel(
    block,
    chunk,
    swapped_ref,
    got_ref,
    grads_ref,
    out_ref,
    part_ref,
    grad_q_ref,
    *scratch,
):
    def finish(step, sources, at, result):
        grad_q_ref[at, :] = result

    backward(
        swapped_ref, got_ref, grads_ref, out_ref, part_ref, finish, block, chunk, *scratch
    )


def backward_second_kernel(
    block,
    chunk,
    got_ref,
    grads_ref,
    out_ref,
    grad_q_ref,
    arrived_ref,
    part_ref,
    piece_ref,
    next_hbm,
    *scratch,
):
    *scratch, next_sem = scratch
    passed = pltpu.make_async_copy(arrived_ref, next_hbm, next_sem)
    passed.start()
    sums = jnp.zeros((SUB, LANES), F32)
    for source in range(grads_ref.shape[0]):
        sums = sums + grads_ref[source].astype(F32)

    def finish(step, sources, at, result):
        result = (result + grad_q_ref[at, :]).reshape(-1, SUB, LANES)
        lane = lax.broadcasted_iota(jnp.int32, result.shape, 2)
        piece_ref[sources] = jnp.where(lane < HEAD_DIM, result, sums[None]).astype(BF16)

    backward(
        got_ref, got_ref, grads_ref, out_ref, part_ref, finish, block, chunk, *scratch
    )
    passed.wait()


def join_kernel(part_ref, other_ref, piece_ref, send_ref):
    for device in range(part_ref.shape[0]):
        send_ref[device, KV_ROWS, :] = (
            part_ref[device].astype(F32) + other_ref[device].astype(F32)
        ).astype(BF16)
        send_ref[device, Q_ROWS, :] = piece_ref[device]


def unpack_kernel(
    groups, got_ref, q_ref, k_ref, v_ref, gain_ref, taps_ref, keys_t, values_t
):
    count = got_ref.shape[0]
    lane = lanes_of(HEAD_DIM)
    for head in range(HEADS):
        at = slice(head * HEAD_DIM, (head + 1) * HEAD_DIM)
        low, high = (
            sum(
                got_ref[head * groups + group, KV_ROWS, :].astype(F32)
                for group in range(parity, groups, 2)
            )
            for parity in range(2)
        )
        keys_t[at, :] = jnp.where(lane < HALF, low, roll_lanes(high, HALF))
        values_t[at, :] = jnp.where(lane < HALF, roll_lanes(low, HALF), high)
    for target, turned in ((k_ref, keys_t), (v_ref, values_t)):
        for tile in range(CH // LANES):
            at = slice(tile * LANES, (tile + 1) * LANES)
            target[:, at] = turned[at, :].T.astype(BF16)
    for half in range(2):
        heads = [
            jnp.concatenate(
                [got_ref[(4 * half + i) * groups + group, Q_ROWS, :] for group in range(groups)],
                axis=0,
            ).astype(F32)
            for i in range(4)
        ]
        for i, block in enumerate(heads_to_tiles(heads)):
            at = slice((3 * half + i) * LANES, (3 * half + i + 1) * LANES)
            q_ref[:, at] = block.astype(BF16)
    lane = lanes_of(8)
    for device in range(count):
        piece = got_ref[device, Q_ROWS, :].astype(F32)
        eight = roll_lanes(piece[0:8], 32)
        for a in range(1, 4):
            eight = jnp.where(
                lane >= 32 * a, roll_lanes(piece[8 * a : 8 * a + 8], 32 * a - 96), eight
            )
        for tile in range(CH // LANES):
            at = slice(tile * LANES, (tile + 1) * LANES)
            if device < TAPS:
                taps_ref[device, :, at] = eight[tile : tile + 1]
            else:
                gain_ref[:, at] = eight[tile : tile + 1]


def exchange(pieces):
    return lax.all_to_all(pieces, "tm", split_axis=0, concat_axis=0, tiled=True)


def local(resid, queries, keys, values, gain, taps, cotangent):
    count = lax.axis_size("tm")
    sections = lax.axis_size("section")
    groups = count // HEADS
    frames = resid.shape[1]
    total = frames * count
    own = total // groups
    half = total // 2
    place = lax.axis_index("tm").astype(jnp.int32).reshape(1)
    edge = 16
    matmul = 2 * own * half * LANES

    resid, queries, keys, values, cotangent = (
        array[0] for array in (resid, queries, keys, values, cotangent)
    )
    up = [(i, i + 1) for i in range(count - 1)]
    down = [(i + 1, i) for i in range(count - 1)]
    partner = [(i, i ^ 1) for i in range(count)]
    before = lax.ppermute(
        jnp.concatenate([resid[frames - SUB :], cotangent[frames - edge :]], axis=0), "tm", up
    )
    after = lax.ppermute(jnp.concatenate([resid[:SUB], cotangent[:edge]], axis=0), "tm", down)

    shape = jax.ShapeDtypeStruct
    pieces = shape((count, PIECE_ROWS, LANES), BF16)
    rows_shape = shape((frames, CH), BF16)
    own_shape = shape((own, LANES), F32)
    sent = call(
        lambda *refs: pack_kernel(groups, *refs),
        pieces,
        [ANY] * 3,
        ANY,
        [pltpu.VMEM((frames, CH), BF16)] * 3
        + [pltpu.VMEM((count, PIECE_ROWS, LANES), BF16)]
        + [pltpu.VMEM((CH, LANES), F32)] * 2
        + [pltpu.SemaphoreType.DMA((3,)), pltpu.SemaphoreType.DMA((HEADS,))],
        56,
        1000000,
        "pack_qkv",
    )(queries, keys, values)
    got = call(
        lambda *refs: None,
        pieces,
        [ANY] * 3,
        ANY,
        [],
        8,
        0,
        "received",
        aliases={0: 0},
    )(exchange(sent), before, after)
    swapped = lax.ppermute(got, "tm", partner)

    block, chunk = 256, 512
    attend_scratch = [
        pltpu.VMEM((LANES, half), BF16),
        pltpu.VMEM((half, LANES), BF16),
        pltpu.VMEM((2, block, half), F32),
    ]
    state = call(
        lambda *refs: forward_first_kernel(block, chunk, *refs),
        (own_shape,) * 3,
        [VMEM],
        (VMEM,) * 3,
        attend_scratch,
        24,
        2 * matmul,
        "attend_forward_own",
        own * half,
    )(got)
    results, head_out = call(
        lambda *refs: forward_second_kernel(block, chunk, groups, *refs),
        (shape((count, 48, LANES), BF16), shape((own, LANES), BF16)),
        [SMEM] + [VMEM] * 5,
        (VMEM,) * 2,
        attend_scratch,
        24,
        2 * matmul,
        "attend_forward_other",
        own * half,
    )(place, got, swapped, *state)
    returned = exchange(results)

    grads_sent, block_out, grad_resid = call(
        lambda *refs: conv_kernel(groups, count, *refs),
        (shape((count, SUB, LANES), BF16), rows_shape, rows_shape),
        [SMEM] + [VMEM] * 7,
        (VMEM,) * 3,
        [
            pltpu.VMEM((frames + 2 * SUB, CH), F32),
            pltpu.VMEM((frames + 2 * SUB, LANES), F32),
            pltpu.VMEM((frames + 2 * edge, LANES), F32),
            pltpu.VMEM((frames, CH), F32),
            pltpu.VMEM((TAPS + 1, CH), F32),
        ],
        16,
        10000000,
        "conv_block",
    )(place, returned, resid, cotangent, before, after, gain, taps.reshape(TAPS, 1, CH))
    grads_got = exchange(grads_sent)
    arrived = lax.ppermute(
        block_out, "section", [(i, (i + 1) % sections) for i in range(sections)]
    )

    block, chunk = 512, 512
    backward_scratch = [
        pltpu.VMEM((LANES, half), BF16),
        pltpu.VMEM((LANES, half), BF16),
        pltpu.VMEM((half, LANES), BF16),
        pltpu.VMEM((HEAD_DIM, half), F32),
        pltpu.VMEM((HEAD_DIM, half), F32),
    ]
    part_shape = shape((count, HEAD_DIM, LANES), BF16)
    other_part, grad_q = call(
        lambda *refs: backward_first_kernel(block, chunk, *refs),
        (part_shape, own_shape),
        [VMEM] * 4,
        (VMEM,) * 2,
        backward_scratch,
        24,
        1000000,
        "attend_backward_other",
    )(swapped, got, grads_got, head_out)
    arrived_part = lax.ppermute(other_part, "tm", partner)
    own_part, grad_q_pieces, next_input = call(
        lambda *refs: backward_second_kernel(block, chunk, *refs),
        (part_shape, shape((count, SUB, LANES), BF16), rows_shape),
        [VMEM] * 4 + [ANY],
        (VMEM,) * 2 + (ANY,),
        backward_scratch + [pltpu.SemaphoreType.DMA],
        24,
        5 * matmul,
        "attend_backward_own",
        own * half,
    )(got, grads_got, head_out, grad_q, arrived)
    grads_out = call(
        join_kernel,
        pieces,
        [VMEM] * 3,
        VMEM,
        [],
        8,
        1000000,
        "join_grads",
    )(own_part, arrived_part, grad_q_pieces)
    back = exchange(grads_out)

    grad_q, grad_k, grad_v, grad_gain, grad_taps = call(
        lambda *refs: unpack_kernel(groups, *refs),
        (
            rows_shape,
            rows_shape,
            rows_shape,
            shape((1, CH), F32),
            shape((TAPS, 1, CH), F32),
        ),
        [VMEM],
        (VMEM,) * 5,
        [pltpu.VMEM((CH, LANES), F32)] * 2,
        8,
        1000000,
        "unpack_grads",
    )(back)
    return (
        next_input[None],
        grad_resid[None],
        grad_q[None],
        grad_k[None],
        grad_v[None],
        grad_gain,
        grad_taps.reshape(1, TAPS, CH),
    )


def solution(mesh):
    rows = P("section", "tm", None)
    in_specs = (rows, rows, rows, rows, P("section", None), P("section", None, None), rows)
    out_specs = (rows, rows, rows, rows, rows, P("section", None), P("section", None, None))
    return jax.shard_map(local, mesh=mesh, in_specs=in_specs, out_specs=out_specs, check_vma=False)
```

```python
import math

import jax
import jax.numpy as jnp
from jax import lax
from jax.experimental import pallas as pl
from jax.experimental.pallas import tpu as pltpu
from jax.sharding import PartitionSpec as P

HEADS = 8
HEAD_DIM = 96
TAPS = 31
CH = 768
LANES = 128
EPS = 1e-06

SCALE = HEAD_DIM ** (-0.5)
SCALE2 = SCALE * math.log2(math.e)

F32 = jnp.float32
BF16 = jnp.bfloat16

KV_ROWS = slice(0, 96)
Q_ROWS = slice(96, 128)
PIECE_ROWS = 128
HALF = 64
SUB = 32

VMEM = pl.BlockSpec(memory_space=pltpu.VMEM)
SMEM = pl.BlockSpec(memory_space=pltpu.SMEM)
ANY = pl.BlockSpec(memory_space=pl.ANY)
MIB = 1024 * 1024


def lanes_of(rows):
    return lax.broadcasted_iota(jnp.int32, (rows, LANES), 1)


def roll_lanes(block, by):
    by = by % LANES
    return block if by == 0 else pltpu.roll(block, by, 1)


def heads_to_tiles(heads):
    lane = lanes_of(heads[0].shape[0])
    second = roll_lanes(heads[1], 96)
    third = roll_lanes(heads[2], 64)
    fourth = roll_lanes(heads[3], 32)
    return (
        jnp.where(lane < 96, heads[0], second),
        jnp.where(lane < 64, second, third),
        jnp.where(lane < 32, third, fourth),
    )


def tiles_to_heads(tiles):
    lane = lanes_of(tiles[0].shape[0])
    return (
        tiles[0],
        roll_lanes(jnp.where(lane >= 96, tiles[0], tiles[1]), 32),
        roll_lanes(jnp.where(lane >= 64, tiles[1], tiles[2]), 64),
        roll_lanes(tiles[2], 96),
    )


def call(kernel, out_shape, in_specs, out_specs, scratch, limit, flops, name, transcendentals=0, aliases={}):
    return pl.pallas_call(
        kernel,
        out_shape=out_shape,
        in_specs=in_specs,
        out_specs=out_specs,
        scratch_shapes=scratch,
        input_output_aliases=aliases,
        compiler_params=pltpu.CompilerParams(vmem_limit_bytes=limit * MIB),
        cost_estimate=pl.CostEstimate(
            flops=flops, bytes_accessed=2 * MIB, transcendentals=transcendentals
        ),
        name=name,
    )


def pack_kernel(
    groups, q_hbm, k_hbm, v_hbm, send_hbm, q_ref, k_ref, v_ref, send_ref, keys_t, values_t, sems, sent
):
    copies = [
        pltpu.make_async_copy(source, target, sems.at[i])
        for i, (source, target) in enumerate(((q_hbm, q_ref), (k_hbm, k_ref), (v_hbm, v_ref)))
    ]
    for copy in copies:
        copy.start()
    copies[0].wait()
    frames = q_ref.shape[0]
    lane = lanes_of(frames)
    for half in range(2):
        tiles = [
            q_ref[:, (3 * half + i) * LANES : (3 * half + i + 1) * LANES] for i in range(3)
        ]
        for i, block in enumerate(tiles_to_heads(tiles)):
            block = jnp.where(lane < HEAD_DIM, block, jnp.zeros_like(block))
            for group in range(groups):
                send_ref[(4 * half + i) * groups + group, Q_ROWS, :] = block[
                    group * SUB : (group + 1) * SUB
                ]
    for copy, source, turned in ((copies[1], k_ref, keys_t), (copies[2], v_ref, values_t)):
        copy.wait()
        for tile in range(CH // LANES):
            at = slice(tile * LANES, (tile + 1) * LANES)
            turned[at, :] = source[:, at].T
    lane = lanes_of(HEAD_DIM)
    out = []
    for head in range(HEADS):
        at = slice(head * HEAD_DIM, (head + 1) * HEAD_DIM)
        keys_here, values_here = keys_t[at, :], values_t[at, :]
        halves = (
            jnp.where(lane < HALF, keys_here, roll_lanes(values_here, HALF)),
            jnp.where(lane < HALF, roll_lanes(keys_here, HALF), values_here),
        )
        for group in range(groups):
            send_ref[head * groups + group, KV_ROWS, :] = halves[group % 2]
        devices = pl.ds(head * groups, groups)
        out.append(
            pltpu.make_async_copy(send_ref.at[devices], send_hbm.at[devices], sent.at[head])
        )
        out[-1].start()
    for copy in out:
        copy.wait()


def fill_half(half_ref, keys_t, values_t, keys, values):
    lane = lanes_of(HEAD_DIM)
    zeros = jnp.zeros((LANES - HEAD_DIM, LANES), BF16)
    for pair in range(half_ref.shape[0] // 2):
        at = slice(pair * LANES, (pair + 1) * LANES)
        even = half_ref[2 * pair, KV_ROWS, :]
        odd = half_ref[2 * pair + 1, KV_ROWS, :]
        for turned, natural, block in (
            (keys_t, keys, jnp.where(lane < HALF, even, roll_lanes(odd, HALF))),
            (values_t, values, jnp.where(lane < HALF, roll_lanes(even, HALF), odd)),
        ):
            block = jnp.concatenate([block, zeros], axis=0)
            if turned is not None:
                turned[:, at] = block
            if natural is not None:
                natural[at, :] = block.T


def attend(got_ref, state, finish, block, chunk, keys, values, scores):
    key_count = keys.shape[1]
    per = block // SUB
    blocks = got_ref.shape[0] // per

    def rows_of(step):
        return got_ref[step * per : (step + 1) * per, Q_ROWS, :].reshape(block, LANES)

    def score(step, rows, start, peak):
        part = jnp.dot(rows, keys[:, start : start + chunk], preferred_element_type=F32)
        scores[step % 2, :, start : start + chunk] = part
        for tile in range(0, chunk, LANES):
            peak = jnp.maximum(peak, part[:, tile : tile + LANES])
        return peak

    lowest = jnp.full((block, LANES), -jnp.inf, F32)
    peak = lowest
    rows = rows_of(0)
    for start in range(0, key_count, chunk):
        peak = score(0, rows, start, peak)
    for step in range(blocks):
        at = slice(step * block, (step + 1) * block)
        top = jnp.broadcast_to(jnp.max(peak, axis=1, keepdims=True) * SCALE2, (block, LANES))
        if state is None:
            total = jnp.zeros((block, LANES), F32)
            result = jnp.zeros((block, LANES), F32)
        else:
            old = state[0][at, :]
            top = jnp.maximum(top, old)
            shrink = jnp.exp2(old - top)
            total = state[1][at, :] * shrink
            result = state[2][at, :] * shrink
        tops = jnp.concatenate([top] * (chunk // LANES), axis=1)
        peak = lowest
        if step + 1 < blocks:
            rows = rows_of(step + 1)
        for start in range(0, key_count, chunk):
            if step + 1 < blocks:
                peak = score(step + 1, rows, start, peak)
            weights = jnp.exp2(scores[step % 2, :, start : start + chunk] * SCALE2 - tops)
            for tile in range(0, chunk, LANES):
                total = total + weights[:, tile : tile + LANES]
            result = result + jnp.dot(
                weights.astype(BF16), values[start : start + chunk, :], preferred_element_type=F32
            )
        finish(at, top, total, result)


def forward_first_kernel(
    block,
    chunk,
    got_ref,
    top_ref,
    total_ref,
    result_ref,
    keys,
    values,
    scores,
):
    fill_half(got_ref, keys, None, None, values)

    def finish(at, top, total, result):
        top_ref[at, :] = top
        total_ref[at, :] = total
        result_ref[at, :] = result

    attend(got_ref, None, finish, block, chunk, keys, values, scores)


def forward_second_kernel(
    block,
    chunk,
    groups,
    place_ref,
    got_ref,
    swapped_ref,
    top_ref,
    total_ref,
    result_ref,
    send_ref,
    out_ref,
    keys,
    values,
    scores,
):
    fill_half(swapped_ref, keys, None, None, values)

    def finish(at, top, total, result):
        total = jnp.sum(total, axis=1, keepdims=True)
        rest = top + jnp.log2(total)
        merged = result / total
        lane = lanes_of(block)
        for spot in range(HEAD_DIM, HEAD_DIM + 3):
            part = rest.astype(BF16).astype(F32)
            merged = jnp.where(lane == spot, part, merged)
            rest = rest - part
        out_ref[at, :] = merged.astype(BF16)

    attend(got_ref, (top_ref, total_ref, result_ref), finish, block, chunk, keys, values, scores)
    count = got_ref.shape[0]
    side = jnp.where(place_ref[0] % groups == groups - 1, -1, 1)
    lane = lanes_of(48)
    for device in range(count):
        near = jnp.clip(device + side, 0, count - 1)
        beside = out_ref[pl.ds(pl.multiple_of(near * SUB, SUB), SUB), :]
        own = out_ref[device * SUB : (device + 1) * SUB, :]
        tail = beside[16:32]
        spare = jnp.concatenate([roll_lanes(tail, by) for by in (96, 64, 32)], axis=0)
        piece = jnp.concatenate([own, beside[0:16]], axis=0)
        send_ref[device] = jnp.where(lane < HEAD_DIM, piece, spare)


def halo_of(piece):
    lane = lanes_of(16)
    tail = jnp.where(
        lane < 32,
        roll_lanes(piece[0:16], 32),
        jnp.where(lane < 64, roll_lanes(piece[16:32], 64), roll_lanes(piece[32:48], 96)),
    )
    return [piece[32:48], tail]


def conv_kernel(
    groups,
    count,
    place_ref,
    got_ref,
    resid_ref,
    cot_ref,
    before_ref,
    after_ref,
    gain_ref,
    taps_ref,
    send_ref,
    out_ref,
    grad_ref,
    mixed,
    normed,
    grad_conv,
    scaled,
    sums,
):
    frames = resid_ref.shape[0]
    sub = frames // groups
    wide = frames + 2 * sub
    half_taps = (TAPS - 1) // 2
    edge = 16
    inner = frames + 2 * edge
    tiles = CH // LANES
    place = place_ref[0]

    square = jnp.zeros((wide, LANES), F32)
    for half in range(2):
        heads = []
        for i in range(4):
            first = (4 * half + i) * groups
            before_piece = got_ref[first + groups - 1].astype(F32)
            after_piece = got_ref[first].astype(F32)
            parts = halo_of(before_piece)
            parts += [got_ref[first + group, 0:sub, :].astype(F32) for group in range(groups)]
            parts += halo_of(after_piece)
            heads.append(jnp.concatenate(parts, axis=0))
        for i, attended in enumerate(heads_to_tiles(heads)):
            at = slice((3 * half + i) * LANES, (3 * half + i + 1) * LANES)
            block = jnp.concatenate(
                [before_ref[0:sub, at], resid_ref[:, at], after_ref[0:sub, at]], axis=0
            ).astype(F32)
            block = block + attended
            mixed[:, at] = block
            square = square + block * block
    inverse = lax.rsqrt(jnp.sum(square, axis=1, keepdims=True) * (1.0 / CH) + EPS)

    row = lax.broadcasted_iota(jnp.int32, (wide, LANES), 0)
    inside = ((row >= sub) | (place > 0)) & ((row < sub + frames) | (place < count - 1))
    lo, hi = sub - edge, sub - edge + inner
    row_inner = lax.broadcasted_iota(jnp.int32, (inner, LANES), 0) + lo
    inside_inner = ((row_inner >= sub) | (place > 0)) & (
        (row_inner < sub + frames) | (place < count - 1)
    )
    own = slice(sub, sub + frames)
    inverse_own = inverse[sub : sub + frames]

    dots = jnp.zeros((frames, LANES), F32)
    for tile in range(tiles):
        at = slice(tile * LANES, (tile + 1) * LANES)
        gain_row = gain_ref[0:1, at]
        value = (mixed[:, at] * inverse * gain_row).astype(BF16).astype(F32)
        normed[...] = jnp.where(inside, value, 0.0)
        conv = jnp.zeros((inner, LANES), F32)
        for tap in range(TAPS):
            first = lo + tap - half_taps
            conv = conv + taps_ref[tap, :, at] * normed[first : first + inner, :]
        sig = jax.nn.sigmoid(conv)
        out_ref[:, at] = (
            mixed[own, at] + (conv * sig)[edge : edge + frames]
        ).astype(BF16)
        cot = jnp.concatenate(
            [before_ref[sub : sub + edge, at], cot_ref[:, at], after_ref[sub : sub + edge, at]],
            axis=0,
        ).astype(F32)
        value = (cot * sig * (1.0 + conv * (1.0 - sig))).astype(BF16).astype(F32)
        grad_conv[...] = jnp.where(inside_inner, value, 0.0)
        grad_normed = jnp.zeros((frames, LANES), F32)
        grad_own = grad_conv[edge : edge + frames, :]
        for tap in range(TAPS):
            first = edge + half_taps - tap
            grad_normed = (
                grad_normed
                + taps_ref[tap, :, at] * grad_conv[first : first + frames, :]
            )
            first = sub + tap - half_taps
            sums[tap : tap + 1, at] = jnp.sum(
                grad_own * normed[first : first + frames, :], axis=0, keepdims=True
            )
        unit = mixed[own, at] * inverse_own
        sums[TAPS : TAPS + 1, at] = jnp.sum(grad_normed * unit, axis=0, keepdims=True)
        here = grad_normed * gain_row
        scaled[:, at] = here
        dots = dots + here * unit
    mean = jnp.sum(dots, axis=1, keepdims=True) * (1.0 / CH)

    lane = lanes_of(sub)
    sublane = lax.broadcasted_iota(jnp.int32, (8, LANES), 0)
    for half in range(2):
        grads = []
        for i in range(3):
            at = slice((3 * half + i) * LANES, (3 * half + i + 1) * LANES)
            unit = mixed[own, at] * inverse_own
            grad = cot_ref[:, at].astype(F32) + inverse_own * (scaled[:, at] - unit * mean)
            grad_ref[:, at] = grad.astype(BF16)
            grads.append(grad)
        for i, block in enumerate(tiles_to_heads(grads)):
            for group in range(groups):
                device = (4 * half + i) * groups + group
                eight = jnp.zeros((8, LANES), F32)
                for tile in range(tiles):
                    line = sums[device : device + 1, tile * LANES : (tile + 1) * LANES]
                    eight = jnp.where(sublane == tile, line, eight)
                spare = jnp.concatenate(
                    [roll_lanes(eight, 96 - 32 * a) for a in range(4)], axis=0
                )
                piece = jnp.where(lane < HEAD_DIM, block[group * sub : (group + 1) * sub], spare)
                send_ref[device] = piece.astype(BF16)


def backward(
    half_ref,
    got_ref,
    grads_ref,
    out_ref,
    part_ref,
    finish,
    block,
    chunk,
    keys_t,
    values_t,
    keys,
    grad_keys,
    grad_values,
):
    fill_half(half_ref, keys_t, values_t, keys, None)
    key_count = keys.shape[0]
    per = block // SUB
    lane = lanes_of(block)
    for step in range(got_ref.shape[0] // per):
        sources = slice(step * per, (step + 1) * per)
        at = slice(step * block, (step + 1) * block)
        rows = got_ref[sources, Q_ROWS, :].reshape(block, LANES)
        grads = grads_ref[sources].reshape(block, LANES).astype(F32)
        grads = jnp.where(lane < HEAD_DIM, grads, 0.0)
        out = out_ref[at, :].astype(F32)
        delta = jnp.sum(grads * out, axis=1, keepdims=True)
        in_log = (lane >= HEAD_DIM) & (lane < HEAD_DIM + 3)
        logs = jnp.sum(jnp.where(in_log, out, 0.0), axis=1, keepdims=True)
        grads = grads.astype(BF16)
        rows_t = rows.T[0:HEAD_DIM]
        grads_t = grads.T[0:HEAD_DIM]
        result = jnp.zeros((block, LANES), F32)
        for start in range(0, key_count, chunk):
            part = slice(start, start + chunk)
            logits = jnp.dot(rows, keys_t[:, part], preferred_element_type=F32)
            probs = jnp.exp2(logits * SCALE2 - logs)
            grad_probs = jnp.dot(grads, values_t[:, part], preferred_element_type=F32)
            grad_scores = (probs * (grad_probs - delta)).astype(BF16)
            result = result + jnp.dot(grad_scores, keys[part, :], preferred_element_type=F32)
            grad_k = jnp.dot(rows_t, grad_scores, preferred_element_type=F32)
            grad_v = jnp.dot(grads_t, probs.astype(BF16), preferred_element_type=F32)
            if step == 0:
                grad_keys[:, part] = grad_k
                grad_values[:, part] = grad_v
            else:
                grad_keys[:, part] += grad_k
                grad_values[:, part] += grad_v
        finish(step, sources, at, result * SCALE)
    lane = lanes_of(HEAD_DIM)
    for pair in range(got_ref.shape[0] // 2):
        at = slice(pair * LANES, (pair + 1) * LANES)
        grad_k = (grad_keys[:, at] * SCALE).astype(BF16)
        grad_v = grad_values[:, at].astype(BF16)
        part_ref[2 * pair] = jnp.where(lane < HALF, grad_k, roll_lanes(grad_v, HALF))
        part_ref[2 * pair + 1] = jnp.where(lane < HALF, roll_lanes(grad_k, HALF), grad_v)


def backward_first_kernel(
    block,
    chunk,
    swapped_ref,
    got_ref,
    grads_ref,
    out_ref,
    part_ref,
    grad_q_ref,
    *scratch,
):
    def finish(step, sources, at, result):
        grad_q_ref[at, :] = result

    backward(
        swapped_ref, got_ref, grads_ref, out_ref, part_ref, finish, block, chunk, *scratch
    )


def backward_second_kernel(
    block,
    chunk,
    got_ref,
    grads_ref,
    out_ref,
    grad_q_ref,
    part_ref,
    piece_ref,
    *scratch,
):
    sums = jnp.zeros((SUB, LANES), F32)
    for source in range(grads_ref.shape[0]):
        sums = sums + grads_ref[source].astype(F32)

    def finish(step, sources, at, result):
        result = (result + grad_q_ref[at, :]).reshape(-1, SUB, LANES)
        lane = lax.broadcasted_iota(jnp.int32, result.shape, 2)
        piece_ref[sources] = jnp.where(lane < HEAD_DIM, result, sums[None]).astype(BF16)

    backward(
        got_ref, got_ref, grads_ref, out_ref, part_ref, finish, block, chunk, *scratch
    )


def join_kernel(part_ref, other_ref, piece_ref, send_ref):
    for device in range(part_ref.shape[0]):
        send_ref[device, KV_ROWS, :] = (
            part_ref[device].astype(F32) + other_ref[device].astype(F32)
        ).astype(BF16)
        send_ref[device, Q_ROWS, :] = piece_ref[device]


def unpack_kernel(
    groups, got_ref, arrived_ref, q_ref, k_ref, v_ref, gain_ref, taps_ref, next_ref, keys_t, values_t
):
    next_ref[...] = arrived_ref[...]
    count = got_ref.shape[0]
    lane = lanes_of(HEAD_DIM)
    for head in range(HEADS):
        at = slice(head * HEAD_DIM, (head + 1) * HEAD_DIM)
        low, high = (
            sum(
                got_ref[head * groups + group, KV_ROWS, :].astype(F32)
                for group in range(parity, groups, 2)
            ).astype(BF16)
            for parity in range(2)
        )
        keys_t[at, :] = jnp.where(lane < HALF, low, roll_lanes(high, HALF))
        values_t[at, :] = jnp.where(lane < HALF, roll_lanes(low, HALF), high)
    for target, turned in ((k_ref, keys_t), (v_ref, values_t)):
        for tile in range(CH // LANES):
            at = slice(tile * LANES, (tile + 1) * LANES)
            target[:, at] = turned[at, :].T
    for half in range(2):
        heads = [
            jnp.concatenate(
                [got_ref[(4 * half + i) * groups + group, Q_ROWS, :] for group in range(groups)],
                axis=0,
            )
            for i in range(4)
        ]
        for i, block in enumerate(heads_to_tiles(heads)):
            at = slice((3 * half + i) * LANES, (3 * half + i + 1) * LANES)
            q_ref[:, at] = block
    lane = lanes_of(8)
    for device in range(count):
        piece = got_ref[device, Q_ROWS, :].astype(F32)
        eight = roll_lanes(piece[0:8], 32)
        for a in range(1, 4):
            eight = jnp.where(
                lane >= 32 * a, roll_lanes(piece[8 * a : 8 * a + 8], 32 * a - 96), eight
            )
        for tile in range(CH // LANES):
            at = slice(tile * LANES, (tile + 1) * LANES)
            if device < TAPS:
                taps_ref[device, :, at] = eight[tile : tile + 1]
            else:
                gain_ref[:, at] = eight[tile : tile + 1]


def exchange(pieces):
    return lax.all_to_all(pieces, "tm", split_axis=0, concat_axis=0, tiled=True)


def local(resid, queries, keys, values, gain, taps, cotangent):
    count = lax.axis_size("tm")
    sections = lax.axis_size("section")
    groups = count // HEADS
    frames = resid.shape[1]
    total = frames * count
    own = total // groups
    half = total // 2
    place = lax.axis_index("tm").astype(jnp.int32).reshape(1)
    edge = 16
    matmul = 2 * own * half * LANES

    resid, queries, keys, values, cotangent = (
        array[0] for array in (resid, queries, keys, values, cotangent)
    )
    taps = taps.reshape(TAPS, 1, CH)
    up = [(i, i + 1) for i in range(count - 1)]
    down = [(i + 1, i) for i in range(count - 1)]
    partner = [(i, i ^ 1) for i in range(count)]
    before = lax.ppermute(
        jnp.concatenate([resid[frames - SUB :], cotangent[frames - edge :]], axis=0), "tm", up
    )
    after = lax.ppermute(jnp.concatenate([resid[:SUB], cotangent[:edge]], axis=0), "tm", down)

    shape = jax.ShapeDtypeStruct
    pieces = shape((count, PIECE_ROWS, LANES), BF16)
    rows_shape = shape((frames, CH), BF16)
    own_shape = shape((own, LANES), F32)
    sent = call(
        lambda *refs: pack_kernel(groups, *refs),
        pieces,
        [ANY] * 3,
        ANY,
        [pltpu.VMEM((frames, CH), BF16)] * 3
        + [pltpu.VMEM((count, PIECE_ROWS, LANES), BF16)]
        + [pltpu.VMEM((CH, LANES), BF16)] * 2
        + [pltpu.SemaphoreType.DMA((3,)), pltpu.SemaphoreType.DMA((HEADS,))],
        56,
        1000000,
        "pack_qkv",
    )(queries, keys, values)
    got = call(
        lambda *refs: None,
        pieces,
        [ANY] * 5,
        ANY,
        [],
        8,
        0,
        "received",
        aliases={0: 0},
    )(exchange(sent), before, after, gain, taps)
    swapped = lax.ppermute(got, "tm", partner)

    block, chunk = 256, 512
    attend_scratch = [
        pltpu.VMEM((LANES, half), BF16),
        pltpu.VMEM((half, LANES), BF16),
        pltpu.VMEM((2, block, half), F32),
    ]
    state = call(
        lambda *refs: forward_first_kernel(block, chunk, *refs),
        (own_shape,) * 3,
        [VMEM],
        (VMEM,) * 3,
        attend_scratch,
        24,
        2 * matmul,
        "attend_forward_own",
        own * half,
    )(got)
    results, head_out = call(
        lambda *refs: forward_second_kernel(block, chunk, groups, *refs),
        (shape((count, 48, LANES), BF16), shape((own, LANES), BF16)),
        [SMEM] + [VMEM] * 5,
        (VMEM,) * 2,
        attend_scratch,
        24,
        2 * matmul,
        "attend_forward_other",
        own * half,
    )(place, got, swapped, *state)
    returned = exchange(results)

    grads_sent, block_out, grad_resid = call(
        lambda *refs: conv_kernel(groups, count, *refs),
        (shape((count, SUB, LANES), BF16), rows_shape, rows_shape),
        [SMEM] + [VMEM] * 7,
        (VMEM,) * 3,
        [
            pltpu.VMEM((frames + 2 * SUB, CH), F32),
            pltpu.VMEM((frames + 2 * SUB, LANES), F32),
            pltpu.VMEM((frames + 2 * edge, LANES), F32),
            pltpu.VMEM((frames, CH), F32),
            pltpu.VMEM((TAPS + 1, CH), F32),
        ],
        16,
        10000000,
        "conv_block",
    )(place, returned, resid, cotangent, before, after, gain, taps)
    grads_got = exchange(grads_sent)
    arrived = lax.ppermute(
        block_out, "section", [(i, (i + 1) % sections) for i in range(sections)]
    )

    block, chunk = 512, 512
    backward_scratch = [
        pltpu.VMEM((LANES, half), BF16),
        pltpu.VMEM((LANES, half), BF16),
        pltpu.VMEM((half, LANES), BF16),
        pltpu.VMEM((HEAD_DIM, half), F32),
        pltpu.VMEM((HEAD_DIM, half), F32),
    ]
    part_shape = shape((count, HEAD_DIM, LANES), BF16)
    other_part, grad_q = call(
        lambda *refs: backward_first_kernel(block, chunk, *refs),
        (part_shape, own_shape),
        [VMEM] * 4,
        (VMEM,) * 2,
        backward_scratch,
        24,
        5 * matmul,
        "attend_backward_other",
    )(swapped, got, grads_got, head_out)
    arrived_part = lax.ppermute(other_part, "tm", partner)
    own_part, grad_q_pieces = call(
        lambda *refs: backward_second_kernel(block, chunk, *refs),
        (part_shape, shape((count, SUB, LANES), BF16)),
        [VMEM] * 4,
        (VMEM,) * 2,
        backward_scratch,
        24,
        5 * matmul,
        "attend_backward_own",
        own * half,
    )(got, grads_got, head_out, grad_q)
    grads_out = call(
        join_kernel,
        pieces,
        [VMEM] * 3,
        VMEM,
        [],
        8,
        1000000,
        "join_grads",
    )(own_part, arrived_part, grad_q_pieces)
    back = exchange(grads_out)

    grad_q, grad_k, grad_v, grad_gain, grad_taps, next_input = call(
        lambda *refs: unpack_kernel(groups, *refs),
        (
            rows_shape,
            rows_shape,
            rows_shape,
            shape((1, CH), F32),
            shape((TAPS, 1, CH), F32),
            rows_shape,
        ),
        [VMEM] * 2,
        (VMEM,) * 6,
        [pltpu.VMEM((CH, LANES), BF16)] * 2,
        8,
        1000000,
        "unpack_grads",
    )(back, arrived)
    return (
        next_input[None],
        grad_resid[None],
        grad_q[None],
        grad_k[None],
        grad_v[None],
        grad_gain,
        grad_taps.reshape(1, TAPS, CH),
    )


def solution(mesh):
    rows = P("section", "tm", None)
    in_specs = (rows, rows, rows, rows, P("section", None), P("section", None, None), rows)
    out_specs = (rows, rows, rows, rows, rows, P("section", None), P("section", None, None))
    return jax.shard_map(local, mesh=mesh, in_specs=in_specs, out_specs=out_specs, check_vma=False)
```

```python
import math

import jax
import jax.numpy as jnp
from jax import lax
from jax.experimental import pallas as pl
from jax.experimental.pallas import tpu as pltpu
from jax.sharding import PartitionSpec as P

HEADS = 8
HEAD_DIM = 96
TAPS = 31
CH = 768
LANES = 128
EPS = 1e-06

SCALE = HEAD_DIM ** (-0.5)
SCALE2 = SCALE * math.log2(math.e)

F32 = jnp.float32
BF16 = jnp.bfloat16

KV_ROWS = slice(0, 96)
Q_ROWS = slice(96, 128)
PIECE_ROWS = 128
HALF = 64
SUB = 32

VMEM = pl.BlockSpec(memory_space=pltpu.VMEM)
SMEM = pl.BlockSpec(memory_space=pltpu.SMEM)
ANY = pl.BlockSpec(memory_space=pl.ANY)
MIB = 1024 * 1024


def lanes_of(rows):
    return lax.broadcasted_iota(jnp.int32, (rows, LANES), 1)


def roll_lanes(block, by):
    by = by % LANES
    return block if by == 0 else pltpu.roll(block, by, 1)


def heads_to_tiles(heads):
    lane = lanes_of(heads[0].shape[0])
    second = roll_lanes(heads[1], 96)
    third = roll_lanes(heads[2], 64)
    fourth = roll_lanes(heads[3], 32)
    return (
        jnp.where(lane < 96, heads[0], second),
        jnp.where(lane < 64, second, third),
        jnp.where(lane < 32, third, fourth),
    )


def tiles_to_heads(tiles):
    lane = lanes_of(tiles[0].shape[0])
    return (
        tiles[0],
        roll_lanes(jnp.where(lane >= 96, tiles[0], tiles[1]), 32),
        roll_lanes(jnp.where(lane >= 64, tiles[1], tiles[2]), 64),
        roll_lanes(tiles[2], 96),
    )


def call(kernel, out_shape, in_specs, out_specs, scratch, limit, flops, name, transcendentals=0, aliases={}):
    return pl.pallas_call(
        kernel,
        out_shape=out_shape,
        in_specs=in_specs,
        out_specs=out_specs,
        scratch_shapes=scratch,
        input_output_aliases=aliases,
        compiler_params=pltpu.CompilerParams(vmem_limit_bytes=limit * MIB),
        cost_estimate=pl.CostEstimate(
            flops=flops, bytes_accessed=2 * MIB, transcendentals=transcendentals
        ),
        name=name,
    )


def pack_kernel(
    groups, q_hbm, k_hbm, v_hbm, send_hbm, q_ref, k_ref, v_ref, send_ref, keys_t, values_t, sems, sent
):
    copies = [
        pltpu.make_async_copy(source, target, sems.at[i])
        for i, (source, target) in enumerate(((q_hbm, q_ref), (k_hbm, k_ref), (v_hbm, v_ref)))
    ]
    for copy in copies:
        copy.start()
    copies[0].wait()
    frames = q_ref.shape[0]
    lane = lanes_of(frames)
    for half in range(2):
        tiles = [
            q_ref[:, (3 * half + i) * LANES : (3 * half + i + 1) * LANES] for i in range(3)
        ]
        for i, block in enumerate(tiles_to_heads(tiles)):
            block = jnp.where(lane < HEAD_DIM, block, jnp.zeros_like(block))
            for group in range(groups):
                send_ref[(4 * half + i) * groups + group, Q_ROWS, :] = block[
                    group * SUB : (group + 1) * SUB
                ]
    for copy, source, turned in ((copies[1], k_ref, keys_t), (copies[2], v_ref, values_t)):
        copy.wait()
        for tile in range(CH // LANES):
            at = slice(tile * LANES, (tile + 1) * LANES)
            turned[at, :] = source[:, at].T
    lane = lanes_of(HEAD_DIM)
    out = []
    for head in range(HEADS):
        at = slice(head * HEAD_DIM, (head + 1) * HEAD_DIM)
        keys_here, values_here = keys_t[at, :], values_t[at, :]
        halves = (
            jnp.where(lane < HALF, keys_here, roll_lanes(values_here, HALF)),
            jnp.where(lane < HALF, roll_lanes(keys_here, HALF), values_here),
        )
        for group in range(groups):
            send_ref[head * groups + group, KV_ROWS, :] = halves[group % 2]
        devices = pl.ds(head * groups, groups)
        out.append(
            pltpu.make_async_copy(send_ref.at[devices], send_hbm.at[devices], sent.at[head])
        )
        out[-1].start()
    for copy in out:
        copy.wait()


def fill_half(half_ref, start, stop, keys_t, values_t, keys, values):
    lane = lanes_of(HEAD_DIM)
    zeros = jnp.zeros((LANES - HEAD_DIM, LANES), BF16)
    for pair in range(start // LANES, stop // LANES):
        at = slice(pair * LANES, (pair + 1) * LANES)
        even = half_ref[2 * pair, KV_ROWS, :]
        odd = half_ref[2 * pair + 1, KV_ROWS, :]
        for turned, natural, block in (
            (keys_t, keys, jnp.where(lane < HALF, even, roll_lanes(odd, HALF))),
            (values_t, values, jnp.where(lane < HALF, roll_lanes(even, HALF), odd)),
        ):
            block = jnp.concatenate([block, zeros], axis=0)
            if turned is not None:
                turned[:, at] = block
            if natural is not None:
                natural[at, :] = block.T


def attend(got_ref, half_ref, state, finish, block, chunk, keys, values, scores):
    key_count = keys.shape[1]
    per = block // SUB
    blocks = got_ref.shape[0] // per

    def rows_of(step):
        return got_ref[step * per : (step + 1) * per, Q_ROWS, :].reshape(block, LANES)

    def score(step, rows, start, peak):
        part = jnp.dot(rows, keys[:, start : start + chunk], preferred_element_type=F32)
        scores[step % 2, :, start : start + chunk] = part
        for tile in range(0, chunk, LANES):
            peak = jnp.maximum(peak, part[:, tile : tile + LANES])
        return peak

    lowest = jnp.full((block, LANES), -jnp.inf, F32)
    peak = lowest
    rows = rows_of(0)
    for start in range(0, key_count, chunk):
        fill_half(half_ref, start, start + chunk, keys, None, None, values)
        peak = score(0, rows, start, peak)
    for step in range(blocks):
        at = slice(step * block, (step + 1) * block)
        top = jnp.broadcast_to(jnp.max(peak, axis=1, keepdims=True) * SCALE2, (block, LANES))
        if state is None:
            total = jnp.zeros((block, LANES), F32)
            result = jnp.zeros((block, LANES), F32)
        else:
            old = state[0][at, :]
            top = jnp.maximum(top, old)
            shrink = jnp.exp2(old - top)
            total = state[1][at, :] * shrink
            result = state[2][at, :] * shrink
        tops = jnp.concatenate([top] * (chunk // LANES), axis=1)
        peak = lowest
        if step + 1 < blocks:
            rows = rows_of(step + 1)
        for start in range(0, key_count, chunk):
            if step + 1 < blocks:
                peak = score(step + 1, rows, start, peak)
            weights = jnp.exp2(scores[step % 2, :, start : start + chunk] * SCALE2 - tops)
            for tile in range(0, chunk, LANES):
                total = total + weights[:, tile : tile + LANES]
            result = result + jnp.dot(
                weights.astype(BF16), values[start : start + chunk, :], preferred_element_type=F32
            )
        finish(at, top, total, result)


def forward_first_kernel(
    block,
    chunk,
    got_ref,
    top_ref,
    total_ref,
    result_ref,
    keys,
    values,
    scores,
):
    def finish(at, top, total, result):
        top_ref[at, :] = top
        total_ref[at, :] = total
        result_ref[at, :] = result

    attend(got_ref, got_ref, None, finish, block, chunk, keys, values, scores)


def forward_second_kernel(
    block,
    chunk,
    groups,
    place_ref,
    got_ref,
    swapped_ref,
    top_ref,
    total_ref,
    result_ref,
    send_ref,
    out_ref,
    keys,
    values,
    scores,
):
    def finish(at, top, total, result):
        total = jnp.sum(total, axis=1, keepdims=True)
        rest = top + jnp.log2(total)
        merged = result / total
        lane = lanes_of(block)
        for spot in range(HEAD_DIM, HEAD_DIM + 3):
            part = rest.astype(BF16).astype(F32)
            merged = jnp.where(lane == spot, part, merged)
            rest = rest - part
        out_ref[at, :] = merged.astype(BF16)

    state = (top_ref, total_ref, result_ref)
    attend(got_ref, swapped_ref, state, finish, block, chunk, keys, values, scores)
    count = got_ref.shape[0]
    side = jnp.where(place_ref[0] % groups == groups - 1, -1, 1)
    lane = lanes_of(48)
    for device in range(count):
        near = jnp.clip(device + side, 0, count - 1)
        beside = out_ref[pl.ds(pl.multiple_of(near * SUB, SUB), SUB), :]
        own = out_ref[device * SUB : (device + 1) * SUB, :]
        tail = beside[16:32]
        spare = jnp.concatenate([roll_lanes(tail, by) for by in (96, 64, 32)], axis=0)
        piece = jnp.concatenate([own, beside[0:16]], axis=0)
        send_ref[device] = jnp.where(lane < HEAD_DIM, piece, spare)


def halo_of(piece):
    lane = lanes_of(16)
    tail = jnp.where(
        lane < 32,
        roll_lanes(piece[0:16], 32),
        jnp.where(lane < 64, roll_lanes(piece[16:32], 64), roll_lanes(piece[32:48], 96)),
    )
    return [piece[32:48], tail]


def conv_kernel(
    groups,
    count,
    place_ref,
    got_ref,
    resid_ref,
    cot_ref,
    before_ref,
    after_ref,
    gain_ref,
    taps_ref,
    send_ref,
    out_ref,
    grad_ref,
    mixed,
    normed,
    grad_conv,
    scaled,
    sums,
    shifted,
    grad_wide,
):
    frames = resid_ref.shape[0]
    sub = frames // groups
    wide = frames + 2 * sub
    edge = 16
    inner = frames + 2 * edge
    tiles = CH // LANES
    place = place_ref[0]

    square = jnp.zeros((wide, LANES), F32)
    for half in range(2):
        heads = []
        for i in range(4):
            first = (4 * half + i) * groups
            before_piece = got_ref[first + groups - 1].astype(F32)
            after_piece = got_ref[first].astype(F32)
            parts = halo_of(before_piece)
            parts += [got_ref[first + group, 0:sub, :].astype(F32) for group in range(groups)]
            parts += halo_of(after_piece)
            heads.append(jnp.concatenate(parts, axis=0))
        for i, attended in enumerate(heads_to_tiles(heads)):
            at = slice((3 * half + i) * LANES, (3 * half + i + 1) * LANES)
            block = jnp.concatenate(
                [before_ref[0:sub, at], resid_ref[:, at], after_ref[0:sub, at]], axis=0
            ).astype(F32)
            block = block + attended
            mixed[:, at] = block
            square = square + block * block
    inverse = lax.rsqrt(jnp.sum(square, axis=1, keepdims=True) * (1.0 / CH) + EPS)

    row = lax.broadcasted_iota(jnp.int32, (wide, LANES), 0)
    inside = ((row >= sub) | (place > 0)) & ((row < sub + frames) | (place < count - 1))
    lo, hi = sub - edge, sub - edge + inner
    row_inner = lax.broadcasted_iota(jnp.int32, (inner, LANES), 0) + lo
    inside_inner = ((row_inner >= sub) | (place > 0)) & (
        (row_inner < sub + frames) | (place < count - 1)
    )
    own = slice(sub, sub + frames)
    inverse_own = inverse[sub : sub + frames]

    grad_wide[0:8, :] = jnp.zeros((8, LANES), F32)
    grad_wide[8 + frames : 16 + frames, :] = jnp.zeros((8, LANES), F32)
    dots = jnp.zeros((frames, LANES), F32)
    for tile in range(tiles):
        at = slice(tile * LANES, (tile + 1) * LANES)
        gain_row = gain_ref[0:1, at]
        value = (mixed[:, at] * inverse * gain_row).astype(BF16).astype(F32)
        normed[...] = jnp.where(inside, value, 0.0)
        conv = jnp.zeros((inner, LANES), F32)
        for b in range(8):
            part = jnp.zeros((inner + 8, LANES), F32)
            for tap in range(b, TAPS, 8):
                part = part + taps_ref[tap, :, at] * normed[tap - b : tap - b + inner + 8, :]
            shifted[...] = part
            conv = conv + shifted[b + 1 : b + 1 + inner, :]
        sig = jax.nn.sigmoid(conv)
        out_ref[:, at] = (
            mixed[own, at] + (conv * sig)[edge : edge + frames]
        ).astype(BF16)
        cot = jnp.concatenate(
            [before_ref[sub : sub + edge, at], cot_ref[:, at], after_ref[sub : sub + edge, at]],
            axis=0,
        ).astype(F32)
        value = (cot * sig * (1.0 + conv * (1.0 - sig))).astype(BF16).astype(F32)
        grad_conv[...] = jnp.where(inside_inner, value, 0.0)
        grad_normed = jnp.zeros((frames, LANES), F32)
        grad_wide[8 : 8 + frames, :] = grad_conv[edge : edge + frames, :]
        for b in range(8):
            part = jnp.zeros((frames + 8, LANES), F32)
            grad_here = grad_wide[7 - b : 15 - b + frames, :]
            for tap in range(b, TAPS, 8):
                first = tap - b
                part = part + taps_ref[TAPS - 1 - tap, :, at] * grad_conv[first : first + frames + 8, :]
                first = first + edge
                sums[tap : tap + 1, at] = jnp.sum(
                    grad_here * normed[first : first + frames + 8, :], axis=0, keepdims=True
                )
            shifted[0 : frames + 8, :] = part
            grad_normed = grad_normed + shifted[b + 1 : b + 1 + frames, :]
        unit = mixed[own, at] * inverse_own
        sums[TAPS : TAPS + 1, at] = jnp.sum(grad_normed * unit, axis=0, keepdims=True)
        here = grad_normed * gain_row
        scaled[:, at] = here
        dots = dots + here * unit
    mean = jnp.sum(dots, axis=1, keepdims=True) * (1.0 / CH)

    lane = lanes_of(sub)
    sublane = lax.broadcasted_iota(jnp.int32, (8, LANES), 0)
    for half in range(2):
        grads = []
        for i in range(3):
            at = slice((3 * half + i) * LANES, (3 * half + i + 1) * LANES)
            unit = mixed[own, at] * inverse_own
            grad = cot_ref[:, at].astype(F32) + inverse_own * (scaled[:, at] - unit * mean)
            grad_ref[:, at] = grad.astype(BF16)
            grads.append(grad)
        for i, block in enumerate(tiles_to_heads(grads)):
            for group in range(groups):
                device = (4 * half + i) * groups + group
                eight = jnp.zeros((8, LANES), F32)
                for tile in range(tiles):
                    line = sums[device : device + 1, tile * LANES : (tile + 1) * LANES]
                    eight = jnp.where(sublane == tile, line, eight)
                spare = jnp.concatenate(
                    [roll_lanes(eight, 96 - 32 * a) for a in range(4)], axis=0
                )
                piece = jnp.where(lane < HEAD_DIM, block[group * sub : (group + 1) * sub], spare)
                send_ref[device] = piece.astype(BF16)


def backward(
    half_ref,
    got_ref,
    grads_ref,
    out_ref,
    part_ref,
    finish,
    block,
    chunk,
    keys_t,
    values_t,
    keys,
    grad_keys,
    grad_values,
):
    fill_half(half_ref, 0, chunk, keys_t, values_t, keys, None)
    key_count = keys.shape[0]
    steps = got_ref.shape[0] * SUB // block
    lane_part = lanes_of(HEAD_DIM)
    per = block // SUB
    lane = lanes_of(block)
    for step in range(steps):
        sources = slice(step * per, (step + 1) * per)
        at = slice(step * block, (step + 1) * block)
        rows = got_ref[sources, Q_ROWS, :].reshape(block, LANES)
        grads = grads_ref[sources].reshape(block, LANES).astype(F32)
        grads = jnp.where(lane < HEAD_DIM, grads, 0.0)
        out = out_ref[at, :].astype(F32)
        delta = jnp.sum(grads * out, axis=1, keepdims=True)
        in_log = (lane >= HEAD_DIM) & (lane < HEAD_DIM + 3)
        logs = jnp.sum(jnp.where(in_log, out, 0.0), axis=1, keepdims=True)
        grads = grads.astype(BF16)
        rows_t = rows.T[0:HEAD_DIM]
        grads_t = grads.T[0:HEAD_DIM]
        result = jnp.zeros((block, LANES), F32)
        for start in range(0, key_count, chunk):
            part = slice(start, start + chunk)
            if step == 0 and start + chunk < key_count:
                fill_half(
                    half_ref, start + chunk, start + 2 * chunk, keys_t, values_t, keys, None
                )
            logits = jnp.dot(rows, keys_t[:, part], preferred_element_type=F32)
            probs = jnp.exp2(logits * SCALE2 - logs)
            grad_probs = jnp.dot(grads, values_t[:, part], preferred_element_type=F32)
            grad_scores = (probs * (grad_probs - delta)).astype(BF16)
            result = result + jnp.dot(grad_scores, keys[part, :], preferred_element_type=F32)
            grad_k = jnp.dot(rows_t, grad_scores, preferred_element_type=F32)
            grad_v = jnp.dot(grads_t, probs.astype(BF16), preferred_element_type=F32)
            if step > 0:
                grad_k = grad_k + grad_keys[:, part]
                grad_v = grad_v + grad_values[:, part]
            if step + 1 < steps:
                grad_keys[:, part] = grad_k
                grad_values[:, part] = grad_v
                continue
            grad_k = (grad_k * SCALE).astype(BF16)
            grad_v = grad_v.astype(BF16)
            for first in range(0, chunk, LANES):
                pair = (start + first) // LANES
                here_k = grad_k[:, first : first + LANES]
                here_v = grad_v[:, first : first + LANES]
                part_ref[2 * pair] = jnp.where(lane_part < HALF, here_k, roll_lanes(here_v, HALF))
                part_ref[2 * pair + 1] = jnp.where(
                    lane_part < HALF, roll_lanes(here_k, HALF), here_v
                )
        finish(step, sources, at, result * SCALE)


def backward_first_kernel(
    block,
    chunk,
    swapped_ref,
    got_ref,
    grads_ref,
    out_ref,
    part_ref,
    grad_q_ref,
    *scratch,
):
    def finish(step, sources, at, result):
        grad_q_ref[at, :] = result

    backward(
        swapped_ref, got_ref, grads_ref, out_ref, part_ref, finish, block, chunk, *scratch
    )


def backward_second_kernel(
    block,
    chunk,
    got_ref,
    grads_ref,
    out_ref,
    grad_q_ref,
    part_ref,
    piece_ref,
    *scratch,
):
    sums = jnp.zeros((SUB, LANES), F32)
    for source in range(grads_ref.shape[0]):
        sums = sums + grads_ref[source].astype(F32)

    def finish(step, sources, at, result):
        result = (result + grad_q_ref[at, :]).reshape(-1, SUB, LANES)
        lane = lax.broadcasted_iota(jnp.int32, result.shape, 2)
        piece_ref[sources] = jnp.where(lane < HEAD_DIM, result, sums[None]).astype(BF16)

    backward(
        got_ref, got_ref, grads_ref, out_ref, part_ref, finish, block, chunk, *scratch
    )


def join_kernel(part_ref, other_ref, piece_ref, send_ref):
    for device in range(part_ref.shape[0]):
        send_ref[device, KV_ROWS, :] = (
            part_ref[device].astype(F32) + other_ref[device].astype(F32)
        ).astype(BF16)
        send_ref[device, Q_ROWS, :] = piece_ref[device]


def unpack_kernel(
    groups, got_ref, arrived_ref, q_ref, k_ref, v_ref, gain_ref, taps_ref, next_ref, keys_t, values_t
):
    next_ref[...] = arrived_ref[...]
    count = got_ref.shape[0]
    lane = lanes_of(HEAD_DIM)
    for head in range(HEADS):
        at = slice(head * HEAD_DIM, (head + 1) * HEAD_DIM)
        low, high = (
            sum(
                got_ref[head * groups + group, KV_ROWS, :].astype(F32)
                for group in range(parity, groups, 2)
            ).astype(BF16)
            for parity in range(2)
        )
        keys_t[at, :] = jnp.where(lane < HALF, low, roll_lanes(high, HALF))
        values_t[at, :] = jnp.where(lane < HALF, roll_lanes(low, HALF), high)
    for target, turned in ((k_ref, keys_t), (v_ref, values_t)):
        for tile in range(CH // LANES):
            at = slice(tile * LANES, (tile + 1) * LANES)
            target[:, at] = turned[at, :].T
    for half in range(2):
        heads = [
            jnp.concatenate(
                [got_ref[(4 * half + i) * groups + group, Q_ROWS, :] for group in range(groups)],
                axis=0,
            )
            for i in range(4)
        ]
        for i, block in enumerate(heads_to_tiles(heads)):
            at = slice((3 * half + i) * LANES, (3 * half + i + 1) * LANES)
            q_ref[:, at] = block
    lane = lanes_of(8)
    for device in range(count):
        piece = got_ref[device, Q_ROWS, :].astype(F32)
        eight = roll_lanes(piece[0:8], 32)
        for a in range(1, 4):
            eight = jnp.where(
                lane >= 32 * a, roll_lanes(piece[8 * a : 8 * a + 8], 32 * a - 96), eight
            )
        for tile in range(CH // LANES):
            at = slice(tile * LANES, (tile + 1) * LANES)
            if device < TAPS:
                taps_ref[device, :, at] = eight[tile : tile + 1]
            else:
                gain_ref[:, at] = eight[tile : tile + 1]


def exchange(pieces):
    return lax.all_to_all(pieces, "tm", split_axis=0, concat_axis=0, tiled=True)


def local(resid, queries, keys, values, gain, taps, cotangent):
    count = lax.axis_size("tm")
    sections = lax.axis_size("section")
    groups = count // HEADS
    frames = resid.shape[1]
    total = frames * count
    own = total // groups
    half = total // 2
    place = lax.axis_index("tm").astype(jnp.int32).reshape(1)
    edge = 16
    matmul = 2 * own * half * LANES

    resid, queries, keys, values, cotangent = (
        array[0] for array in (resid, queries, keys, values, cotangent)
    )
    taps = taps.reshape(TAPS, 1, CH)
    up = [(i, i + 1) for i in range(count - 1)]
    down = [(i + 1, i) for i in range(count - 1)]
    partner = [(i, i ^ 1) for i in range(count)]
    before = lax.ppermute(
        jnp.concatenate([resid[frames - SUB :], cotangent[frames - edge :]], axis=0), "tm", up
    )
    after = lax.ppermute(jnp.concatenate([resid[:SUB], cotangent[:edge]], axis=0), "tm", down)

    shape = jax.ShapeDtypeStruct
    pieces = shape((count, PIECE_ROWS, LANES), BF16)
    rows_shape = shape((frames, CH), BF16)
    own_shape = shape((own, LANES), F32)
    sent = call(
        lambda *refs: pack_kernel(groups, *refs),
        pieces,
        [ANY] * 3,
        ANY,
        [pltpu.VMEM((frames, CH), BF16)] * 3
        + [pltpu.VMEM((count, PIECE_ROWS, LANES), BF16)]
        + [pltpu.VMEM((CH, LANES), BF16)] * 2
        + [pltpu.SemaphoreType.DMA((3,)), pltpu.SemaphoreType.DMA((HEADS,))],
        56,
        1000000,
        "pack_qkv",
    )(queries, keys, values)
    got = call(
        lambda *refs: None,
        pieces,
        [ANY] * 5,
        ANY,
        [],
        8,
        0,
        "received",
        aliases={0: 0},
    )(exchange(sent), before, after, gain, taps)
    swapped = lax.ppermute(got, "tm", partner)

    block, chunk = 256, 512
    attend_scratch = [
        pltpu.VMEM((LANES, half), BF16),
        pltpu.VMEM((half, LANES), BF16),
        pltpu.VMEM((2, block, half), F32),
    ]
    state = call(
        lambda *refs: forward_first_kernel(block, chunk, *refs),
        (own_shape,) * 3,
        [VMEM],
        (VMEM,) * 3,
        attend_scratch,
        24,
        2 * matmul,
        "attend_forward_own",
        own * half,
    )(got)
    results, head_out = call(
        lambda *refs: forward_second_kernel(block, chunk, groups, *refs),
        (shape((count, 48, LANES), BF16), shape((own, LANES), BF16)),
        [SMEM] + [VMEM] * 5,
        (VMEM,) * 2,
        attend_scratch,
        24,
        2 * matmul,
        "attend_forward_other",
        own * half,
    )(place, got, swapped, *state)
    returned = exchange(results)

    grads_sent, block_out, grad_resid = call(
        lambda *refs: conv_kernel(groups, count, *refs),
        (shape((count, SUB, LANES), BF16), rows_shape, rows_shape),
        [SMEM] + [VMEM] * 7,
        (VMEM,) * 3,
        [
            pltpu.VMEM((frames + 2 * SUB, CH), F32),
            pltpu.VMEM((frames + 2 * SUB, LANES), F32),
            pltpu.VMEM((frames + 2 * edge, LANES), F32),
            pltpu.VMEM((frames, CH), F32),
            pltpu.VMEM((TAPS + 1, CH), F32),
            pltpu.VMEM((frames + 2 * edge + 8, LANES), F32),
            pltpu.VMEM((frames + 16, LANES), F32),
        ],
        16,
        10000000,
        "conv_block",
    )(place, returned, resid, cotangent, before, after, gain, taps)
    grads_got = exchange(grads_sent)
    arrived = lax.ppermute(
        block_out, "section", [(i, (i + 1) % sections) for i in range(sections)]
    )

    block, chunk = 512, 512
    backward_scratch = [
        pltpu.VMEM((LANES, half), BF16),
        pltpu.VMEM((LANES, half), BF16),
        pltpu.VMEM((half, LANES), BF16),
        pltpu.VMEM((HEAD_DIM, half), F32),
        pltpu.VMEM((HEAD_DIM, half), F32),
    ]
    part_shape = shape((count, HEAD_DIM, LANES), BF16)
    other_part, grad_q = call(
        lambda *refs: backward_first_kernel(block, chunk, *refs),
        (part_shape, own_shape),
        [VMEM] * 4,
        (VMEM,) * 2,
        backward_scratch,
        24,
        5 * matmul,
        "attend_backward_other",
    )(swapped, got, grads_got, head_out)
    arrived_part = lax.ppermute(other_part, "tm", partner)
    own_part, grad_q_pieces = call(
        lambda *refs: backward_second_kernel(block, chunk, *refs),
        (part_shape, shape((count, SUB, LANES), BF16)),
        [VMEM] * 4,
        (VMEM,) * 2,
        backward_scratch,
        24,
        5 * matmul,
        "attend_backward_own",
        own * half,
    )(got, grads_got, head_out, grad_q)
    grads_out = call(
        join_kernel,
        pieces,
        [VMEM] * 3,
        VMEM,
        [],
        8,
        1000000,
        "join_grads",
    )(own_part, arrived_part, grad_q_pieces)
    back = exchange(grads_out)

    grad_q, grad_k, grad_v, grad_gain, grad_taps, next_input = call(
        lambda *refs: unpack_kernel(groups, *refs),
        (
            rows_shape,
            rows_shape,
            rows_shape,
            shape((1, CH), F32),
            shape((TAPS, 1, CH), F32),
            rows_shape,
        ),
        [VMEM] * 2,
        (VMEM,) * 6,
        [pltpu.VMEM((CH, LANES), BF16)] * 2,
        8,
        1000000,
        "unpack_grads",
    )(back, arrived)
    return (
        next_input[None],
        grad_resid[None],
        grad_q[None],
        grad_k[None],
        grad_v[None],
        grad_gain,
        grad_taps.reshape(1, TAPS, CH),
    )


def solution(mesh):
    rows = P("section", "tm", None)
    in_specs = (rows, rows, rows, rows, P("section", None), P("section", None, None), rows)
    out_specs = (rows, rows, rows, rows, rows, P("section", None), P("section", None, None))
    return jax.shard_map(local, mesh=mesh, in_specs=in_specs, out_specs=out_specs, check_vma=False)
```

```python
import math

import jax
import jax.numpy as jnp
from jax import lax
from jax.experimental import pallas as pl
from jax.experimental.pallas import tpu as pltpu
from jax.sharding import PartitionSpec as P

HEADS = 8
HEAD_DIM = 96
TAPS = 31
CH = 768
LANES = 128
EPS = 1e-06

SCALE = HEAD_DIM ** (-0.5)
SCALE2 = SCALE * math.log2(math.e)

F32 = jnp.float32
BF16 = jnp.bfloat16

KV_ROWS = slice(0, 96)
Q_ROWS = slice(96, 128)
PIECE_ROWS = 128
HALF = 64
OWN_FACTOR = range(96, 99)
OTHER_FACTOR = range(99, 102)
SUB = 32

VMEM = pl.BlockSpec(memory_space=pltpu.VMEM)
SMEM = pl.BlockSpec(memory_space=pltpu.SMEM)
ANY = pl.BlockSpec(memory_space=pl.ANY)
MIB = 1024 * 1024


def lanes_of(rows):
    return lax.broadcasted_iota(jnp.int32, (rows, LANES), 1)


def roll_lanes(block, by):
    by = by % LANES
    return block if by == 0 else pltpu.roll(block, by, 1)


def heads_to_tiles(heads):
    lane = lanes_of(heads[0].shape[0])
    second = roll_lanes(heads[1], 96)
    third = roll_lanes(heads[2], 64)
    fourth = roll_lanes(heads[3], 32)
    return (
        jnp.where(lane < 96, heads[0], second),
        jnp.where(lane < 64, second, third),
        jnp.where(lane < 32, third, fourth),
    )


def tiles_to_heads(tiles):
    lane = lanes_of(tiles[0].shape[0])
    return (
        tiles[0],
        roll_lanes(jnp.where(lane >= 96, tiles[0], tiles[1]), 32),
        roll_lanes(jnp.where(lane >= 64, tiles[1], tiles[2]), 64),
        roll_lanes(tiles[2], 96),
    )


def call(kernel, out_shape, in_specs, out_specs, scratch, limit, flops, name, transcendentals=0, aliases={}):
    return pl.pallas_call(
        kernel,
        out_shape=out_shape,
        in_specs=in_specs,
        out_specs=out_specs,
        scratch_shapes=scratch,
        input_output_aliases=aliases,
        compiler_params=pltpu.CompilerParams(vmem_limit_bytes=limit * MIB),
        cost_estimate=pl.CostEstimate(
            flops=flops, bytes_accessed=2 * MIB, transcendentals=transcendentals
        ),
        name=name,
    )


def pack_kernel(
    groups, q_hbm, k_hbm, v_hbm, send_hbm, q_ref, k_ref, v_ref, send_ref, keys_t, values_t, sems, sent
):
    copies = [
        pltpu.make_async_copy(source, target, sems.at[i])
        for i, (source, target) in enumerate(((q_hbm, q_ref), (k_hbm, k_ref), (v_hbm, v_ref)))
    ]
    for copy in copies:
        copy.start()
    copies[0].wait()
    frames = q_ref.shape[0]
    lane = lanes_of(frames)
    for half in range(2):
        tiles = [
            q_ref[:, (3 * half + i) * LANES : (3 * half + i + 1) * LANES] for i in range(3)
        ]
        for i, block in enumerate(tiles_to_heads(tiles)):
            block = jnp.where(lane < HEAD_DIM, block, jnp.zeros_like(block))
            for group in range(groups):
                send_ref[(4 * half + i) * groups + group, Q_ROWS, :] = block[
                    group * SUB : (group + 1) * SUB
                ]
    for copy, source, turned in ((copies[1], k_ref, keys_t), (copies[2], v_ref, values_t)):
        copy.wait()
        for tile in range(CH // LANES):
            at = slice(tile * LANES, (tile + 1) * LANES)
            turned[at, :] = source[:, at].T
    lane = lanes_of(HEAD_DIM)
    out = []
    for head in range(HEADS):
        at = slice(head * HEAD_DIM, (head + 1) * HEAD_DIM)
        keys_here, values_here = keys_t[at, :], values_t[at, :]
        halves = (
            jnp.where(lane < HALF, keys_here, roll_lanes(values_here, HALF)),
            jnp.where(lane < HALF, roll_lanes(keys_here, HALF), values_here),
        )
        for group in range(groups):
            send_ref[head * groups + group, KV_ROWS, :] = halves[group % 2]
        devices = pl.ds(head * groups, groups)
        out.append(
            pltpu.make_async_copy(send_ref.at[devices], send_hbm.at[devices], sent.at[head])
        )
        out[-1].start()
    for copy in out:
        copy.wait()


def fill_half(half_ref, start, stop, keys_t, values_t, keys, values):
    lane = lanes_of(HEAD_DIM)
    zeros = jnp.zeros((LANES - HEAD_DIM, LANES), BF16)
    for pair in range(start // LANES, stop // LANES):
        at = slice(pair * LANES, (pair + 1) * LANES)
        even = half_ref[2 * pair, KV_ROWS, :]
        odd = half_ref[2 * pair + 1, KV_ROWS, :]
        for turned, natural, block in (
            (keys_t, keys, jnp.where(lane < HALF, even, roll_lanes(odd, HALF))),
            (values_t, values, jnp.where(lane < HALF, roll_lanes(even, HALF), odd)),
        ):
            block = jnp.concatenate([block, zeros], axis=0)
            if turned is not None:
                turned[:, at] = block
            if natural is not None:
                natural[at, :] = block.T


def attend(got_ref, half_ref, state, finish, block, chunk, kept_ref, keys, values, scores):
    key_count = keys.shape[1]
    per = block // SUB
    blocks = got_ref.shape[0] // per

    def rows_of(step):
        return got_ref[step * per : (step + 1) * per, Q_ROWS, :].reshape(block, LANES)

    def score(step, rows, start, peak):
        part = jnp.dot(rows, keys[:, start : start + chunk], preferred_element_type=F32)
        scores[step % 2, :, start : start + chunk] = part
        for tile in range(0, chunk, LANES):
            peak = jnp.maximum(peak, part[:, tile : tile + LANES])
        return peak

    lowest = jnp.full((block, LANES), -jnp.inf, F32)
    peak = lowest
    rows = rows_of(0)
    for start in range(0, key_count, chunk):
        fill_half(half_ref, start, start + chunk, keys, None, None, values)
        peak = score(0, rows, start, peak)
    for step in range(blocks):
        at = slice(step * block, (step + 1) * block)
        top = jnp.broadcast_to(jnp.max(peak, axis=1, keepdims=True) * SCALE2, (block, LANES))
        if state is None:
            total = jnp.zeros((block, LANES), F32)
            result = jnp.zeros((block, LANES), F32)
        else:
            old = state[0][at, :]
            top = jnp.maximum(top, old)
            shrink = jnp.exp2(old - top)
            total = state[1][at, :] * shrink
            result = state[2][at, :] * shrink
        tops = jnp.concatenate([top] * (chunk // LANES), axis=1)
        peak = lowest
        if step + 1 < blocks:
            rows = rows_of(step + 1)
        for start in range(0, key_count, chunk):
            if step + 1 < blocks:
                peak = score(step + 1, rows, start, peak)
            weights = jnp.exp2(scores[step % 2, :, start : start + chunk] * SCALE2 - tops)
            for tile in range(0, chunk, LANES):
                total = total + weights[:, tile : tile + LANES]
            weights = weights.astype(BF16)
            kept_ref[at, start : start + chunk] = weights
            result = result + jnp.dot(
                weights, values[start : start + chunk, :], preferred_element_type=F32
            )
        finish(at, top, total, result)


def forward_first_kernel(
    block,
    chunk,
    got_ref,
    top_ref,
    total_ref,
    result_ref,
    kept_ref,
    keys,
    values,
    scores,
):
    def finish(at, top, total, result):
        top_ref[at, :] = top
        total_ref[at, :] = total
        result_ref[at, :] = result

    attend(got_ref, got_ref, None, finish, block, chunk, kept_ref, keys, values, scores)


def forward_second_kernel(
    block,
    chunk,
    groups,
    place_ref,
    got_ref,
    swapped_ref,
    top_ref,
    total_ref,
    result_ref,
    send_ref,
    out_ref,
    kept_ref,
    keys,
    values,
    scores,
):
    def finish(at, top, total, result):
        total = jnp.sum(total, axis=1, keepdims=True)
        merged = result / total
        lane = lanes_of(block)
        for spots, rest in (
            (OWN_FACTOR, jnp.exp2(top_ref[at, :] - top) / total),
            (OTHER_FACTOR, jnp.broadcast_to(1.0 / total, (block, LANES))),
        ):
            for spot in spots:
                part = rest.astype(BF16).astype(F32)
                merged = jnp.where(lane == spot, part, merged)
                rest = rest - part
        out_ref[at, :] = merged.astype(BF16)

    state = (top_ref, total_ref, result_ref)
    attend(got_ref, swapped_ref, state, finish, block, chunk, kept_ref, keys, values, scores)
    count = got_ref.shape[0]
    side = jnp.where(place_ref[0] % groups == groups - 1, -1, 1)
    lane = lanes_of(48)
    for device in range(count):
        near = jnp.clip(device + side, 0, count - 1)
        beside = out_ref[pl.ds(pl.multiple_of(near * SUB, SUB), SUB), :]
        own = out_ref[device * SUB : (device + 1) * SUB, :]
        tail = beside[16:32]
        spare = jnp.concatenate([roll_lanes(tail, by) for by in (96, 64, 32)], axis=0)
        piece = jnp.concatenate([own, beside[0:16]], axis=0)
        send_ref[device] = jnp.where(lane < HEAD_DIM, piece, spare)


def halo_of(piece):
    lane = lanes_of(16)
    tail = jnp.where(
        lane < 32,
        roll_lanes(piece[0:16], 32),
        jnp.where(lane < 64, roll_lanes(piece[16:32], 64), roll_lanes(piece[32:48], 96)),
    )
    return [piece[32:48], tail]


def conv_kernel(
    groups,
    count,
    place_ref,
    got_ref,
    resid_ref,
    cot_ref,
    before_ref,
    after_ref,
    gain_ref,
    taps_ref,
    send_ref,
    out_ref,
    grad_ref,
    mixed,
    normed,
    grad_conv,
    scaled,
    sums,
    shifted,
    grad_wide,
):
    frames = resid_ref.shape[0]
    sub = frames // groups
    wide = frames + 2 * sub
    edge = 16
    inner = frames + 2 * edge
    tiles = CH // LANES
    place = place_ref[0]

    square = jnp.zeros((wide, LANES), F32)
    for half in range(2):
        heads = []
        for i in range(4):
            first = (4 * half + i) * groups
            before_piece = got_ref[first + groups - 1].astype(F32)
            after_piece = got_ref[first].astype(F32)
            parts = halo_of(before_piece)
            parts += [got_ref[first + group, 0:sub, :].astype(F32) for group in range(groups)]
            parts += halo_of(after_piece)
            heads.append(jnp.concatenate(parts, axis=0))
        for i, attended in enumerate(heads_to_tiles(heads)):
            at = slice((3 * half + i) * LANES, (3 * half + i + 1) * LANES)
            block = jnp.concatenate(
                [before_ref[0:sub, at], resid_ref[:, at], after_ref[0:sub, at]], axis=0
            ).astype(F32)
            block = block + attended
            mixed[:, at] = block
            square = square + block * block
    inverse = lax.rsqrt(jnp.sum(square, axis=1, keepdims=True) * (1.0 / CH) + EPS)

    row = lax.broadcasted_iota(jnp.int32, (wide, LANES), 0)
    inside = ((row >= sub) | (place > 0)) & ((row < sub + frames) | (place < count - 1))
    lo, hi = sub - edge, sub - edge + inner
    row_inner = lax.broadcasted_iota(jnp.int32, (inner, LANES), 0) + lo
    inside_inner = ((row_inner >= sub) | (place > 0)) & (
        (row_inner < sub + frames) | (place < count - 1)
    )
    own = slice(sub, sub + frames)
    inverse_own = inverse[sub : sub + frames]

    grad_wide[0:8, :] = jnp.zeros((8, LANES), F32)
    grad_wide[8 + frames : 16 + frames, :] = jnp.zeros((8, LANES), F32)
    dots = jnp.zeros((frames, LANES), F32)
    for tile in range(tiles):
        at = slice(tile * LANES, (tile + 1) * LANES)
        gain_row = gain_ref[0:1, at]
        value = (mixed[:, at] * inverse * gain_row).astype(BF16).astype(F32)
        normed[...] = jnp.where(inside, value, 0.0)
        conv = jnp.zeros((inner, LANES), F32)
        for b in range(8):
            part = jnp.zeros((inner + 8, LANES), F32)
            for tap in range(b, TAPS, 8):
                part = part + taps_ref[tap, :, at] * normed[tap - b : tap - b + inner + 8, :]
            shifted[...] = part
            conv = conv + shifted[b + 1 : b + 1 + inner, :]
        sig = jax.nn.sigmoid(conv)
        out_ref[:, at] = (
            mixed[own, at] + (conv * sig)[edge : edge + frames]
        ).astype(BF16)
        cot = jnp.concatenate(
            [before_ref[sub : sub + edge, at], cot_ref[:, at], after_ref[sub : sub + edge, at]],
            axis=0,
        ).astype(F32)
        value = (cot * sig * (1.0 + conv * (1.0 - sig))).astype(BF16).astype(F32)
        grad_conv[...] = jnp.where(inside_inner, value, 0.0)
        grad_normed = jnp.zeros((frames, LANES), F32)
        grad_wide[8 : 8 + frames, :] = grad_conv[edge : edge + frames, :]
        for b in range(8):
            part = jnp.zeros((frames + 8, LANES), F32)
            grad_here = grad_wide[7 - b : 15 - b + frames, :]
            for tap in range(b, TAPS, 8):
                first = tap - b
                part = part + taps_ref[TAPS - 1 - tap, :, at] * grad_conv[first : first + frames + 8, :]
                first = first + edge
                sums[tap : tap + 1, at] = jnp.sum(
                    grad_here * normed[first : first + frames + 8, :], axis=0, keepdims=True
                )
            shifted[0 : frames + 8, :] = part
            grad_normed = grad_normed + shifted[b + 1 : b + 1 + frames, :]
        unit = mixed[own, at] * inverse_own
        sums[TAPS : TAPS + 1, at] = jnp.sum(grad_normed * unit, axis=0, keepdims=True)
        here = grad_normed * gain_row
        scaled[:, at] = here
        dots = dots + here * unit
    mean = jnp.sum(dots, axis=1, keepdims=True) * (1.0 / CH)

    lane = lanes_of(sub)
    sublane = lax.broadcasted_iota(jnp.int32, (8, LANES), 0)
    for half in range(2):
        grads = []
        for i in range(3):
            at = slice((3 * half + i) * LANES, (3 * half + i + 1) * LANES)
            unit = mixed[own, at] * inverse_own
            grad = cot_ref[:, at].astype(F32) + inverse_own * (scaled[:, at] - unit * mean)
            grad_ref[:, at] = grad.astype(BF16)
            grads.append(grad)
        for i, block in enumerate(tiles_to_heads(grads)):
            for group in range(groups):
                device = (4 * half + i) * groups + group
                eight = jnp.zeros((8, LANES), F32)
                for tile in range(tiles):
                    line = sums[device : device + 1, tile * LANES : (tile + 1) * LANES]
                    eight = jnp.where(sublane == tile, line, eight)
                spare = jnp.concatenate(
                    [roll_lanes(eight, 96 - 32 * a) for a in range(4)], axis=0
                )
                piece = jnp.where(lane < HEAD_DIM, block[group * sub : (group + 1) * sub], spare)
                send_ref[device] = piece.astype(BF16)


def backward(
    factor_lanes,
    kept_ref,
    half_ref,
    got_ref,
    grads_ref,
    out_ref,
    part_ref,
    finish,
    block,
    chunk,
    values_t,
    keys,
    grad_keys,
    grad_values,
):
    fill_half(half_ref, 0, chunk, None, values_t, keys, None)
    key_count = keys.shape[0]
    steps = got_ref.shape[0] * SUB // block
    lane_part = lanes_of(HEAD_DIM)
    per = block // SUB
    lane = lanes_of(block)
    for step in range(steps):
        sources = slice(step * per, (step + 1) * per)
        at = slice(step * block, (step + 1) * block)
        rows = got_ref[sources, Q_ROWS, :].reshape(block, LANES)
        grads = grads_ref[sources].reshape(block, LANES).astype(F32)
        out = out_ref[at, :].astype(F32)
        in_factor = (lane >= factor_lanes.start) & (lane < factor_lanes.stop)
        factor = jnp.sum(jnp.where(in_factor, out, 0.0), axis=1, keepdims=True)
        grads = jnp.where(lane < HEAD_DIM, grads * factor, 0.0).astype(BF16)
        delta = jnp.sum(grads.astype(F32) * out, axis=1, keepdims=True)
        rows_t = rows.T[0:HEAD_DIM]
        grads_t = grads.T[0:HEAD_DIM]
        result = jnp.zeros((block, LANES), F32)
        for start in range(0, key_count, chunk):
            part = slice(start, start + chunk)
            if step == 0 and start + chunk < key_count:
                fill_half(half_ref, start + chunk, start + 2 * chunk, None, values_t, keys, None)
            weights = kept_ref[at, part]
            grad_probs = jnp.dot(grads, values_t[:, part], preferred_element_type=F32)
            grad_scores = (weights.astype(F32) * (grad_probs - delta)).astype(BF16)
            result = result + jnp.dot(grad_scores, keys[part, :], preferred_element_type=F32)
            grad_k = jnp.dot(rows_t, grad_scores, preferred_element_type=F32)
            grad_v = jnp.dot(grads_t, weights, preferred_element_type=F32)
            if step > 0:
                grad_k = grad_k + grad_keys[:, part]
                grad_v = grad_v + grad_values[:, part]
            if step + 1 < steps:
                grad_keys[:, part] = grad_k
                grad_values[:, part] = grad_v
                continue
            grad_k = (grad_k * SCALE).astype(BF16)
            grad_v = grad_v.astype(BF16)
            for first in range(0, chunk, LANES):
                pair = (start + first) // LANES
                here_k = grad_k[:, first : first + LANES]
                here_v = grad_v[:, first : first + LANES]
                part_ref[2 * pair] = jnp.where(lane_part < HALF, here_k, roll_lanes(here_v, HALF))
                part_ref[2 * pair + 1] = jnp.where(
                    lane_part < HALF, roll_lanes(here_k, HALF), here_v
                )
        finish(step, sources, at, result * SCALE)


def backward_first_kernel(
    block,
    chunk,
    kept_ref,
    swapped_ref,
    got_ref,
    grads_ref,
    out_ref,
    part_ref,
    grad_q_ref,
    *scratch,
):
    def finish(step, sources, at, result):
        grad_q_ref[at, :] = result

    given = (kept_ref, swapped_ref, got_ref, grads_ref, out_ref)
    backward(OTHER_FACTOR, *given, part_ref, finish, block, chunk, *scratch)


def backward_second_kernel(
    block,
    chunk,
    kept_ref,
    got_ref,
    grads_ref,
    out_ref,
    grad_q_ref,
    part_ref,
    piece_ref,
    *scratch,
):
    sums = jnp.zeros((SUB, LANES), F32)
    for source in range(grads_ref.shape[0]):
        sums = sums + grads_ref[source].astype(F32)

    def finish(step, sources, at, result):
        result = (result + grad_q_ref[at, :]).reshape(-1, SUB, LANES)
        lane = lax.broadcasted_iota(jnp.int32, result.shape, 2)
        piece_ref[sources] = jnp.where(lane < HEAD_DIM, result, sums[None]).astype(BF16)

    given = (kept_ref, got_ref, got_ref, grads_ref, out_ref)
    backward(OWN_FACTOR, *given, part_ref, finish, block, chunk, *scratch)


def join_kernel(part_ref, other_ref, piece_ref, send_ref):
    for device in range(part_ref.shape[0]):
        send_ref[device, KV_ROWS, :] = (
            part_ref[device].astype(F32) + other_ref[device].astype(F32)
        ).astype(BF16)
        send_ref[device, Q_ROWS, :] = piece_ref[device]


def unpack_kernel(
    groups, got_ref, arrived_ref, q_ref, k_ref, v_ref, gain_ref, taps_ref, next_ref, keys_t, values_t
):
    next_ref[...] = arrived_ref[...]
    count = got_ref.shape[0]
    lane = lanes_of(HEAD_DIM)
    for head in range(HEADS):
        at = slice(head * HEAD_DIM, (head + 1) * HEAD_DIM)
        low, high = (
            sum(
                got_ref[head * groups + group, KV_ROWS, :].astype(F32)
                for group in range(parity, groups, 2)
            ).astype(BF16)
            for parity in range(2)
        )
        keys_t[at, :] = jnp.where(lane < HALF, low, roll_lanes(high, HALF))
        values_t[at, :] = jnp.where(lane < HALF, roll_lanes(low, HALF), high)
    for target, turned in ((k_ref, keys_t), (v_ref, values_t)):
        for tile in range(CH // LANES):
            at = slice(tile * LANES, (tile + 1) * LANES)
            target[:, at] = turned[at, :].T
    for half in range(2):
        heads = [
            jnp.concatenate(
                [got_ref[(4 * half + i) * groups + group, Q_ROWS, :] for group in range(groups)],
                axis=0,
            )
            for i in range(4)
        ]
        for i, block in enumerate(heads_to_tiles(heads)):
            at = slice((3 * half + i) * LANES, (3 * half + i + 1) * LANES)
            q_ref[:, at] = block
    lane = lanes_of(8)
    for device in range(count):
        piece = got_ref[device, Q_ROWS, :].astype(F32)
        eight = roll_lanes(piece[0:8], 32)
        for a in range(1, 4):
            eight = jnp.where(
                lane >= 32 * a, roll_lanes(piece[8 * a : 8 * a + 8], 32 * a - 96), eight
            )
        for tile in range(CH // LANES):
            at = slice(tile * LANES, (tile + 1) * LANES)
            if device < TAPS:
                taps_ref[device, :, at] = eight[tile : tile + 1]
            else:
                gain_ref[:, at] = eight[tile : tile + 1]


def exchange(pieces):
    return lax.all_to_all(pieces, "tm", split_axis=0, concat_axis=0, tiled=True)


def local(resid, queries, keys, values, gain, taps, cotangent):
    count = lax.axis_size("tm")
    sections = lax.axis_size("section")
    groups = count // HEADS
    frames = resid.shape[1]
    total = frames * count
    own = total // groups
    half = total // 2
    place = lax.axis_index("tm").astype(jnp.int32).reshape(1)
    edge = 16
    matmul = 2 * own * half * LANES

    resid, queries, keys, values, cotangent = (
        array[0] for array in (resid, queries, keys, values, cotangent)
    )
    taps = taps.reshape(TAPS, 1, CH)
    up = [(i, i + 1) for i in range(count - 1)]
    down = [(i + 1, i) for i in range(count - 1)]
    partner = [(i, i ^ 1) for i in range(count)]
    before = lax.ppermute(
        jnp.concatenate([resid[frames - SUB :], cotangent[frames - edge :]], axis=0), "tm", up
    )
    after = lax.ppermute(jnp.concatenate([resid[:SUB], cotangent[:edge]], axis=0), "tm", down)

    shape = jax.ShapeDtypeStruct
    pieces = shape((count, PIECE_ROWS, LANES), BF16)
    rows_shape = shape((frames, CH), BF16)
    own_shape = shape((own, LANES), F32)
    kept_shape = shape((own, half), BF16)
    sent = call(
        lambda *refs: pack_kernel(groups, *refs),
        pieces,
        [ANY] * 3,
        ANY,
        [pltpu.VMEM((frames, CH), BF16)] * 3
        + [pltpu.VMEM((count, PIECE_ROWS, LANES), BF16)]
        + [pltpu.VMEM((CH, LANES), BF16)] * 2
        + [pltpu.SemaphoreType.DMA((3,)), pltpu.SemaphoreType.DMA((HEADS,))],
        56,
        1000000,
        "pack_qkv",
    )(queries, keys, values)
    got = call(
        lambda *refs: None,
        pieces,
        [ANY] * 5,
        ANY,
        [],
        8,
        0,
        "received",
        aliases={0: 0},
    )(exchange(sent), before, after, gain, taps)
    swapped = lax.ppermute(got, "tm", partner)

    block, chunk = 256, 512
    attend_scratch = [
        pltpu.VMEM((LANES, half), BF16),
        pltpu.VMEM((half, LANES), BF16),
        pltpu.VMEM((2, block, half), F32),
    ]
    *state, own_kept = call(
        lambda *refs: forward_first_kernel(block, chunk, *refs),
        (own_shape,) * 3 + (kept_shape,),
        [VMEM],
        (VMEM,) * 4,
        attend_scratch,
        24,
        2 * matmul,
        "attend_forward_own",
        own * half,
    )(got)
    results, head_out, other_kept = call(
        lambda *refs: forward_second_kernel(block, chunk, groups, *refs),
        (shape((count, 48, LANES), BF16), shape((own, LANES), BF16), kept_shape),
        [SMEM] + [VMEM] * 5,
        (VMEM,) * 3,
        attend_scratch,
        24,
        2 * matmul,
        "attend_forward_other",
        own * half,
    )(place, got, swapped, *state)
    returned = exchange(results)

    grads_sent, block_out, grad_resid = call(
        lambda *refs: conv_kernel(groups, count, *refs),
        (shape((count, SUB, LANES), BF16), rows_shape, rows_shape),
        [SMEM] + [VMEM] * 7,
        (VMEM,) * 3,
        [
            pltpu.VMEM((frames + 2 * SUB, CH), F32),
            pltpu.VMEM((frames + 2 * SUB, LANES), F32),
            pltpu.VMEM((frames + 2 * edge, LANES), F32),
            pltpu.VMEM((frames, CH), F32),
            pltpu.VMEM((TAPS + 1, CH), F32),
            pltpu.VMEM((frames + 2 * edge + 8, LANES), F32),
            pltpu.VMEM((frames + 16, LANES), F32),
        ],
        16,
        10000000,
        "conv_block",
    )(place, returned, resid, cotangent, before, after, gain, taps)
    grads_got = exchange(grads_sent)
    arrived = lax.ppermute(
        block_out, "section", [(i, (i + 1) % sections) for i in range(sections)]
    )

    block, chunk = 512, 512
    backward_scratch = [
        pltpu.VMEM((LANES, half), BF16),
        pltpu.VMEM((half, LANES), BF16),
        pltpu.VMEM((HEAD_DIM, half), F32),
        pltpu.VMEM((HEAD_DIM, half), F32),
    ]
    part_shape = shape((count, HEAD_DIM, LANES), BF16)
    other_part, grad_q = call(
        lambda *refs: backward_first_kernel(block, chunk, *refs),
        (part_shape, own_shape),
        [VMEM] * 5,
        (VMEM,) * 2,
        backward_scratch,
        24,
        4 * matmul,
        "attend_backward_other",
    )(other_kept, swapped, got, grads_got, head_out)
    arrived_part = lax.ppermute(other_part, "tm", partner)
    own_part, grad_q_pieces = call(
        lambda *refs: backward_second_kernel(block, chunk, *refs),
        (part_shape, shape((count, SUB, LANES), BF16)),
        [VMEM] * 5,
        (VMEM,) * 2,
        backward_scratch,
        24,
        4 * matmul,
        "attend_backward_own",
    )(own_kept, got, grads_got, head_out, grad_q)
    grads_out = call(
        join_kernel,
        pieces,
        [VMEM] * 3,
        VMEM,
        [],
        8,
        1000000,
        "join_grads",
    )(own_part, arrived_part, grad_q_pieces)
    back = exchange(grads_out)

    grad_q, grad_k, grad_v, grad_gain, grad_taps, next_input = call(
        lambda *refs: unpack_kernel(groups, *refs),
        (
            rows_shape,
            rows_shape,
            rows_shape,
            shape((1, CH), F32),
            shape((TAPS, 1, CH), F32),
            rows_shape,
        ),
        [VMEM] * 2,
        (VMEM,) * 6,
        [pltpu.VMEM((CH, LANES), BF16)] * 2,
        8,
        1000000,
        "unpack_grads",
    )(back, arrived)
    return (
        next_input[None],
        grad_resid[None],
        grad_q[None],
        grad_k[None],
        grad_v[None],
        grad_gain,
        grad_taps.reshape(1, TAPS, CH),
    )


def solution(mesh):
    rows = P("section", "tm", None)
    in_specs = (rows, rows, rows, rows, P("section", None), P("section", None, None), rows)
    out_specs = (rows, rows, rows, rows, rows, P("section", None), P("section", None, None))
    return jax.shard_map(local, mesh=mesh, in_specs=in_specs, out_specs=out_specs, check_vma=False)
```

```python
import math

import jax
import jax.numpy as jnp
from jax import lax
from jax.experimental import pallas as pl
from jax.experimental.pallas import tpu as pltpu
from jax.sharding import PartitionSpec as P

HEADS = 8
HEAD_DIM = 96
TAPS = 31
CH = 768
LANES = 128
EPS = 1e-06

SCALE = HEAD_DIM ** (-0.5)
SCALE2 = SCALE * math.log2(math.e)

F32 = jnp.float32
BF16 = jnp.bfloat16

KV_ROWS = slice(0, 96)
Q_ROWS = slice(96, 128)
PIECE_ROWS = 128
HALF = 64
OWN_FACTOR = range(96, 99)
OTHER_FACTOR = range(99, 102)
SUB = 32

VMEM = pl.BlockSpec(memory_space=pltpu.VMEM)
SMEM = pl.BlockSpec(memory_space=pltpu.SMEM)
ANY = pl.BlockSpec(memory_space=pl.ANY)
MIB = 1024 * 1024


def lanes_of(rows):
    return lax.broadcasted_iota(jnp.int32, (rows, LANES), 1)


def roll_lanes(block, by):
    by = by % LANES
    return block if by == 0 else pltpu.roll(block, by, 1)


def heads_to_tiles(heads):
    lane = lanes_of(heads[0].shape[0])
    second = roll_lanes(heads[1], 96)
    third = roll_lanes(heads[2], 64)
    fourth = roll_lanes(heads[3], 32)
    return (
        jnp.where(lane < 96, heads[0], second),
        jnp.where(lane < 64, second, third),
        jnp.where(lane < 32, third, fourth),
    )


def tiles_to_heads(tiles):
    lane = lanes_of(tiles[0].shape[0])
    return (
        tiles[0],
        roll_lanes(jnp.where(lane >= 96, tiles[0], tiles[1]), 32),
        roll_lanes(jnp.where(lane >= 64, tiles[1], tiles[2]), 64),
        roll_lanes(tiles[2], 96),
    )


def call(kernel, out_shape, in_specs, out_specs, scratch, limit, flops, name, transcendentals=0, aliases={}):
    return pl.pallas_call(
        kernel,
        out_shape=out_shape,
        in_specs=in_specs,
        out_specs=out_specs,
        scratch_shapes=scratch,
        input_output_aliases=aliases,
        compiler_params=pltpu.CompilerParams(vmem_limit_bytes=limit * MIB),
        cost_estimate=pl.CostEstimate(
            flops=flops, bytes_accessed=2 * MIB, transcendentals=transcendentals
        ),
        name=name,
    )


def pack_kernel(
    groups, q_hbm, k_hbm, v_hbm, send_hbm, q_ref, k_ref, v_ref, send_ref, keys_t, values_t, sems, sent
):
    copies = [
        pltpu.make_async_copy(source, target, sems.at[i])
        for i, (source, target) in enumerate(((q_hbm, q_ref), (k_hbm, k_ref), (v_hbm, v_ref)))
    ]
    for copy in copies:
        copy.start()
    copies[0].wait()
    frames = q_ref.shape[0]
    lane = lanes_of(frames)
    for half in range(2):
        tiles = [
            q_ref[:, (3 * half + i) * LANES : (3 * half + i + 1) * LANES] for i in range(3)
        ]
        for i, block in enumerate(tiles_to_heads(tiles)):
            block = jnp.where(lane < HEAD_DIM, block, jnp.zeros_like(block))
            for group in range(groups):
                send_ref[(4 * half + i) * groups + group, Q_ROWS, :] = block[
                    group * SUB : (group + 1) * SUB
                ]
    for copy, source, turned in ((copies[1], k_ref, keys_t), (copies[2], v_ref, values_t)):
        copy.wait()
        for tile in range(CH // LANES):
            at = slice(tile * LANES, (tile + 1) * LANES)
            turned[at, :] = source[:, at].T
    lane = lanes_of(HEAD_DIM)
    out = []
    for head in range(HEADS):
        at = slice(head * HEAD_DIM, (head + 1) * HEAD_DIM)
        keys_here, values_here = keys_t[at, :], values_t[at, :]
        halves = (
            jnp.where(lane < HALF, keys_here, roll_lanes(values_here, HALF)),
            jnp.where(lane < HALF, roll_lanes(keys_here, HALF), values_here),
        )
        for group in range(groups):
            send_ref[head * groups + group, KV_ROWS, :] = halves[group % 2]
        devices = pl.ds(head * groups, groups)
        out.append(
            pltpu.make_async_copy(send_ref.at[devices], send_hbm.at[devices], sent.at[head])
        )
        out[-1].start()
    for copy in out:
        copy.wait()


def fill_half(half_ref, start, stop, keys_t, values_t, keys, values):
    lane = lanes_of(HEAD_DIM)
    zeros = jnp.zeros((LANES - HEAD_DIM, LANES), BF16)
    for pair in range(start // LANES, stop // LANES):
        at = slice(pair * LANES, (pair + 1) * LANES)
        even = half_ref[2 * pair, KV_ROWS, :]
        odd = half_ref[2 * pair + 1, KV_ROWS, :]
        for turned, natural, block in (
            (keys_t, keys, jnp.where(lane < HALF, even, roll_lanes(odd, HALF))),
            (values_t, values, jnp.where(lane < HALF, roll_lanes(even, HALF), odd)),
        ):
            block = jnp.concatenate([block, zeros], axis=0)
            if turned is not None:
                turned[:, at] = block
            if natural is not None:
                natural[at, :] = block.T


def attend(got_ref, half_ref, state, finish, block, chunk, kept_ref, keys, values, scores):
    key_count = keys.shape[1]
    per = block // SUB
    blocks = got_ref.shape[0] // per

    def rows_of(step):
        return got_ref[step * per : (step + 1) * per, Q_ROWS, :].reshape(block, LANES)

    def score(step, rows, start, peak):
        part = jnp.dot(rows, keys[:, start : start + chunk], preferred_element_type=F32)
        scores[step % 2, :, start : start + chunk] = part
        for tile in range(0, chunk, LANES):
            peak = jnp.maximum(peak, part[:, tile : tile + LANES])
        return peak

    lowest = jnp.full((block, LANES), -jnp.inf, F32)
    peak = lowest
    rows = rows_of(0)
    for start in range(0, key_count, chunk):
        fill_half(half_ref, start, start + chunk, keys, None, None, values)
        peak = score(0, rows, start, peak)
    for step in range(blocks):
        at = slice(step * block, (step + 1) * block)
        top = jnp.broadcast_to(jnp.max(peak, axis=1, keepdims=True) * SCALE2, (block, LANES))
        if state is None:
            total = jnp.zeros((block, LANES), F32)
            result = jnp.zeros((block, LANES), F32)
        else:
            old = state[0][at, :]
            top = jnp.maximum(top, old)
            shrink = jnp.exp2(old - top)
            total = state[1][at, :] * shrink
            result = state[2][at, :] * shrink
        tops = jnp.concatenate([top] * (chunk // LANES), axis=1)
        peak = lowest
        if step + 1 < blocks:
            rows = rows_of(step + 1)
        for start in range(0, key_count, chunk):
            if step + 1 < blocks:
                peak = score(step + 1, rows, start, peak)
            weights = jnp.exp2(scores[step % 2, :, start : start + chunk] * SCALE2 - tops)
            for tile in range(0, chunk, LANES):
                total = total + weights[:, tile : tile + LANES]
            weights = weights.astype(BF16)
            kept_ref[at, start : start + chunk] = weights
            result = result + jnp.dot(
                weights, values[start : start + chunk, :], preferred_element_type=F32
            )
        finish(at, top, total, result)


def forward_first_kernel(
    block,
    chunk,
    got_ref,
    top_ref,
    total_ref,
    result_ref,
    kept_ref,
    keys,
    values,
    scores,
):
    def finish(at, top, total, result):
        top_ref[at, :] = top
        total_ref[at, :] = total
        result_ref[at, :] = result

    attend(got_ref, got_ref, None, finish, block, chunk, kept_ref, keys, values, scores)


def forward_second_kernel(
    block,
    chunk,
    groups,
    place_ref,
    got_ref,
    swapped_ref,
    top_ref,
    total_ref,
    result_ref,
    send_ref,
    out_ref,
    kept_ref,
    keys,
    values,
    scores,
):
    def finish(at, top, total, result):
        total = jnp.sum(total, axis=1, keepdims=True)
        merged = result / total
        lane = lanes_of(block)
        for spots, rest in (
            (OWN_FACTOR, jnp.exp2(top_ref[at, :] - top) / total),
            (OTHER_FACTOR, jnp.broadcast_to(1.0 / total, (block, LANES))),
        ):
            for spot in spots:
                part = rest.astype(BF16).astype(F32)
                merged = jnp.where(lane == spot, part, merged)
                rest = rest - part
        out_ref[at, :] = merged.astype(BF16)

    state = (top_ref, total_ref, result_ref)
    attend(got_ref, swapped_ref, state, finish, block, chunk, kept_ref, keys, values, scores)
    count = got_ref.shape[0]
    side = jnp.where(place_ref[0] % groups == groups - 1, -1, 1)
    lane = lanes_of(48)
    for device in range(count):
        near = jnp.clip(device + side, 0, count - 1)
        beside = out_ref[pl.ds(pl.multiple_of(near * SUB, SUB), SUB), :]
        own = out_ref[device * SUB : (device + 1) * SUB, :]
        tail = beside[16:32]
        spare = jnp.concatenate([roll_lanes(tail, by) for by in (96, 64, 32)], axis=0)
        piece = jnp.concatenate([own, beside[0:16]], axis=0)
        send_ref[device] = jnp.where(lane < HEAD_DIM, piece, spare)


def halo_of(piece):
    lane = lanes_of(16)
    tail = jnp.where(
        lane < 32,
        roll_lanes(piece[0:16], 32),
        jnp.where(lane < 64, roll_lanes(piece[16:32], 64), roll_lanes(piece[32:48], 96)),
    )
    return [piece[32:48], tail]


def conv_kernel(
    groups,
    count,
    place_ref,
    got_ref,
    resid_ref,
    cot_ref,
    before_ref,
    after_ref,
    gain_ref,
    taps_ref,
    send_ref,
    out_ref,
    grad_ref,
    mixed,
    normed,
    grad_conv,
    scaled,
    sums,
    shifted,
    grad_wide,
):
    frames = resid_ref.shape[0]
    sub = frames // groups
    wide = frames + 2 * sub
    edge = 16
    inner = frames + 2 * edge
    tiles = CH // LANES
    place = place_ref[0]

    square = jnp.zeros((wide, LANES), F32)
    for half in range(2):
        heads = []
        for i in range(4):
            first = (4 * half + i) * groups
            before_piece = got_ref[first + groups - 1].astype(F32)
            after_piece = got_ref[first].astype(F32)
            parts = halo_of(before_piece)
            parts += [got_ref[first + group, 0:sub, :].astype(F32) for group in range(groups)]
            parts += halo_of(after_piece)
            heads.append(jnp.concatenate(parts, axis=0))
        for i, attended in enumerate(heads_to_tiles(heads)):
            at = slice((3 * half + i) * LANES, (3 * half + i + 1) * LANES)
            block = jnp.concatenate(
                [before_ref[0:sub, at], resid_ref[:, at], after_ref[0:sub, at]], axis=0
            ).astype(F32)
            block = block + attended
            mixed[:, at] = block
            square = square + block * block
    inverse = lax.rsqrt(jnp.sum(square, axis=1, keepdims=True) * (1.0 / CH) + EPS)

    row = lax.broadcasted_iota(jnp.int32, (wide, LANES), 0)
    inside = ((row >= sub) | (place > 0)) & ((row < sub + frames) | (place < count - 1))
    lo, hi = sub - edge, sub - edge + inner
    row_inner = lax.broadcasted_iota(jnp.int32, (inner, LANES), 0) + lo
    inside_inner = ((row_inner >= sub) | (place > 0)) & (
        (row_inner < sub + frames) | (place < count - 1)
    )
    own = slice(sub, sub + frames)
    inverse_own = inverse[sub : sub + frames]

    grad_wide[0:8, :] = jnp.zeros((8, LANES), F32)
    grad_wide[8 + frames : 16 + frames, :] = jnp.zeros((8, LANES), F32)
    dots = jnp.zeros((frames, LANES), F32)
    for tile in range(tiles):
        at = slice(tile * LANES, (tile + 1) * LANES)
        gain_row = gain_ref[0:1, at]
        value = (mixed[:, at] * inverse * gain_row).astype(BF16).astype(F32)
        normed[...] = jnp.where(inside, value, 0.0)
        conv = jnp.zeros((inner, LANES), F32)
        for b in range(8):
            part = jnp.zeros((inner + 8, LANES), F32)
            for tap in range(b, TAPS, 8):
                part = part + taps_ref[tap, :, at] * normed[tap - b : tap - b + inner + 8, :]
            shifted[...] = part
            conv = conv + shifted[b + 1 : b + 1 + inner, :]
        sig = jax.nn.sigmoid(conv)
        out_ref[:, at] = (
            mixed[own, at] + (conv * sig)[edge : edge + frames]
        ).astype(BF16)
        cot = jnp.concatenate(
            [before_ref[sub : sub + edge, at], cot_ref[:, at], after_ref[sub : sub + edge, at]],
            axis=0,
        ).astype(F32)
        value = (cot * sig * (1.0 + conv * (1.0 - sig))).astype(BF16).astype(F32)
        grad_conv[...] = jnp.where(inside_inner, value, 0.0)
        grad_normed = jnp.zeros((frames, LANES), F32)
        grad_wide[8 : 8 + frames, :] = grad_conv[edge : edge + frames, :]
        for b in range(8):
            part = jnp.zeros((frames + 8, LANES), F32)
            grad_here = grad_wide[7 - b : 15 - b + frames, :]
            for tap in range(b, TAPS, 8):
                first = tap - b
                part = part + taps_ref[TAPS - 1 - tap, :, at] * grad_conv[first : first + frames + 8, :]
                first = first + edge
                sums[tap : tap + 1, at] = jnp.sum(
                    grad_here * normed[first : first + frames + 8, :], axis=0, keepdims=True
                )
            shifted[0 : frames + 8, :] = part
            grad_normed = grad_normed + shifted[b + 1 : b + 1 + frames, :]
        unit = mixed[own, at] * inverse_own
        sums[TAPS : TAPS + 1, at] = jnp.sum(grad_normed * unit, axis=0, keepdims=True)
        here = grad_normed * gain_row
        scaled[:, at] = here
        dots = dots + here * unit
    mean = jnp.sum(dots, axis=1, keepdims=True) * (1.0 / CH)

    lane = lanes_of(sub)
    sublane = lax.broadcasted_iota(jnp.int32, (8, LANES), 0)
    for half in range(2):
        grads = []
        for i in range(3):
            at = slice((3 * half + i) * LANES, (3 * half + i + 1) * LANES)
            unit = mixed[own, at] * inverse_own
            grad = cot_ref[:, at].astype(F32) + inverse_own * (scaled[:, at] - unit * mean)
            grad_ref[:, at] = grad.astype(BF16)
            grads.append(grad)
        for i, block in enumerate(tiles_to_heads(grads)):
            for group in range(groups):
                device = (4 * half + i) * groups + group
                eight = jnp.zeros((8, LANES), F32)
                for tile in range(tiles):
                    line = sums[device : device + 1, tile * LANES : (tile + 1) * LANES]
                    eight = jnp.where(sublane == tile, line, eight)
                spare = jnp.concatenate(
                    [roll_lanes(eight, 96 - 32 * a) for a in range(4)], axis=0
                )
                piece = jnp.where(lane < HEAD_DIM, block[group * sub : (group + 1) * sub], spare)
                send_ref[device] = piece.astype(BF16)


def backward(
    factor_lanes,
    kept_ref,
    half_ref,
    got_ref,
    grads_ref,
    out_ref,
    part_ref,
    finish,
    block,
    chunk,
    values_t,
    keys,
    grad_keys,
    grad_values,
):
    fill_half(half_ref, 0, chunk, None, values_t, keys, None)
    key_count = keys.shape[0]
    steps = got_ref.shape[0] * SUB // block
    lane_part = lanes_of(HEAD_DIM)
    per = block // SUB
    lane = lanes_of(block)
    for step in range(steps):
        sources = slice(step * per, (step + 1) * per)
        at = slice(step * block, (step + 1) * block)
        rows = got_ref[sources, Q_ROWS, :].reshape(block, LANES)
        grads = grads_ref[sources].reshape(block, LANES).astype(F32)
        out = out_ref[at, :].astype(F32)
        in_factor = (lane >= factor_lanes.start) & (lane < factor_lanes.stop)
        factor = jnp.sum(jnp.where(in_factor, out, 0.0), axis=1, keepdims=True)
        grads = jnp.where(lane < HEAD_DIM, grads * factor, 0.0).astype(BF16)
        delta = jnp.sum(grads.astype(F32) * out, axis=1, keepdims=True)
        rows_t = rows.T[0:HEAD_DIM]
        grads_t = grads.T[0:HEAD_DIM]
        result = jnp.zeros((block, LANES), F32)
        for start in range(0, key_count, chunk):
            part = slice(start, start + chunk)
            if step == 0 and start + chunk < key_count:
                fill_half(half_ref, start + chunk, start + 2 * chunk, None, values_t, keys, None)
            weights = kept_ref[at, part]
            grad_probs = jnp.dot(grads, values_t[:, part], preferred_element_type=F32)
            grad_scores = (weights.astype(F32) * (grad_probs - delta)).astype(BF16)
            result = result + jnp.dot(grad_scores, keys[part, :], preferred_element_type=F32)
            grad_k = jnp.dot(rows_t, grad_scores, preferred_element_type=F32)
            grad_v = jnp.dot(grads_t, weights, preferred_element_type=F32)
            if step > 0:
                grad_k = grad_k + grad_keys[:, part]
                grad_v = grad_v + grad_values[:, part]
            if step + 1 < steps:
                grad_keys[:, part] = grad_k
                grad_values[:, part] = grad_v
                continue
            grad_k = (grad_k * SCALE).astype(BF16)
            grad_v = grad_v.astype(BF16)
            for first in range(0, chunk, LANES):
                pair = (start + first) // LANES
                here_k = grad_k[:, first : first + LANES]
                here_v = grad_v[:, first : first + LANES]
                part_ref[2 * pair] = jnp.where(lane_part < HALF, here_k, roll_lanes(here_v, HALF))
                part_ref[2 * pair + 1] = jnp.where(
                    lane_part < HALF, roll_lanes(here_k, HALF), here_v
                )
        finish(step, sources, at, result * SCALE)


def backward_first_kernel(
    block,
    chunk,
    kept_ref,
    swapped_ref,
    got_ref,
    grads_ref,
    out_ref,
    part_ref,
    grad_q_ref,
    *scratch,
):
    def finish(step, sources, at, result):
        grad_q_ref[at, :] = result

    given = (kept_ref, swapped_ref, got_ref, grads_ref, out_ref)
    backward(OTHER_FACTOR, *given, part_ref, finish, block, chunk, *scratch)


def backward_second_kernel(
    block,
    chunk,
    kept_ref,
    got_ref,
    grads_ref,
    out_ref,
    grad_q_ref,
    part_ref,
    piece_ref,
    *scratch,
):
    sums = jnp.zeros((SUB, LANES), F32)
    for source in range(grads_ref.shape[0]):
        sums = sums + grads_ref[source].astype(F32)

    def finish(step, sources, at, result):
        result = (result + grad_q_ref[at, :]).reshape(-1, SUB, LANES)
        lane = lax.broadcasted_iota(jnp.int32, result.shape, 2)
        piece_ref[sources] = jnp.where(lane < HEAD_DIM, result, sums[None]).astype(BF16)

    given = (kept_ref, got_ref, got_ref, grads_ref, out_ref)
    backward(OWN_FACTOR, *given, part_ref, finish, block, chunk, *scratch)


def join_kernel(part_ref, other_ref, piece_ref, send_ref):
    for device in range(part_ref.shape[0]):
        send_ref[device, KV_ROWS, :] = (
            part_ref[device].astype(F32) + other_ref[device].astype(F32)
        ).astype(BF16)
        send_ref[device, Q_ROWS, :] = piece_ref[device]


def unpack_kernel(
    groups, got_ref, arrived_ref, q_ref, k_ref, v_ref, gain_ref, taps_ref, next_ref, keys_t, values_t
):
    next_ref[...] = arrived_ref[...]
    count = got_ref.shape[0]
    lane = lanes_of(HEAD_DIM)
    for head in range(HEADS):
        at = slice(head * HEAD_DIM, (head + 1) * HEAD_DIM)
        low, high = (
            sum(
                got_ref[head * groups + group, KV_ROWS, :].astype(F32)
                for group in range(parity, groups, 2)
            ).astype(BF16)
            for parity in range(2)
        )
        keys_t[at, :] = jnp.where(lane < HALF, low, roll_lanes(high, HALF))
        values_t[at, :] = jnp.where(lane < HALF, roll_lanes(low, HALF), high)
    for target, turned in ((k_ref, keys_t), (v_ref, values_t)):
        for tile in range(CH // LANES):
            at = slice(tile * LANES, (tile + 1) * LANES)
            target[:, at] = turned[at, :].T
    for half in range(2):
        heads = [
            jnp.concatenate(
                [got_ref[(4 * half + i) * groups + group, Q_ROWS, :] for group in range(groups)],
                axis=0,
            )
            for i in range(4)
        ]
        for i, block in enumerate(heads_to_tiles(heads)):
            at = slice((3 * half + i) * LANES, (3 * half + i + 1) * LANES)
            q_ref[:, at] = block
    lane = lanes_of(8)
    for device in range(count):
        piece = got_ref[device, Q_ROWS, :].astype(F32)
        eight = roll_lanes(piece[0:8], 32)
        for a in range(1, 4):
            eight = jnp.where(
                lane >= 32 * a, roll_lanes(piece[8 * a : 8 * a + 8], 32 * a - 96), eight
            )
        for tile in range(CH // LANES):
            at = slice(tile * LANES, (tile + 1) * LANES)
            if device < TAPS:
                taps_ref[device, :, at] = eight[tile : tile + 1]
            else:
                gain_ref[:, at] = eight[tile : tile + 1]


def exchange(pieces):
    return lax.all_to_all(pieces, "tm", split_axis=0, concat_axis=0, tiled=True)


def local(resid, queries, keys, values, gain, taps, cotangent):
    count = lax.axis_size("tm")
    sections = lax.axis_size("section")
    groups = count // HEADS
    frames = resid.shape[1]
    total = frames * count
    own = total // groups
    half = total // 2
    place = lax.axis_index("tm").astype(jnp.int32).reshape(1)
    edge = 16
    matmul = 2 * own * half * LANES

    resid, queries, keys, values, cotangent = (
        array[0] for array in (resid, queries, keys, values, cotangent)
    )
    taps = taps.reshape(TAPS, 1, CH)
    up = [(i, i + 1) for i in range(count - 1)]
    down = [(i + 1, i) for i in range(count - 1)]
    partner = [(i, i ^ 1) for i in range(count)]
    before = lax.ppermute(
        jnp.concatenate([resid[frames - SUB :], cotangent[frames - edge :]], axis=0), "tm", up
    )
    after = lax.ppermute(jnp.concatenate([resid[:SUB], cotangent[:edge]], axis=0), "tm", down)

    shape = jax.ShapeDtypeStruct
    pieces = shape((count, PIECE_ROWS, LANES), BF16)
    rows_shape = shape((frames, CH), BF16)
    own_shape = shape((own, LANES), F32)
    kept_shape = shape((own, half), BF16)
    sent = call(
        lambda *refs: pack_kernel(groups, *refs),
        pieces,
        [ANY] * 3,
        ANY,
        [pltpu.VMEM((frames, CH), BF16)] * 3
        + [pltpu.VMEM((count, PIECE_ROWS, LANES), BF16)]
        + [pltpu.VMEM((CH, LANES), BF16)] * 2
        + [pltpu.SemaphoreType.DMA((3,)), pltpu.SemaphoreType.DMA((HEADS,))],
        56,
        1000000,
        "pack_qkv",
    )(queries, keys, values)
    got = call(
        lambda *refs: None,
        pieces,
        [ANY] * 5,
        ANY,
        [],
        8,
        0,
        "received",
        aliases={0: 0},
    )(exchange(sent), before, after, gain, taps)
    swapped = lax.ppermute(got, "tm", partner)

    block, chunk = 512, 512
    attend_scratch = [
        pltpu.VMEM((LANES, half), BF16),
        pltpu.VMEM((half, LANES), BF16),
        pltpu.VMEM((2, block, half), F32),
    ]
    *state, own_kept = call(
        lambda *refs: forward_first_kernel(block, chunk, *refs),
        (own_shape,) * 3 + (kept_shape,),
        [VMEM],
        (VMEM,) * 4,
        attend_scratch,
        36,
        2 * matmul,
        "attend_forward_own",
        own * half,
    )(got)
    results, head_out, other_kept = call(
        lambda *refs: forward_second_kernel(block, chunk, groups, *refs),
        (shape((count, 48, LANES), BF16), shape((own, LANES), BF16), kept_shape),
        [SMEM] + [VMEM] * 5,
        (VMEM,) * 3,
        attend_scratch,
        36,
        2 * matmul,
        "attend_forward_other",
        own * half,
    )(place, got, swapped, *state)
    returned = exchange(results)

    grads_sent, block_out, grad_resid = call(
        lambda *refs: conv_kernel(groups, count, *refs),
        (shape((count, SUB, LANES), BF16), rows_shape, rows_shape),
        [SMEM] + [VMEM] * 7,
        (VMEM,) * 3,
        [
            pltpu.VMEM((frames + 2 * SUB, CH), F32),
            pltpu.VMEM((frames + 2 * SUB, LANES), F32),
            pltpu.VMEM((frames + 2 * edge, LANES), F32),
            pltpu.VMEM((frames, CH), F32),
            pltpu.VMEM((TAPS + 1, CH), F32),
            pltpu.VMEM((frames + 2 * edge + 8, LANES), F32),
            pltpu.VMEM((frames + 16, LANES), F32),
        ],
        16,
        10000000,
        "conv_block",
    )(place, returned, resid, cotangent, before, after, gain, taps)
    grads_got = exchange(grads_sent)
    arrived = lax.ppermute(
        block_out, "section", [(i, (i + 1) % sections) for i in range(sections)]
    )

    block, chunk = own, 512
    backward_scratch = [
        pltpu.VMEM((LANES, half), BF16),
        pltpu.VMEM((half, LANES), BF16),
        pltpu.VMEM((HEAD_DIM, half), F32),
        pltpu.VMEM((HEAD_DIM, half), F32),
    ]
    part_shape = shape((count, HEAD_DIM, LANES), BF16)
    other_part, grad_q = call(
        lambda *refs: backward_first_kernel(block, chunk, *refs),
        (part_shape, own_shape),
        [VMEM] * 5,
        (VMEM,) * 2,
        backward_scratch,
        36,
        4 * matmul,
        "attend_backward_other",
    )(other_kept, swapped, got, grads_got, head_out)
    arrived_part = lax.ppermute(other_part, "tm", partner)
    own_part, grad_q_pieces = call(
        lambda *refs: backward_second_kernel(block, chunk, *refs),
        (part_shape, shape((count, SUB, LANES), BF16)),
        [VMEM] * 5,
        (VMEM,) * 2,
        backward_scratch,
        36,
        4 * matmul,
        "attend_backward_own",
    )(own_kept, got, grads_got, head_out, grad_q)
    grads_out = call(
        join_kernel,
        pieces,
        [VMEM] * 3,
        VMEM,
        [],
        8,
        1000000,
        "join_grads",
    )(own_part, arrived_part, grad_q_pieces)
    back = exchange(grads_out)

    grad_q, grad_k, grad_v, grad_gain, grad_taps, next_input = call(
        lambda *refs: unpack_kernel(groups, *refs),
        (
            rows_shape,
            rows_shape,
            rows_shape,
            shape((1, CH), F32),
            shape((TAPS, 1, CH), F32),
            rows_shape,
        ),
        [VMEM] * 2,
        (VMEM,) * 6,
        [pltpu.VMEM((CH, LANES), BF16)] * 2,
        8,
        1000000,
        "unpack_grads",
    )(back, arrived)
    return (
        next_input[None],
        grad_resid[None],
        grad_q[None],
        grad_k[None],
        grad_v[None],
        grad_gain,
        grad_taps.reshape(1, TAPS, CH),
    )


def solution(mesh):
    rows = P("section", "tm", None)
    in_specs = (rows, rows, rows, rows, P("section", None), P("section", None, None), rows)
    out_specs = (rows, rows, rows, rows, rows, P("section", None), P("section", None, None))
    return jax.shard_map(local, mesh=mesh, in_specs=in_specs, out_specs=out_specs, check_vma=False)
```

```python
import math

import jax
import jax.numpy as jnp
from jax import lax
from jax.experimental import pallas as pl
from jax.experimental.pallas import tpu as pltpu
from jax.sharding import PartitionSpec as P

HEADS = 8
HEAD_DIM = 96
TAPS = 31
CH = 768
LANES = 128
EPS = 1e-06

SCALE = HEAD_DIM ** (-0.5)
SCALE2 = SCALE * math.log2(math.e)

F32 = jnp.float32
BF16 = jnp.bfloat16

KV_ROWS = slice(0, 96)
Q_ROWS = slice(96, 128)
PIECE_ROWS = 128
HALF = 64
OWN_FACTOR = range(96, 99)
OTHER_FACTOR = range(99, 102)
SUB = 32

VMEM = pl.BlockSpec(memory_space=pltpu.VMEM)
SMEM = pl.BlockSpec(memory_space=pltpu.SMEM)
ANY = pl.BlockSpec(memory_space=pl.ANY)
MIB = 1024 * 1024


def stripes(block, group):
    low, high = 16 * group, HALF + 16 * group
    return jnp.concatenate([block[low : low + 16], block[high : high + 16]], axis=0)


def lanes_of(rows):
    return lax.broadcasted_iota(jnp.int32, (rows, LANES), 1)


def roll_lanes(block, by):
    by = by % LANES
    return block if by == 0 else pltpu.roll(block, by, 1)


def heads_to_tiles(heads):
    lane = lanes_of(heads[0].shape[0])
    second = roll_lanes(heads[1], 96)
    third = roll_lanes(heads[2], 64)
    fourth = roll_lanes(heads[3], 32)
    return (
        jnp.where(lane < 96, heads[0], second),
        jnp.where(lane < 64, second, third),
        jnp.where(lane < 32, third, fourth),
    )


def tiles_to_heads(tiles):
    lane = lanes_of(tiles[0].shape[0])
    return (
        tiles[0],
        roll_lanes(jnp.where(lane >= 96, tiles[0], tiles[1]), 32),
        roll_lanes(jnp.where(lane >= 64, tiles[1], tiles[2]), 64),
        roll_lanes(tiles[2], 96),
    )


def call(kernel, out_shape, in_specs, out_specs, scratch, limit, flops, name, transcendentals=0, aliases={}):
    return pl.pallas_call(
        kernel,
        out_shape=out_shape,
        in_specs=in_specs,
        out_specs=out_specs,
        scratch_shapes=scratch,
        input_output_aliases=aliases,
        compiler_params=pltpu.CompilerParams(vmem_limit_bytes=limit * MIB),
        cost_estimate=pl.CostEstimate(
            flops=flops, bytes_accessed=2 * MIB, transcendentals=transcendentals
        ),
        name=name,
    )


def pack_kernel(
    groups, q_hbm, k_hbm, v_hbm, send_hbm, q_ref, k_ref, v_ref, send_ref, keys_t, values_t, sems, sent
):
    copies = [
        pltpu.make_async_copy(source, target, sems.at[i])
        for i, (source, target) in enumerate(((q_hbm, q_ref), (k_hbm, k_ref), (v_hbm, v_ref)))
    ]
    for copy in copies:
        copy.start()
    copies[0].wait()
    frames = q_ref.shape[0]
    lane = lanes_of(frames)
    for half in range(2):
        tiles = [
            q_ref[:, (3 * half + i) * LANES : (3 * half + i + 1) * LANES] for i in range(3)
        ]
        for i, block in enumerate(tiles_to_heads(tiles)):
            block = jnp.where(lane < HEAD_DIM, block, jnp.zeros_like(block))
            for group in range(groups):
                send_ref[(4 * half + i) * groups + group, Q_ROWS, :] = stripes(block, group)
    for copy, source, turned in ((copies[1], k_ref, keys_t), (copies[2], v_ref, values_t)):
        copy.wait()
        for tile in range(CH // LANES):
            at = slice(tile * LANES, (tile + 1) * LANES)
            turned[at, :] = source[:, at].T
    lane = lanes_of(HEAD_DIM)
    out = []
    for head in range(HEADS):
        at = slice(head * HEAD_DIM, (head + 1) * HEAD_DIM)
        keys_here, values_here = keys_t[at, :], values_t[at, :]
        halves = (
            jnp.where(lane < HALF, keys_here, roll_lanes(values_here, HALF)),
            jnp.where(lane < HALF, roll_lanes(keys_here, HALF), values_here),
        )
        for group in range(groups):
            send_ref[head * groups + group, KV_ROWS, :] = halves[group % 2]
        devices = pl.ds(head * groups, groups)
        out.append(
            pltpu.make_async_copy(send_ref.at[devices], send_hbm.at[devices], sent.at[head])
        )
        out[-1].start()
    for copy in out:
        copy.wait()


def fill_half(half_ref, start, stop, keys_t, values_t, keys, values):
    lane = lanes_of(HEAD_DIM)
    zeros = jnp.zeros((LANES - HEAD_DIM, LANES), BF16)
    for pair in range(start // LANES, stop // LANES):
        at = slice(pair * LANES, (pair + 1) * LANES)
        even = half_ref[2 * pair, KV_ROWS, :]
        odd = half_ref[2 * pair + 1, KV_ROWS, :]
        for turned, natural, block in (
            (keys_t, keys, jnp.where(lane < HALF, even, roll_lanes(odd, HALF))),
            (values_t, values, jnp.where(lane < HALF, roll_lanes(even, HALF), odd)),
        ):
            block = jnp.concatenate([block, zeros], axis=0)
            if turned is not None:
                turned[:, at] = block
            if natural is not None:
                natural[at, :] = block.T


def attend(got_ref, half_ref, state, finish, block, chunk, kept_ref, keys, values, scores):
    key_count = keys.shape[1]
    per = block // SUB
    blocks = got_ref.shape[0] // per

    def rows_of(step):
        return got_ref[step * per : (step + 1) * per, Q_ROWS, :].reshape(block, LANES)

    def score(step, rows, start, peak):
        part = jnp.dot(rows, keys[:, start : start + chunk], preferred_element_type=F32)
        scores[step % 2, :, start : start + chunk] = part
        for tile in range(0, chunk, LANES):
            peak = jnp.maximum(peak, part[:, tile : tile + LANES])
        return peak

    lowest = jnp.full((block, LANES), -jnp.inf, F32)
    peak = lowest
    rows = rows_of(0)
    for start in range(0, key_count, chunk):
        fill_half(half_ref, start, start + chunk, keys, None, None, values)
        peak = score(0, rows, start, peak)
    for step in range(blocks):
        at = slice(step * block, (step + 1) * block)
        top = jnp.broadcast_to(jnp.max(peak, axis=1, keepdims=True) * SCALE2, (block, LANES))
        if state is None:
            total = jnp.zeros((block, LANES), F32)
            result = jnp.zeros((block, LANES), F32)
        else:
            old = state[0][at, :]
            top = jnp.maximum(top, old)
            shrink = jnp.exp2(old - top)
            total = state[1][at, :] * shrink
            result = state[2][at, :] * shrink
        tops = jnp.concatenate([top] * (chunk // LANES), axis=1)
        peak = lowest
        if step + 1 < blocks:
            rows = rows_of(step + 1)
        for start in range(0, key_count, chunk):
            if step + 1 < blocks:
                peak = score(step + 1, rows, start, peak)
            weights = jnp.exp2(scores[step % 2, :, start : start + chunk] * SCALE2 - tops)
            for tile in range(0, chunk, LANES):
                total = total + weights[:, tile : tile + LANES]
            weights = weights.astype(BF16)
            kept_ref[at, start : start + chunk] = weights
            result = result + jnp.dot(
                weights, values[start : start + chunk, :], preferred_element_type=F32
            )
        finish(at, top, total, result)


def forward_first_kernel(
    block,
    chunk,
    got_ref,
    top_ref,
    total_ref,
    result_ref,
    kept_ref,
    keys,
    values,
    scores,
):
    def finish(at, top, total, result):
        top_ref[at, :] = top
        total_ref[at, :] = total
        result_ref[at, :] = result

    attend(got_ref, got_ref, None, finish, block, chunk, kept_ref, keys, values, scores)


def forward_second_kernel(
    block,
    chunk,
    groups,
    place_ref,
    got_ref,
    swapped_ref,
    top_ref,
    total_ref,
    result_ref,
    send_ref,
    out_ref,
    kept_ref,
    keys,
    values,
    scores,
):
    def finish(at, top, total, result):
        total = jnp.sum(total, axis=1, keepdims=True)
        merged = result / total
        lane = lanes_of(block)
        for spots, rest in (
            (OWN_FACTOR, jnp.exp2(top_ref[at, :] - top) / total),
            (OTHER_FACTOR, jnp.broadcast_to(1.0 / total, (block, LANES))),
        ):
            for spot in spots:
                part = rest.astype(BF16).astype(F32)
                merged = jnp.where(lane == spot, part, merged)
                rest = rest - part
        out_ref[at, :] = merged.astype(BF16)

    state = (top_ref, total_ref, result_ref)
    attend(got_ref, swapped_ref, state, finish, block, chunk, kept_ref, keys, values, scores)
    count = got_ref.shape[0]
    before = place_ref[0] % groups >= groups // 2
    side, offset = jnp.where(before, -1, 1), jnp.where(before, 16, 0)
    for device in range(count):
        near = jnp.clip(device + side, 0, count - 1) * SUB + offset
        send_ref[device, 0:SUB, :] = out_ref[device * SUB : (device + 1) * SUB, :]
        send_ref[device, SUB:48, :] = out_ref[pl.ds(pl.multiple_of(near, 16), 16), :]


def conv_kernel(
    groups,
    count,
    place_ref,
    got_ref,
    resid_ref,
    cot_ref,
    before_ref,
    after_ref,
    gain_ref,
    taps_ref,
    send_ref,
    out_ref,
    grad_ref,
    mixed,
    normed_both,
    grad_conv_both,
    scaled,
    sums,
    shifted,
    grad_wide_both,
):
    frames = resid_ref.shape[0]
    sub = frames // groups
    wide = frames + 2 * sub
    edge = 16
    inner = frames + 2 * edge
    tiles = CH // LANES
    place = place_ref[0]

    square = jnp.zeros((wide, LANES), F32)
    for half in range(2):
        heads = []
        for i in range(4):
            first = (4 * half + i) * groups
            pieces = [got_ref[first + group].astype(F32) for group in range(groups)]
            parts = [piece[32:48] for piece in pieces[2:]]
            parts += [piece[0:16] for piece in pieces] + [piece[16:32] for piece in pieces]
            parts += [piece[32:48] for piece in pieces[:2]]
            heads.append(jnp.concatenate(parts, axis=0))
        for i, attended in enumerate(heads_to_tiles(heads)):
            at = slice((3 * half + i) * LANES, (3 * half + i + 1) * LANES)
            block = jnp.concatenate(
                [before_ref[0:sub, at], resid_ref[:, at], after_ref[0:sub, at]], axis=0
            ).astype(F32)
            block = block + attended
            mixed[:, at] = block
            square = square + block * block
    inverse = lax.rsqrt(jnp.sum(square, axis=1, keepdims=True) * (1.0 / CH) + EPS)

    row = lax.broadcasted_iota(jnp.int32, (wide, LANES), 0)
    inside = ((row >= sub) | (place > 0)) & ((row < sub + frames) | (place < count - 1))
    lo, hi = sub - edge, sub - edge + inner
    row_inner = lax.broadcasted_iota(jnp.int32, (inner, LANES), 0) + lo
    inside_inner = ((row_inner >= sub) | (place > 0)) & (
        (row_inner < sub + frames) | (place < count - 1)
    )
    own = slice(sub, sub + frames)
    inverse_own = inverse[sub : sub + frames]

    for tile in range(2):
        grad_wide_both[tile, 0:8, :] = jnp.zeros((8, LANES), F32)
        grad_wide_both[tile, 8 + frames : 16 + frames, :] = jnp.zeros((8, LANES), F32)
    dots = jnp.zeros((frames, LANES), F32)
    for tile in range(tiles):
        at = slice(tile * LANES, (tile + 1) * LANES)
        gain_row = gain_ref[0:1, at]
        value = (mixed[:, at] * inverse * gain_row).astype(BF16).astype(F32)
        normed = normed_both.at[tile % 2]
        grad_conv = grad_conv_both.at[tile % 2]
        grad_wide = grad_wide_both.at[tile % 2]
        normed[...] = jnp.where(inside, value, 0.0)
        conv = jnp.zeros((inner, LANES), F32)
        for b in range(8):
            part = jnp.zeros((inner + 8, LANES), F32)
            for tap in range(b, TAPS, 8):
                part = part + taps_ref[tap, :, at] * normed[tap - b : tap - b + inner + 8, :]
            shifted[b] = part
            conv = conv + shifted[b, b + 1 : b + 1 + inner, :]
        sig = jax.nn.sigmoid(conv)
        out_ref[:, at] = (
            mixed[own, at] + (conv * sig)[edge : edge + frames]
        ).astype(BF16)
        cot = jnp.concatenate(
            [before_ref[sub : sub + edge, at], cot_ref[:, at], after_ref[sub : sub + edge, at]],
            axis=0,
        ).astype(F32)
        value = (cot * sig * (1.0 + conv * (1.0 - sig))).astype(BF16).astype(F32)
        grad_conv[...] = jnp.where(inside_inner, value, 0.0)
        grad_normed = jnp.zeros((frames, LANES), F32)
        grad_wide[8 : 8 + frames, :] = grad_conv[edge : edge + frames, :]
        for b in range(8):
            part = jnp.zeros((frames + 8, LANES), F32)
            grad_here = grad_wide[7 - b : 15 - b + frames, :]
            for tap in range(b, TAPS, 8):
                first = tap - b
                part = part + taps_ref[TAPS - 1 - tap, :, at] * grad_conv[first : first + frames + 8, :]
                first = first + edge
                sums[tap : tap + 1, at] = jnp.sum(
                    grad_here * normed[first : first + frames + 8, :], axis=0, keepdims=True
                )
            shifted[8 + b, 0 : frames + 8, :] = part
            grad_normed = grad_normed + shifted[8 + b, b + 1 : b + 1 + frames, :]
        unit = mixed[own, at] * inverse_own
        sums[TAPS : TAPS + 1, at] = jnp.sum(grad_normed * unit, axis=0, keepdims=True)
        here = grad_normed * gain_row
        scaled[:, at] = here
        dots = dots + here * unit
    mean = jnp.sum(dots, axis=1, keepdims=True) * (1.0 / CH)

    lane = lanes_of(sub)
    sublane = lax.broadcasted_iota(jnp.int32, (8, LANES), 0)
    for half in range(2):
        grads = []
        for i in range(3):
            at = slice((3 * half + i) * LANES, (3 * half + i + 1) * LANES)
            unit = mixed[own, at] * inverse_own
            grad = cot_ref[:, at].astype(F32) + inverse_own * (scaled[:, at] - unit * mean)
            grad_ref[:, at] = grad.astype(BF16)
            grads.append(grad)
        for i, block in enumerate(tiles_to_heads(grads)):
            for group in range(groups):
                device = (4 * half + i) * groups + group
                eight = jnp.zeros((8, LANES), F32)
                for tile in range(tiles):
                    line = sums[device : device + 1, tile * LANES : (tile + 1) * LANES]
                    eight = jnp.where(sublane == tile, line, eight)
                spare = jnp.concatenate(
                    [roll_lanes(eight, 96 - 32 * a) for a in range(4)], axis=0
                )
                piece = jnp.where(lane < HEAD_DIM, stripes(block, group), spare)
                send_ref[device] = piece.astype(BF16)


def backward(
    factor_lanes,
    kept_ref,
    half_ref,
    got_ref,
    grads_ref,
    out_ref,
    part_ref,
    finish,
    block,
    chunk,
    values_t,
    keys,
    grad_keys,
    grad_values,
):
    fill_half(half_ref, 0, chunk, None, values_t, keys, None)
    key_count = keys.shape[0]
    steps = got_ref.shape[0] * SUB // block
    lane_part = lanes_of(HEAD_DIM)
    per = block // SUB
    lane = lanes_of(block)
    for step in range(steps):
        sources = slice(step * per, (step + 1) * per)
        at = slice(step * block, (step + 1) * block)
        rows = got_ref[sources, Q_ROWS, :].reshape(block, LANES)
        grads = grads_ref[sources].reshape(block, LANES).astype(F32)
        out = out_ref[at, :].astype(F32)
        in_factor = (lane >= factor_lanes.start) & (lane < factor_lanes.stop)
        factor = jnp.sum(jnp.where(in_factor, out, 0.0), axis=1, keepdims=True)
        grads = jnp.where(lane < HEAD_DIM, grads * factor, 0.0).astype(BF16)
        delta = jnp.sum(grads.astype(F32) * out, axis=1, keepdims=True)
        rows_t = rows.T[0:HEAD_DIM]
        grads_t = grads.T[0:HEAD_DIM]
        result = jnp.zeros((block, LANES), F32)
        for start in range(0, key_count, chunk):
            part = slice(start, start + chunk)
            if step == 0 and start + chunk < key_count:
                fill_half(half_ref, start + chunk, start + 2 * chunk, None, values_t, keys, None)
            weights = kept_ref[at, part]
            grad_probs = jnp.dot(grads, values_t[:, part], preferred_element_type=F32)
            grad_scores = (weights.astype(F32) * (grad_probs - delta)).astype(BF16)
            result = result + jnp.dot(grad_scores, keys[part, :], preferred_element_type=F32)
            grad_k = jnp.dot(rows_t, grad_scores, preferred_element_type=F32)
            grad_v = jnp.dot(grads_t, weights, preferred_element_type=F32)
            if step > 0:
                grad_k = grad_k + grad_keys[:, part]
                grad_v = grad_v + grad_values[:, part]
            if step + 1 < steps:
                grad_keys[:, part] = grad_k
                grad_values[:, part] = grad_v
                continue
            grad_k = (grad_k * SCALE).astype(BF16)
            grad_v = grad_v.astype(BF16)
            for first in range(0, chunk, LANES):
                pair = (start + first) // LANES
                here_k = grad_k[:, first : first + LANES]
                here_v = grad_v[:, first : first + LANES]
                part_ref[2 * pair] = jnp.where(lane_part < HALF, here_k, roll_lanes(here_v, HALF))
                part_ref[2 * pair + 1] = jnp.where(
                    lane_part < HALF, roll_lanes(here_k, HALF), here_v
                )
        finish(step, sources, at, result * SCALE)


def backward_first_kernel(
    block,
    chunk,
    kept_ref,
    swapped_ref,
    got_ref,
    grads_ref,
    out_ref,
    part_ref,
    grad_q_ref,
    *scratch,
):
    def finish(step, sources, at, result):
        grad_q_ref[at, :] = result

    given = (kept_ref, swapped_ref, got_ref, grads_ref, out_ref)
    backward(OTHER_FACTOR, *given, part_ref, finish, block, chunk, *scratch)


def backward_second_kernel(
    block,
    chunk,
    kept_ref,
    got_ref,
    grads_ref,
    out_ref,
    grad_q_ref,
    part_ref,
    piece_ref,
    *scratch,
):
    sums = jnp.zeros((SUB, LANES), F32)
    for source in range(grads_ref.shape[0]):
        sums = sums + grads_ref[source].astype(F32)

    def finish(step, sources, at, result):
        result = (result + grad_q_ref[at, :]).reshape(-1, SUB, LANES)
        lane = lax.broadcasted_iota(jnp.int32, result.shape, 2)
        piece_ref[sources] = jnp.where(lane < HEAD_DIM, result, sums[None]).astype(BF16)

    given = (kept_ref, got_ref, got_ref, grads_ref, out_ref)
    backward(OWN_FACTOR, *given, part_ref, finish, block, chunk, *scratch)


def join_kernel(part_ref, other_ref, piece_ref, send_ref):
    for device in range(part_ref.shape[0]):
        send_ref[device, KV_ROWS, :] = (
            part_ref[device].astype(F32) + other_ref[device].astype(F32)
        ).astype(BF16)
        send_ref[device, Q_ROWS, :] = piece_ref[device]


def unpack_kernel(
    groups, got_ref, arrived_ref, q_ref, k_ref, v_ref, gain_ref, taps_ref, next_ref, keys_t, values_t
):
    next_ref[...] = arrived_ref[...]
    count = got_ref.shape[0]
    lane = lanes_of(HEAD_DIM)
    for head in range(HEADS):
        at = slice(head * HEAD_DIM, (head + 1) * HEAD_DIM)
        low, high = (
            sum(
                got_ref[head * groups + group, KV_ROWS, :].astype(F32)
                for group in range(parity, groups, 2)
            ).astype(BF16)
            for parity in range(2)
        )
        keys_t[at, :] = jnp.where(lane < HALF, low, roll_lanes(high, HALF))
        values_t[at, :] = jnp.where(lane < HALF, roll_lanes(low, HALF), high)
    for target, turned in ((k_ref, keys_t), (v_ref, values_t)):
        for tile in range(CH // LANES):
            at = slice(tile * LANES, (tile + 1) * LANES)
            target[:, at] = turned[at, :].T
    for half in range(2):
        heads = [
            jnp.concatenate(
                [
                    got_ref[(4 * half + i) * groups + group, Q_ROWS.start + row : Q_ROWS.start + row + 16, :]
                    for row in (0, 16)
                    for group in range(groups)
                ],
                axis=0,
            )
            for i in range(4)
        ]
        for i, block in enumerate(heads_to_tiles(heads)):
            at = slice((3 * half + i) * LANES, (3 * half + i + 1) * LANES)
            q_ref[:, at] = block
    lane = lanes_of(8)
    for device in range(count):
        piece = got_ref[device, Q_ROWS, :].astype(F32)
        eight = roll_lanes(piece[0:8], 32)
        for a in range(1, 4):
            eight = jnp.where(
                lane >= 32 * a, roll_lanes(piece[8 * a : 8 * a + 8], 32 * a - 96), eight
            )
        for tile in range(CH // LANES):
            at = slice(tile * LANES, (tile + 1) * LANES)
            if device < TAPS:
                taps_ref[device, :, at] = eight[tile : tile + 1]
            else:
                gain_ref[:, at] = eight[tile : tile + 1]


def exchange(pieces):
    return lax.all_to_all(pieces, "tm", split_axis=0, concat_axis=0, tiled=True)


def local(resid, queries, keys, values, gain, taps, cotangent):
    count = lax.axis_size("tm")
    sections = lax.axis_size("section")
    groups = count // HEADS
    frames = resid.shape[1]
    total = frames * count
    own = total // groups
    half = total // 2
    place = lax.axis_index("tm").astype(jnp.int32).reshape(1)
    edge = 16
    matmul = 2 * own * half * LANES

    resid, queries, keys, values, cotangent = (
        array[0] for array in (resid, queries, keys, values, cotangent)
    )
    taps = taps.reshape(TAPS, 1, CH)
    up = [(i, i + 1) for i in range(count - 1)]
    down = [(i + 1, i) for i in range(count - 1)]
    partner = [(i, i ^ 1) for i in range(count)]
    before = lax.ppermute(
        jnp.concatenate([resid[frames - SUB :], cotangent[frames - edge :]], axis=0), "tm", up
    )
    after = lax.ppermute(jnp.concatenate([resid[:SUB], cotangent[:edge]], axis=0), "tm", down)

    shape = jax.ShapeDtypeStruct
    pieces = shape((count, PIECE_ROWS, LANES), BF16)
    rows_shape = shape((frames, CH), BF16)
    own_shape = shape((own, LANES), F32)
    kept_shape = shape((own, half), BF16)
    sent = call(
        lambda *refs: pack_kernel(groups, *refs),
        pieces,
        [ANY] * 3,
        ANY,
        [pltpu.VMEM((frames, CH), BF16)] * 3
        + [pltpu.VMEM((count, PIECE_ROWS, LANES), BF16)]
        + [pltpu.VMEM((CH, LANES), BF16)] * 2
        + [pltpu.SemaphoreType.DMA((3,)), pltpu.SemaphoreType.DMA((HEADS,))],
        56,
        1000000,
        "pack_qkv",
    )(queries, keys, values)
    got = call(
        lambda *refs: None,
        pieces,
        [ANY] * 5,
        ANY,
        [],
        8,
        0,
        "received",
        aliases={0: 0},
    )(exchange(sent), before, after, gain, taps)
    swapped = lax.ppermute(got, "tm", partner)

    block, chunk = 512, 512
    attend_scratch = [
        pltpu.VMEM((LANES, half), BF16),
        pltpu.VMEM((half, LANES), BF16),
        pltpu.VMEM((2, block, half), F32),
    ]
    *state, own_kept = call(
        lambda *refs: forward_first_kernel(block, chunk, *refs),
        (own_shape,) * 3 + (kept_shape,),
        [VMEM],
        (VMEM,) * 4,
        attend_scratch,
        36,
        2 * matmul,
        "attend_forward_own",
        own * half,
    )(got)
    results, head_out, other_kept = call(
        lambda *refs: forward_second_kernel(block, chunk, groups, *refs),
        (shape((count, 48, LANES), BF16), shape((own, LANES), BF16), kept_shape),
        [SMEM] + [VMEM] * 5,
        (VMEM,) * 3,
        attend_scratch,
        36,
        2 * matmul,
        "attend_forward_other",
        own * half,
    )(place, got, swapped, *state)
    returned = exchange(results)

    grads_sent, block_out, grad_resid = call(
        lambda *refs: conv_kernel(groups, count, *refs),
        (shape((count, SUB, LANES), BF16), rows_shape, rows_shape),
        [SMEM] + [VMEM] * 7,
        (VMEM,) * 3,
        [
            pltpu.VMEM((frames + 2 * SUB, CH), F32),
            pltpu.VMEM((2, frames + 2 * SUB, LANES), F32),
            pltpu.VMEM((2, frames + 2 * edge, LANES), F32),
            pltpu.VMEM((frames, CH), F32),
            pltpu.VMEM((TAPS + 1, CH), F32),
            pltpu.VMEM((16, frames + 2 * edge + 8, LANES), F32),
            pltpu.VMEM((2, frames + 16, LANES), F32),
        ],
        16,
        10000000,
        "conv_block",
    )(place, returned, resid, cotangent, before, after, gain, taps)
    grads_got = exchange(grads_sent)
    arrived = lax.ppermute(
        block_out, "section", [(i, (i + 1) % sections) for i in range(sections)]
    )

    block, chunk = own, 512
    backward_scratch = [
        pltpu.VMEM((LANES, half), BF16),
        pltpu.VMEM((half, LANES), BF16),
        pltpu.VMEM((HEAD_DIM, half), F32),
        pltpu.VMEM((HEAD_DIM, half), F32),
    ]
    part_shape = shape((count, HEAD_DIM, LANES), BF16)
    other_part, grad_q = call(
        lambda *refs: backward_first_kernel(block, chunk, *refs),
        (part_shape, own_shape),
        [VMEM] * 5,
        (VMEM,) * 2,
        backward_scratch,
        36,
        4 * matmul,
        "attend_backward_other",
    )(other_kept, swapped, got, grads_got, head_out)
    arrived_part = lax.ppermute(other_part, "tm", partner)
    own_part, grad_q_pieces = call(
        lambda *refs: backward_second_kernel(block, chunk, *refs),
        (part_shape, shape((count, SUB, LANES), BF16)),
        [VMEM] * 5,
        (VMEM,) * 2,
        backward_scratch,
        36,
        4 * matmul,
        "attend_backward_own",
    )(own_kept, got, grads_got, head_out, grad_q)
    grads_out = call(
        join_kernel,
        pieces,
        [VMEM] * 3,
        VMEM,
        [],
        8,
        1000000,
        "join_grads",
    )(own_part, arrived_part, grad_q_pieces)
    back = exchange(grads_out)

    grad_q, grad_k, grad_v, grad_gain, grad_taps, next_input = call(
        lambda *refs: unpack_kernel(groups, *refs),
        (
            rows_shape,
            rows_shape,
            rows_shape,
            shape((1, CH), F32),
            shape((TAPS, 1, CH), F32),
            rows_shape,
        ),
        [VMEM] * 2,
        (VMEM,) * 6,
        [pltpu.VMEM((CH, LANES), BF16)] * 2,
        8,
        1000000,
        "unpack_grads",
    )(back, arrived)
    return (
        next_input[None],
        grad_resid[None],
        grad_q[None],
        grad_k[None],
        grad_v[None],
        grad_gain,
        grad_taps.reshape(1, TAPS, CH),
    )


def solution(mesh):
    rows = P("section", "tm", None)
    in_specs = (rows, rows, rows, rows, P("section", None), P("section", None, None), rows)
    out_specs = (rows, rows, rows, rows, rows, P("section", None), P("section", None, None))
    return jax.shard_map(local, mesh=mesh, in_specs=in_specs, out_specs=out_specs, check_vma=False)
```

```python
import math

import jax
import jax.numpy as jnp
from jax import lax
from jax.experimental import pallas as pl
from jax.experimental.pallas import tpu as pltpu
from jax.sharding import PartitionSpec as P

HEADS = 8
HEAD_DIM = 96
TAPS = 31
CH = 768
LANES = 128
EPS = 1e-06

SCALE = HEAD_DIM ** (-0.5)
SCALE2 = SCALE * math.log2(math.e)

F32 = jnp.float32
BF16 = jnp.bfloat16

KV_ROWS = slice(0, 96)
Q_ROWS = slice(96, 128)
PIECE_ROWS = 128
HALF = 64
OWN_FACTOR = range(96, 99)
OTHER_FACTOR = range(99, 102)
SUB = 32

VMEM = pl.BlockSpec(memory_space=pltpu.VMEM)
SMEM = pl.BlockSpec(memory_space=pltpu.SMEM)
ANY = pl.BlockSpec(memory_space=pl.ANY)
MIB = 1024 * 1024


def stripes(block, group):
    low, high = 16 * group, HALF + 16 * group
    return jnp.concatenate([block[low : low + 16], block[high : high + 16]], axis=0)


def lanes_of(rows):
    return lax.broadcasted_iota(jnp.int32, (rows, LANES), 1)


def roll_lanes(block, by):
    by = by % LANES
    return block if by == 0 else pltpu.roll(block, by, 1)


def heads_to_tiles(heads):
    lane = lanes_of(heads[0].shape[0])
    second = roll_lanes(heads[1], 96)
    third = roll_lanes(heads[2], 64)
    fourth = roll_lanes(heads[3], 32)
    return (
        jnp.where(lane < 96, heads[0], second),
        jnp.where(lane < 64, second, third),
        jnp.where(lane < 32, third, fourth),
    )


def tiles_to_heads(tiles):
    lane = lanes_of(tiles[0].shape[0])
    return (
        tiles[0],
        roll_lanes(jnp.where(lane >= 96, tiles[0], tiles[1]), 32),
        roll_lanes(jnp.where(lane >= 64, tiles[1], tiles[2]), 64),
        roll_lanes(tiles[2], 96),
    )


def call(kernel, out_shape, in_specs, out_specs, scratch, limit, flops, name, transcendentals=0, aliases={}):
    return pl.pallas_call(
        kernel,
        out_shape=out_shape,
        in_specs=in_specs,
        out_specs=out_specs,
        scratch_shapes=scratch,
        input_output_aliases=aliases,
        compiler_params=pltpu.CompilerParams(vmem_limit_bytes=limit * MIB),
        cost_estimate=pl.CostEstimate(
            flops=flops, bytes_accessed=2 * MIB, transcendentals=transcendentals
        ),
        name=name,
    )


def pack_kernel(
    groups, q_hbm, k_hbm, v_hbm, send_hbm, q_ref, k_ref, v_ref, send_ref, keys_t, values_t, sems, sent
):
    copies = [
        pltpu.make_async_copy(source, target, sems.at[i])
        for i, (source, target) in enumerate(((q_hbm, q_ref), (k_hbm, k_ref), (v_hbm, v_ref)))
    ]
    for copy in copies:
        copy.start()
    copies[0].wait()
    frames = q_ref.shape[0]
    lane = lanes_of(frames)
    for half in range(2):
        tiles = [
            q_ref[:, (3 * half + i) * LANES : (3 * half + i + 1) * LANES] for i in range(3)
        ]
        for i, block in enumerate(tiles_to_heads(tiles)):
            block = jnp.where(lane < HEAD_DIM, block, jnp.zeros_like(block))
            for group in range(groups):
                send_ref[(4 * half + i) * groups + group, Q_ROWS, :] = stripes(block, group)
    for copy, source, turned in ((copies[1], k_ref, keys_t), (copies[2], v_ref, values_t)):
        copy.wait()
        for tile in range(CH // LANES):
            at = slice(tile * LANES, (tile + 1) * LANES)
            turned[at, :] = source[:, at].T
    lane = lanes_of(HEAD_DIM)
    out = []
    for head in range(HEADS):
        at = slice(head * HEAD_DIM, (head + 1) * HEAD_DIM)
        keys_here, values_here = keys_t[at, :], values_t[at, :]
        halves = (
            jnp.where(lane < HALF, keys_here, roll_lanes(values_here, HALF)),
            jnp.where(lane < HALF, roll_lanes(keys_here, HALF), values_here),
        )
        for group in range(groups):
            send_ref[head * groups + group, KV_ROWS, :] = halves[group % 2]
        devices = pl.ds(head * groups, groups)
        out.append(
            pltpu.make_async_copy(send_ref.at[devices], send_hbm.at[devices], sent.at[head])
        )
        out[-1].start()
    for copy in out:
        copy.wait()


def fill_half(half_ref, start, stop, keys_t, values_t, keys, values):
    lane = lanes_of(HEAD_DIM)
    zeros = jnp.zeros((LANES - HEAD_DIM, LANES), BF16)
    first_row = lax.broadcasted_iota(jnp.int32, zeros.shape, 0) == 0
    ones = jnp.where(first_row, 1.0, 0.0).astype(BF16)
    for pair in range(start // LANES, stop // LANES):
        at = slice(pair * LANES, (pair + 1) * LANES)
        even = half_ref[2 * pair, KV_ROWS, :]
        odd = half_ref[2 * pair + 1, KV_ROWS, :]
        for turned, natural, pad, block in (
            (keys_t, keys, zeros, jnp.where(lane < HALF, even, roll_lanes(odd, HALF))),
            (values_t, values, ones, jnp.where(lane < HALF, roll_lanes(even, HALF), odd)),
        ):
            block = jnp.concatenate([block, pad], axis=0)
            if turned is not None:
                turned[:, at] = block
            if natural is not None:
                natural[at, :] = block.T


def attend(got_ref, half_ref, state, finish, block, chunk, kept_ref, keys, values, scores):
    key_count = keys.shape[1]
    per = block // SUB
    blocks = got_ref.shape[0] // per

    def rows_of(step):
        return got_ref[step * per : (step + 1) * per, Q_ROWS, :].reshape(block, LANES)

    def score(step, rows, start, peak):
        part = jnp.dot(rows, keys[:, start : start + chunk], preferred_element_type=F32)
        scores[step % 2, :, start : start + chunk] = part
        for tile in range(0, chunk, LANES):
            peak = jnp.maximum(peak, part[:, tile : tile + LANES])
        return peak

    lowest = jnp.full((block, LANES), -jnp.inf, F32)
    peak = lowest
    rows = rows_of(0)
    for start in range(0, key_count, chunk):
        fill_half(half_ref, start, start + chunk, keys, None, None, values)
        peak = score(0, rows, start, peak)
    for step in range(blocks):
        at = slice(step * block, (step + 1) * block)
        top = jnp.broadcast_to(jnp.max(peak, axis=1, keepdims=True) * SCALE2, (block, LANES))
        if state is None:
            result = jnp.zeros((block, LANES), F32)
        else:
            old = state[0][at, :]
            top = jnp.maximum(top, old)
            shrink = jnp.exp2(old - top)
            result = state[1][at, :] * shrink
        tops = jnp.concatenate([top] * (chunk // LANES), axis=1)
        peak = lowest
        if step + 1 < blocks:
            rows = rows_of(step + 1)
        for start in range(0, key_count, chunk):
            if step + 1 < blocks:
                peak = score(step + 1, rows, start, peak)
            weights = jnp.exp2(scores[step % 2, :, start : start + chunk] * SCALE2 - tops)
            weights = weights.astype(BF16)
            kept_ref[at, start : start + chunk] = weights
            result = result + jnp.dot(
                weights, values[start : start + chunk, :], preferred_element_type=F32
            )
        finish(at, top, result)


def forward_first_kernel(
    block,
    chunk,
    got_ref,
    top_ref,
    result_ref,
    kept_ref,
    keys,
    values,
    scores,
):
    def finish(at, top, result):
        top_ref[at, :] = top
        result_ref[at, :] = result

    attend(got_ref, got_ref, None, finish, block, chunk, kept_ref, keys, values, scores)


def forward_second_kernel(
    block,
    chunk,
    groups,
    place_ref,
    got_ref,
    swapped_ref,
    top_ref,
    result_ref,
    send_ref,
    out_ref,
    kept_ref,
    keys,
    values,
    scores,
):
    def finish(at, top, result):
        lane = lanes_of(block)
        total = jnp.sum(jnp.where(lane == HEAD_DIM, result, 0.0), axis=1, keepdims=True)
        merged = result / total
        for spots, rest in (
            (OWN_FACTOR, jnp.exp2(top_ref[at, :] - top) / total),
            (OTHER_FACTOR, jnp.broadcast_to(1.0 / total, (block, LANES))),
        ):
            for spot in spots:
                part = rest.astype(BF16).astype(F32)
                merged = jnp.where(lane == spot, part, merged)
                rest = rest - part
        out_ref[at, :] = merged.astype(BF16)

    state = (top_ref, result_ref)
    attend(got_ref, swapped_ref, state, finish, block, chunk, kept_ref, keys, values, scores)
    count = got_ref.shape[0]
    before = place_ref[0] % groups >= groups // 2
    side, offset = jnp.where(before, -1, 1), jnp.where(before, 16, 0)
    for device in range(count):
        near = jnp.clip(device + side, 0, count - 1) * SUB + offset
        send_ref[device, 0:SUB, :] = out_ref[device * SUB : (device + 1) * SUB, :]
        send_ref[device, SUB:48, :] = out_ref[pl.ds(pl.multiple_of(near, 16), 16), :]


def conv_kernel(
    groups,
    count,
    place_ref,
    got_ref,
    resid_ref,
    cot_ref,
    before_ref,
    after_ref,
    gain_ref,
    taps_ref,
    send_ref,
    out_ref,
    grad_ref,
    mixed,
    normed_both,
    grad_conv_both,
    scaled,
    sums,
    shifted,
    grad_wide_both,
):
    frames = resid_ref.shape[0]
    sub = frames // groups
    wide = frames + 2 * sub
    edge = 16
    inner = frames + 2 * edge
    tiles = CH // LANES
    place = place_ref[0]

    square = jnp.zeros((wide, LANES), F32)
    for half in range(2):
        heads = []
        for i in range(4):
            first = (4 * half + i) * groups
            pieces = [got_ref[first + group].astype(F32) for group in range(groups)]
            parts = [piece[32:48] for piece in pieces[2:]]
            parts += [piece[0:16] for piece in pieces] + [piece[16:32] for piece in pieces]
            parts += [piece[32:48] for piece in pieces[:2]]
            heads.append(jnp.concatenate(parts, axis=0))
        for i, attended in enumerate(heads_to_tiles(heads)):
            at = slice((3 * half + i) * LANES, (3 * half + i + 1) * LANES)
            block = jnp.concatenate(
                [before_ref[0:sub, at], resid_ref[:, at], after_ref[0:sub, at]], axis=0
            ).astype(F32)
            block = block + attended
            mixed[:, at] = block
            square = square + block * block
    inverse = lax.rsqrt(jnp.sum(square, axis=1, keepdims=True) * (1.0 / CH) + EPS)

    row = lax.broadcasted_iota(jnp.int32, (wide, LANES), 0)
    inside = ((row >= sub) | (place > 0)) & ((row < sub + frames) | (place < count - 1))
    lo, hi = sub - edge, sub - edge + inner
    row_inner = lax.broadcasted_iota(jnp.int32, (inner, LANES), 0) + lo
    inside_inner = ((row_inner >= sub) | (place > 0)) & (
        (row_inner < sub + frames) | (place < count - 1)
    )
    own = slice(sub, sub + frames)
    inverse_own = inverse[sub : sub + frames]

    for tile in range(2):
        grad_wide_both[tile, 0:8, :] = jnp.zeros((8, LANES), F32)
        grad_wide_both[tile, 8 + frames : 16 + frames, :] = jnp.zeros((8, LANES), F32)
    dots = jnp.zeros((frames, LANES), F32)
    for tile in range(tiles):
        at = slice(tile * LANES, (tile + 1) * LANES)
        gain_row = gain_ref[0:1, at]
        value = (mixed[:, at] * inverse * gain_row).astype(BF16).astype(F32)
        normed = normed_both.at[tile % 2]
        grad_conv = grad_conv_both.at[tile % 2]
        grad_wide = grad_wide_both.at[tile % 2]
        normed[...] = jnp.where(inside, value, 0.0)
        for b in range(8):
            part = None
            for tap in range(b, TAPS, 8):
                term = taps_ref[tap, :, at] * normed[tap - b : tap - b + inner + 8, :]
                part = term if part is None else part + term
            shifted[b] = part
            term = shifted[b, b + 1 : b + 1 + inner, :]
            conv = term if b == 0 else conv + term
        sig = jax.nn.sigmoid(conv)
        out_ref[:, at] = (
            mixed[own, at] + (conv * sig)[edge : edge + frames]
        ).astype(BF16)
        cot = jnp.concatenate(
            [before_ref[sub : sub + edge, at], cot_ref[:, at], after_ref[sub : sub + edge, at]],
            axis=0,
        ).astype(F32)
        value = (cot * sig * (1.0 + conv * (1.0 - sig))).astype(BF16).astype(F32)
        grad_conv[...] = jnp.where(inside_inner, value, 0.0)
        grad_wide[8 : 8 + frames, :] = grad_conv[edge : edge + frames, :]
        for b in range(8):
            part = None
            grad_here = grad_wide[7 - b : 15 - b + frames, :]
            for tap in range(b, TAPS, 8):
                first = tap - b
                term = taps_ref[TAPS - 1 - tap, :, at] * grad_conv[first : first + frames + 8, :]
                part = term if part is None else part + term
                first = first + edge
                sums[tap : tap + 1, at] = jnp.sum(
                    grad_here * normed[first : first + frames + 8, :], axis=0, keepdims=True
                )
            shifted[8 + b, 0 : frames + 8, :] = part
            term = shifted[8 + b, b + 1 : b + 1 + frames, :]
            grad_normed = term if b == 0 else grad_normed + term
        unit = mixed[own, at] * inverse_own
        sums[TAPS : TAPS + 1, at] = jnp.sum(grad_normed * unit, axis=0, keepdims=True)
        here = grad_normed * gain_row
        scaled[:, at] = here
        dots = dots + here * unit
    mean = jnp.sum(dots, axis=1, keepdims=True) * (1.0 / CH)

    lane = lanes_of(sub)
    sublane = lax.broadcasted_iota(jnp.int32, (8, LANES), 0)
    for half in range(2):
        grads = []
        for i in range(3):
            at = slice((3 * half + i) * LANES, (3 * half + i + 1) * LANES)
            unit = mixed[own, at] * inverse_own
            grad = cot_ref[:, at].astype(F32) + inverse_own * (scaled[:, at] - unit * mean)
            grad_ref[:, at] = grad.astype(BF16)
            grads.append(grad)
        for i, block in enumerate(tiles_to_heads(grads)):
            for group in range(groups):
                device = (4 * half + i) * groups + group
                eight = jnp.zeros((8, LANES), F32)
                for tile in range(tiles):
                    line = sums[device : device + 1, tile * LANES : (tile + 1) * LANES]
                    eight = jnp.where(sublane == tile, line, eight)
                spare = jnp.concatenate(
                    [roll_lanes(eight, 96 - 32 * a) for a in range(4)], axis=0
                )
                piece = jnp.where(lane < HEAD_DIM, stripes(block, group), spare)
                send_ref[device] = piece.astype(BF16)


def backward(
    factor_lanes,
    kept_ref,
    half_ref,
    got_ref,
    grads_ref,
    out_ref,
    part_ref,
    finish,
    block,
    chunk,
    values_t,
    keys,
    grad_keys,
    grad_values,
):
    fill_half(half_ref, 0, chunk, None, values_t, keys, None)
    key_count = keys.shape[0]
    steps = got_ref.shape[0] * SUB // block
    lane_part = lanes_of(HEAD_DIM)
    per = block // SUB
    lane = lanes_of(block)
    for step in range(steps):
        sources = slice(step * per, (step + 1) * per)
        at = slice(step * block, (step + 1) * block)
        rows = got_ref[sources, Q_ROWS, :].reshape(block, LANES)
        grads = grads_ref[sources].reshape(block, LANES).astype(F32)
        out = out_ref[at, :].astype(F32)
        in_factor = (lane >= factor_lanes.start) & (lane < factor_lanes.stop)
        factor = jnp.sum(jnp.where(in_factor, out, 0.0), axis=1, keepdims=True)
        grads = jnp.where(lane < HEAD_DIM, grads * factor, 0.0).astype(BF16)
        delta = jnp.sum(grads.astype(F32) * out, axis=1, keepdims=True)
        rows_t = rows.T[0:HEAD_DIM]
        grads_t = grads.T[0:HEAD_DIM]
        result = jnp.zeros((block, LANES), F32)
        for start in range(0, key_count, chunk):
            part = slice(start, start + chunk)
            if step == 0 and start + chunk < key_count:
                fill_half(half_ref, start + chunk, start + 2 * chunk, None, values_t, keys, None)
            weights = kept_ref[at, part]
            grad_probs = jnp.dot(grads, values_t[:, part], preferred_element_type=F32)
            grad_scores = (weights.astype(F32) * (grad_probs - delta)).astype(BF16)
            result = result + jnp.dot(grad_scores, keys[part, :], preferred_element_type=F32)
            grad_k = jnp.dot(rows_t, grad_scores, preferred_element_type=F32)
            grad_v = jnp.dot(grads_t, weights, preferred_element_type=F32)
            if step > 0:
                grad_k = grad_k + grad_keys[:, part]
                grad_v = grad_v + grad_values[:, part]
            if step + 1 < steps:
                grad_keys[:, part] = grad_k
                grad_values[:, part] = grad_v
                continue
            grad_k = (grad_k * SCALE).astype(BF16)
            grad_v = grad_v.astype(BF16)
            for first in range(0, chunk, LANES):
                pair = (start + first) // LANES
                here_k = grad_k[:, first : first + LANES]
                here_v = grad_v[:, first : first + LANES]
                part_ref[2 * pair] = jnp.where(lane_part < HALF, here_k, roll_lanes(here_v, HALF))
                part_ref[2 * pair + 1] = jnp.where(
                    lane_part < HALF, roll_lanes(here_k, HALF), here_v
                )
        finish(step, sources, at, result * SCALE)


def backward_first_kernel(
    block,
    chunk,
    kept_ref,
    swapped_ref,
    got_ref,
    grads_ref,
    out_ref,
    part_ref,
    grad_q_ref,
    *scratch,
):
    def finish(step, sources, at, result):
        grad_q_ref[at, :] = result

    given = (kept_ref, swapped_ref, got_ref, grads_ref, out_ref)
    backward(OTHER_FACTOR, *given, part_ref, finish, block, chunk, *scratch)


def backward_second_kernel(
    block,
    chunk,
    kept_ref,
    got_ref,
    grads_ref,
    out_ref,
    grad_q_ref,
    part_ref,
    piece_ref,
    *scratch,
):
    sums = jnp.zeros((SUB, LANES), F32)
    for source in range(grads_ref.shape[0]):
        sums = sums + grads_ref[source].astype(F32)

    def finish(step, sources, at, result):
        result = (result + grad_q_ref[at, :]).reshape(-1, SUB, LANES)
        lane = lax.broadcasted_iota(jnp.int32, result.shape, 2)
        piece_ref[sources] = jnp.where(lane < HEAD_DIM, result, sums[None]).astype(BF16)

    given = (kept_ref, got_ref, got_ref, grads_ref, out_ref)
    backward(OWN_FACTOR, *given, part_ref, finish, block, chunk, *scratch)


def join_kernel(part_ref, other_ref, piece_ref, send_ref):
    for device in range(part_ref.shape[0]):
        send_ref[device, KV_ROWS, :] = (
            part_ref[device].astype(F32) + other_ref[device].astype(F32)
        ).astype(BF16)
        send_ref[device, Q_ROWS, :] = piece_ref[device]


def unpack_kernel(
    groups, got_ref, arrived_ref, q_ref, k_ref, v_ref, gain_ref, taps_ref, next_ref, keys_t, values_t
):
    next_ref[...] = arrived_ref[...]
    count = got_ref.shape[0]
    lane = lanes_of(HEAD_DIM)
    for head in range(HEADS):
        at = slice(head * HEAD_DIM, (head + 1) * HEAD_DIM)
        low, high = (
            sum(
                got_ref[head * groups + group, KV_ROWS, :].astype(F32)
                for group in range(parity, groups, 2)
            ).astype(BF16)
            for parity in range(2)
        )
        keys_t[at, :] = jnp.where(lane < HALF, low, roll_lanes(high, HALF))
        values_t[at, :] = jnp.where(lane < HALF, roll_lanes(low, HALF), high)
    for target, turned in ((k_ref, keys_t), (v_ref, values_t)):
        for tile in range(CH // LANES):
            at = slice(tile * LANES, (tile + 1) * LANES)
            target[:, at] = turned[at, :].T
    for half in range(2):
        heads = [
            jnp.concatenate(
                [
                    got_ref[(4 * half + i) * groups + group, Q_ROWS.start + row : Q_ROWS.start + row + 16, :]
                    for row in (0, 16)
                    for group in range(groups)
                ],
                axis=0,
            )
            for i in range(4)
        ]
        for i, block in enumerate(heads_to_tiles(heads)):
            at = slice((3 * half + i) * LANES, (3 * half + i + 1) * LANES)
            q_ref[:, at] = block
    lane = lanes_of(8)
    for device in range(count):
        piece = got_ref[device, Q_ROWS, :].astype(F32)
        eight = roll_lanes(piece[0:8], 32)
        for a in range(1, 4):
            eight = jnp.where(
                lane >= 32 * a, roll_lanes(piece[8 * a : 8 * a + 8], 32 * a - 96), eight
            )
        for tile in range(CH // LANES):
            at = slice(tile * LANES, (tile + 1) * LANES)
            if device < TAPS:
                taps_ref[device, :, at] = eight[tile : tile + 1]
            else:
                gain_ref[:, at] = eight[tile : tile + 1]


def exchange(pieces):
    return lax.all_to_all(pieces, "tm", split_axis=0, concat_axis=0, tiled=True)


def local(resid, queries, keys, values, gain, taps, cotangent):
    count = lax.axis_size("tm")
    sections = lax.axis_size("section")
    groups = count // HEADS
    frames = resid.shape[1]
    total = frames * count
    own = total // groups
    half = total // 2
    place = lax.axis_index("tm").astype(jnp.int32).reshape(1)
    edge = 16
    matmul = 2 * own * half * LANES

    resid, queries, keys, values, cotangent = (
        array[0] for array in (resid, queries, keys, values, cotangent)
    )
    taps = taps.reshape(TAPS, 1, CH)
    up = [(i, i + 1) for i in range(count - 1)]
    down = [(i + 1, i) for i in range(count - 1)]
    partner = [(i, i ^ 1) for i in range(count)]
    before = lax.ppermute(
        jnp.concatenate([resid[frames - SUB :], cotangent[frames - edge :]], axis=0), "tm", up
    )
    after = lax.ppermute(jnp.concatenate([resid[:SUB], cotangent[:edge]], axis=0), "tm", down)

    shape = jax.ShapeDtypeStruct
    pieces = shape((count, PIECE_ROWS, LANES), BF16)
    rows_shape = shape((frames, CH), BF16)
    own_shape = shape((own, LANES), F32)
    kept_shape = shape((own, half), BF16)
    sent = call(
        lambda *refs: pack_kernel(groups, *refs),
        pieces,
        [ANY] * 3,
        ANY,
        [pltpu.VMEM((frames, CH), BF16)] * 3
        + [pltpu.VMEM((count, PIECE_ROWS, LANES), BF16)]
        + [pltpu.VMEM((CH, LANES), BF16)] * 2
        + [pltpu.SemaphoreType.DMA((3,)), pltpu.SemaphoreType.DMA((HEADS,))],
        56,
        1000000,
        "pack_qkv",
    )(queries, keys, values)
    got = call(
        lambda *refs: None,
        pieces,
        [ANY] * 5,
        ANY,
        [],
        8,
        0,
        "received",
        aliases={0: 0},
    )(exchange(sent), before, after, gain, taps)
    swapped = lax.ppermute(got, "tm", partner)

    block, chunk = 512, 512
    attend_scratch = [
        pltpu.VMEM((LANES, half), BF16),
        pltpu.VMEM((half, LANES), BF16),
        pltpu.VMEM((2, block, half), F32),
    ]
    *state, own_kept = call(
        lambda *refs: forward_first_kernel(block, chunk, *refs),
        (own_shape,) * 2 + (kept_shape,),
        [VMEM],
        (VMEM,) * 3,
        attend_scratch,
        36,
        2 * matmul,
        "attend_forward_own",
        own * half,
    )(got)
    results, head_out, other_kept = call(
        lambda *refs: forward_second_kernel(block, chunk, groups, *refs),
        (shape((count, 48, LANES), BF16), shape((own, LANES), BF16), kept_shape),
        [SMEM] + [VMEM] * 4,
        (VMEM,) * 3,
        attend_scratch,
        36,
        2 * matmul,
        "attend_forward_other",
        own * half,
    )(place, got, swapped, *state)
    returned = exchange(results)

    grads_sent, block_out, grad_resid = call(
        lambda *refs: conv_kernel(groups, count, *refs),
        (shape((count, SUB, LANES), BF16), rows_shape, rows_shape),
        [SMEM] + [VMEM] * 7,
        (VMEM,) * 3,
        [
            pltpu.VMEM((frames + 2 * SUB, CH), F32),
            pltpu.VMEM((2, frames + 2 * SUB, LANES), F32),
            pltpu.VMEM((2, frames + 2 * edge, LANES), F32),
            pltpu.VMEM((frames, CH), F32),
            pltpu.VMEM((TAPS + 1, CH), F32),
            pltpu.VMEM((16, frames + 2 * edge + 8, LANES), F32),
            pltpu.VMEM((2, frames + 16, LANES), F32),
        ],
        16,
        10000000,
        "conv_block",
    )(place, returned, resid, cotangent, before, after, gain, taps)
    grads_got = exchange(grads_sent)
    arrived = lax.ppermute(
        block_out, "section", [(i, (i + 1) % sections) for i in range(sections)]
    )

    block, chunk = own, 512
    backward_scratch = [
        pltpu.VMEM((LANES, half), BF16),
        pltpu.VMEM((half, LANES), BF16),
        pltpu.VMEM((HEAD_DIM, half), F32),
        pltpu.VMEM((HEAD_DIM, half), F32),
    ]
    part_shape = shape((count, HEAD_DIM, LANES), BF16)
    other_part, grad_q = call(
        lambda *refs: backward_first_kernel(block, chunk, *refs),
        (part_shape, own_shape),
        [VMEM] * 5,
        (VMEM,) * 2,
        backward_scratch,
        36,
        4 * matmul,
        "attend_backward_other",
    )(other_kept, swapped, got, grads_got, head_out)
    arrived_part = lax.ppermute(other_part, "tm", partner)
    own_part, grad_q_pieces = call(
        lambda *refs: backward_second_kernel(block, chunk, *refs),
        (part_shape, shape((count, SUB, LANES), BF16)),
        [VMEM] * 5,
        (VMEM,) * 2,
        backward_scratch,
        36,
        4 * matmul,
        "attend_backward_own",
    )(own_kept, got, grads_got, head_out, grad_q)
    grads_out = call(
        join_kernel,
        pieces,
        [VMEM] * 3,
        VMEM,
        [],
        8,
        1000000,
        "join_grads",
    )(own_part, arrived_part, grad_q_pieces)
    back = exchange(grads_out)

    grad_q, grad_k, grad_v, grad_gain, grad_taps, next_input = call(
        lambda *refs: unpack_kernel(groups, *refs),
        (
            rows_shape,
            rows_shape,
            rows_shape,
            shape((1, CH), F32),
            shape((TAPS, 1, CH), F32),
            rows_shape,
        ),
        [VMEM] * 2,
        (VMEM,) * 6,
        [pltpu.VMEM((CH, LANES), BF16)] * 2,
        8,
        1000000,
        "unpack_grads",
    )(back, arrived)
    return (
        next_input[None],
        grad_resid[None],
        grad_q[None],
        grad_k[None],
        grad_v[None],
        grad_gain,
        grad_taps.reshape(1, TAPS, CH),
    )


def solution(mesh):
    rows = P("section", "tm", None)
    in_specs = (rows, rows, rows, rows, P("section", None), P("section", None, None), rows)
    out_specs = (rows, rows, rows, rows, rows, P("section", None), P("section", None, None))
    return jax.shard_map(local, mesh=mesh, in_specs=in_specs, out_specs=out_specs, check_vma=False)
```
